32 devices in a mesh: gx: 4 (over y, core), gy: 8 (over z, x).
Axes of the slice: x: 2, y: 2, z: 4, core: 2. Of those that a mesh axis runs over, the one named last changes fastest.
Arguments:
- input_cells: bfloat16 [3, 256, 320, 256], P(None, ('gx', 'gy')), may hold values from -6 to 6
- time_embed: bfloat16 [3, 8, 1024], replicated, may hold values from -6 to 6
- first_gain: bfloat16 [256], P(('gx', 'gy')), may hold values from 0.25 to 1.75
- first_shift: bfloat16 [256], P(('gx', 'gy')), may hold values from -3 to 3
- first_kernel: bfloat16 [2304, 256], P(('gx', 'gy')), may hold values from -0.125 to 0.125
- first_offset: bfloat16 [256], P(('gx', 'gy')), may hold values from -3 to 3
- time_kernel: bfloat16 [1024, 512], P(('gx', 'gy')), may hold values from -0.1875 to 0.1875
- time_offset: bfloat16 [512], P(('gx', 'gy')), may hold values from -3 to 3
- second_gain: bfloat16 [256], P(('gx', 'gy')), may hold values from 0.25 to 1.75
- second_shift: bfloat16 [256], P(('gx', 'gy')), may hold values from -3 to 3
- second_kernel: bfloat16 [2304, 256], P(('gx', 'gy')), may hold values from -0.125 to 0.125
- second_offset: bfloat16 [256], P(('gx', 'gy')), may hold values from -3 to 3
- output_grad: bfloat16 [3, 256, 320, 256], P(None, ('gx', 'gy')), may hold values from -6 to 6
- slot_image: int32 [3, 32], replicated, may hold values from 0 to 7, as said below
- image_height: int32 [3, 8], replicated, may hold values from 12 to 40, as said below
Outputs:
- output_cells: bfloat16 [3, 256, 320, 256], P(None, ('gx', 'gy'))
- input_grad: bfloat16 [3, 256, 320, 256], P(None, ('gx', 'gy'))
- first_gain_grad: float32 [256], P(('gx', 'gy'))
- first_shift_grad: float32 [256], P(('gx', 'gy'))
- first_kernel_grad: float32 [2304, 256], P(('gx', 'gy'))
- first_offset_grad: float32 [256], P(('gx', 'gy'))
- time_kernel_grad: float32 [1024, 512], P(('gx', 'gy'))
- time_offset_grad: float32 [512], P(('gx', 'gy'))
- second_gain_grad: float32 [256], P(('gx', 'gy'))
- second_shift_grad: float32 [256], P(('gx', 'gy'))
- second_kernel_grad: float32 [2304, 256], P(('gx', 'gy'))
- second_offset_grad: float32 [256], P(('gx', 'gy'))
The draws below stay inside these ranges and needn't reach their ends.
Inputs may be any that keep to these rules, and one draw needn't show every extreme that they name: `slot_image`: in each batch the 8 images hold runs of consecutive blocks in an order drawn from the seed: image i holds 3 blocks if i < 4, else 5. `image_height`: image i has 12 to 24 valid rows if i < 4, else 40 - 12 to 40.
All inputs are finite; a program needn't handle non-finite values.
Results may differ from the reference program's by a relative error of at most 0.0085.
Values may be sent and summed in bfloat16 or wider, within the bound.
A program may use at most 256 MiB of HBM per device.

```python
import jax
import jax.numpy as jnp
from jax import lax

C = 256
E = 1024
NORM_GROUPS = 32
IMAGES = 8
BR = 8
W = 320
IMAGE_BATCHES = 3
BATCH_BLOCKS = 32
NARROW = 192
WIDE_BLK = 3
TALL_BLK = 5
WIDE_ROWS = 24
TALL_ROWS = 40
CUT = 12
ROWS = 256


def draw_slot_image(key, part):
    key = jax.random.fold_in(key, 11)
    batch_keys = jax.random.split(key, IMAGE_BATCHES)
    block_numbers = jnp.arange(BATCH_BLOCKS, dtype=jnp.int32)

    def one_batch(batch_key):
        order = jax.random.permutation(batch_key, IMAGES).astype(jnp.int32)
        length = jnp.where(order < IMAGES // 2, WIDE_BLK, TALL_BLK).astype(jnp.int32)
        ends = jnp.cumsum(length)
        block_position = jnp.sum((block_numbers[:, None] >= ends[None, :]).astype(jnp.int32), axis=1)
        return order[block_position]
    return jax.vmap(one_batch)(batch_keys).astype(jnp.int32)


def draw_image_height(key, part):
    key = jax.random.fold_in(key, 23)
    key_cut, key_short, key_tall = jax.random.split(key, 3)
    image_ids = jnp.arange(IMAGES, dtype=jnp.int32)
    full_rows = jnp.where(image_ids < IMAGES // 2, WIDE_ROWS, TALL_ROWS).astype(jnp.int32)
    cut_rows = jax.random.randint(key_cut, (IMAGE_BATCHES, IMAGES), 0, CUT + 1).astype(jnp.int32)
    short_image = jax.random.randint(key_short, (IMAGE_BATCHES, 1), 0, IMAGES // 2).astype(jnp.int32)
    tall_image = IMAGES // 2 + jax.random.randint(key_tall, (IMAGE_BATCHES, 1), 0, IMAGES // 2).astype(jnp.int32)
    cut_rows = jnp.where(image_ids[None, :] == short_image, CUT, cut_rows)
    cut_rows = jnp.where(image_ids[None, :] == tall_image, 0, cut_rows)
    return (full_rows[None, :] - cut_rows).astype(jnp.int32)


def raised(values, rng, source, target, shards_of, factor):
    def block_of(position):
        return (jnp.arange(values.shape[position]) // (values.shape[position] // shards_of)).reshape((-1,) + (1,) * (values.ndim - 1 - position))

    near = jax.random.permutation(rng, shards_of)[block_of(target)]
    far = (block_of(target) + shards_of // 2) % shards_of
    return jnp.where((block_of(source) == near) | (block_of(source) == far), factor * values, values)


def shard_levels(key, dims, pieces, smallest, largest):
    level = 1.0
    for position, shards_of in pieces:
        draws = jax.random.uniform(jax.random.fold_in(jax.random.fold_in(key, 6), position), (shards_of,), jnp.float32, smallest / len(pieces), largest / len(pieces))
        level = level * jnp.repeat(jnp.exp(draws), dims[position] // shards_of).reshape((-1,) + (1,) * (len(dims) - 1 - position))
    return level


def bell_draw(own_key, dims, width, reach, shards=(), kind=jnp.bfloat16):
    values = jax.random.normal(own_key, dims, jnp.float32) * width
    if len(shards) > 0:
        values = shard_levels(own_key, dims, shards, -0.22, 0.18) * values
    return jnp.clip(values, min=-reach, max=reach).astype(kind)


def bell_draw_with(stream_key, shape, scale, limit, cuts, heavy, kind=jnp.bfloat16):
    values = scale * jax.random.normal(stream_key, shape, jnp.float32)
    if cuts:
        values = values * shard_levels(stream_key, shape, cuts, -0.22, 0.18)
    return jnp.clip(raised(values, jax.random.fold_in(stream_key, 3), *heavy), -limit, limit).astype(kind)


def setup_inputs(seed: int = 0) -> dict:
    keys = jax.random.split(jax.random.key(seed), 16)
    return {
        "input_cells": bell_draw(keys[0], (IMAGE_BATCHES, ROWS, W, C), 1.0, 6.0, ((1, 32),)),
        "time_embed": bell_draw(keys[1], (IMAGE_BATCHES, IMAGES, E), 1.0, 6.0),
        "first_gain": jnp.clip(1.0 + 0.15 * jax.random.normal(keys[2], (C,), jnp.float32), 0.25, 1.75).astype(jnp.bfloat16),
        "first_shift": bell_draw(keys[3], (C,), 0.5, 3.0, ((0, 32),)),
        "first_kernel": bell_draw(keys[4], (9 * C, C), (9 * C) ** -0.5, 0.125, ((0, 32),)),
        "first_offset": bell_draw(keys[5], (C,), 0.5, 3.0, ((0, 32),)),
        "time_kernel": bell_draw(keys[6], (E, 2 * C), E ** -0.5, 0.1875, ((0, 32),)),
        "time_offset": bell_draw(keys[7], (2 * C,), 0.5, 3.0, ((0, 32),)),
        "second_gain": jnp.clip(1.0 + 0.15 * jax.random.normal(keys[8], (C,), jnp.float32), 0.25, 1.75).astype(jnp.bfloat16),
        "second_shift": bell_draw(keys[9], (C,), 0.5, 3.0, ((0, 32),)),
        "second_kernel": bell_draw(keys[10], (9 * C, C), (9 * C) ** -0.5, 0.125, ((0, 32),)),
        "second_offset": bell_draw(keys[11], (C,), 0.5, 3.0, ((0, 32),)),
        "output_grad": bell_draw_with(keys[12], (IMAGE_BATCHES, ROWS, W, C), 1.0, 6.0, ((1, 32),), (1, 3, 32, 2.75)),
        "slot_image": draw_slot_image(jax.random.fold_in(keys[15], 71), 0),
        "image_height": draw_image_height(jax.random.fold_in(keys[15], 71), 0),
    }


EPS = 1e-05
HIGHEST_PRECISION = lax.Precision.HIGHEST

@jax.custom_vjp
def low(v):
    return lax.optimization_barrier(v.astype(jnp.bfloat16)).astype(jnp.float32)

@jax.custom_vjp
def low_back(v):
    return v

def low_keep(v):
    return (low(v), None)

def low_pass(kept, grad):
    return (grad,)

def back_keep(v):
    return (v, None)

def back_low(kept, grad):
    return (low(grad),)
low.defvjp(low_keep, low_pass)
low_back.defvjp(back_keep, back_low)

def layout(slot_row, height_row):
    slot_count = slot_row.shape[0]
    block_numbers = jnp.arange(slot_count, dtype=jnp.int32)
    image_ids = jnp.arange(IMAGES, dtype=jnp.int32)
    first_slot = lax.optimization_barrier(jnp.min(jnp.where(slot_row[None, :] == image_ids[:, None], block_numbers[None, :], slot_count), axis=1)).astype(jnp.int32)
    image_width = jnp.where(image_ids < IMAGES // 2, W, NARROW).astype(jnp.int32)
    row_image = jnp.repeat(slot_row, BR)
    onehot = (row_image[:, None] == image_ids[None, :]).astype(jnp.float32)
    row_ids = jnp.arange(slot_count * BR, dtype=jnp.int32)
    row_in_image = row_ids - BR * first_slot[row_image]
    row_ok = row_in_image < height_row[row_image]
    col_ok = jnp.arange(W, dtype=jnp.int32)[None, :] < image_width[row_image][:, None]
    valid_cells = (row_ok[:, None] & col_ok).astype(jnp.float32)
    same_image = (row_image[1:] == row_image[:-1]).astype(jnp.float32)
    zero_one = jnp.zeros((1,), jnp.float32)
    same_up = jnp.concatenate([zero_one, same_image])
    same_down = jnp.concatenate([same_image, zero_one])
    cell_count = (height_row * image_width * (C // NORM_GROUPS)).astype(jnp.float32)
    return (valid_cells, onehot, cell_count, same_up, same_down)

def group_stat(values, onehot):
    row_count = values.shape[0]
    per_row = lax.optimization_barrier(jnp.sum(values, axis=1)).reshape(row_count, NORM_GROUPS, C // NORM_GROUPS)
    per_row = lax.optimization_barrier(jnp.sum(per_row, axis=2))
    return jnp.dot(onehot.T, per_row, precision=HIGHEST_PRECISION)

def to_rows(stat, onehot):
    per_row = jnp.dot(onehot, stat, precision=HIGHEST_PRECISION)
    return jnp.repeat(per_row, C // NORM_GROUPS, axis=1)[:, None, :]

def group_norm(values, gain, shift, valid_cells, onehot, cell_count):
    keep_cells = valid_cells[:, :, None]
    mean_value = group_stat(values * keep_cells, onehot) / cell_count[:, None]
    centered = (values - to_rows(mean_value, onehot)) * keep_cells
    variance = group_stat(centered * centered, onehot) / cell_count[:, None]
    inv_std = lax.rsqrt(variance + EPS)
    return (values - to_rows(mean_value, onehot)) * to_rows(inv_std, onehot) * gain + shift

def conv(field, kernel, same_up, same_down):
    row_count, col_count, channels = field.shape
    zero_row = jnp.zeros((1, col_count, channels), jnp.float32)
    above = jnp.concatenate([zero_row, field[:-1]], axis=0) * same_up[:, None, None]
    below = jnp.concatenate([field[1:], zero_row], axis=0) * same_down[:, None, None]
    result = jnp.zeros((row_count * col_count, channels), jnp.float32)
    for row_tap, source in enumerate((above, field, below)):
        padded = jnp.pad(source, ((0, 0), (1, 1), (0, 0)))
        window = jnp.concatenate([padded[:, col_tap:col_tap + col_count] for col_tap in range(3)], axis=2)
        block_rows = kernel[row_tap * 3 * channels:(row_tap + 1) * 3 * channels]
        result = result + jnp.dot(window.reshape(row_count * col_count, 3 * channels), block_rows, precision=HIGHEST_PRECISION)
    return result.reshape(row_count, col_count, channels)

def forward_group(cells, embed, slot_row, height_row, weights):
    first_gain, first_shift, first_kernel, first_offset, time_kernel, time_offset, second_gain, second_shift, second_kernel, second_offset = weights
    valid_cells, onehot, cell_count, same_up, same_down = layout(slot_row, height_row)
    keep_cells = valid_cells[:, :, None]
    normed_one = group_norm(cells, first_gain, first_shift, valid_cells, onehot, cell_count)
    act_one = low(keep_cells * jax.nn.silu(normed_one))
    hidden_one = low_back(conv(act_one, first_kernel, same_up, same_down) + first_offset)
    embed_low = low(jax.nn.silu(embed))
    time_out = jnp.dot(embed_low, time_kernel, precision=HIGHEST_PRECISION) + time_offset
    time_rows = jnp.dot(onehot, time_out, precision=HIGHEST_PRECISION)
    scale_rows = time_rows[:, None, :C]
    shift_rows = time_rows[:, None, C:]
    normed_two = group_norm(hidden_one, second_gain, second_shift, valid_cells, onehot, cell_count)
    act_two = low(keep_cells * jax.nn.silu(normed_two * (1.0 + scale_rows) + shift_rows))
    hidden_two = low_back(conv(act_two, second_kernel, same_up, same_down) + second_offset)
    return keep_cells * (cells + hidden_two)

def reference(input_cells, time_embed, first_gain, first_shift, first_kernel, first_offset, time_kernel, time_offset, second_gain, second_shift, second_kernel, second_offset, output_grad, slot_image, image_height):
    weights = tuple((item.astype(jnp.float32) for item in (first_gain, first_shift, first_kernel, first_offset, time_kernel, time_offset, second_gain, second_shift, second_kernel, second_offset)))
    embed_full = time_embed.astype(jnp.float32)

    def forward(cells_full, params):

        def one_batch(item):
            cells, embed, slot_row, height_row = item
            return forward_group(cells, embed, slot_row, height_row, params)
        return lax.map(jax.checkpoint(one_batch), (cells_full, embed_full, slot_image, image_height))
    complete_output, pull = jax.vjp(forward, input_cells.astype(jnp.float32), weights)
    grad_cells, grads = pull(output_grad.astype(jnp.float32))
    return (complete_output.astype(jnp.bfloat16), grad_cells.astype(jnp.bfloat16), grads[0], grads[1], grads[2], grads[3], grads[4], grads[5], grads[6], grads[7], grads[8], grads[9])
```

```python
import jax
import jax.numpy as jnp
from jax import lax
from jax.experimental import pallas as pl
from jax.experimental.pallas import tpu as pltpu
from jax.sharding import PartitionSpec as P

NORM_GROUPS = 32
EPS = 1e-05
HIGHEST = lax.Precision.HIGHEST
MESH = pl.DeviceIdType.MESH
F32 = jnp.float32
BF16 = jnp.bfloat16


def silu(values):
    return values * (0.5 + 0.5 * jnp.tanh(0.5 * values))


def silu_slope(values):
    gate = 0.5 + 0.5 * jnp.tanh(0.5 * values)
    return gate * (1.0 + values * (1.0 - gate))


def fold(values):
    rows, channels = values.shape
    return jnp.sum(values.reshape(rows // 8, 8, channels), axis=0)


class Plan:
    def __init__(self, mesh_shape, cells, time_embed, slot_image, kernel_rows, embed_rows):
        self.gx, self.gy = mesh_shape["gx"], mesh_shape["gy"]
        self.n = self.gx * self.gy
        self.ny = self.gx // 2
        self.nx = self.ny if self.gy % self.ny == 0 else 1
        self.nz = self.gy // self.nx
        self.batches, self.rows, self.cols, self.channels = cells
        self.images, self.embed = time_embed[1], time_embed[2]
        self.reach = slot_image[1] * 5 // 32 - 1
        self.shard = kernel_rows
        self.padded = (kernel_rows + 15) // 16 * 16
        self.embed_rows = embed_rows
        tight = self.n > 64
        self.parts, self.grad_rows, self.held = (2, 2, BF16) if tight else (1, 4, F32)


def build_kernel(plan):
    n, gx_size, gy_size = plan.n, plan.gx, plan.gy
    nx, ny, nz = plan.nx, plan.ny, plan.nz
    batches, rows, cols, channels = plan.batches, plan.rows, plan.cols, plan.channels
    images, reach = plan.images, plan.reach
    shard, padded, embed_rows = plan.shard, plan.padded, plan.embed_rows
    group = channels // NORM_GROUPS
    group_shift = group.bit_length() - 1
    narrow = cols * 3 // 5
    taps = 9 * channels
    param_width = channels // n
    time_width = 2 * channels // n

    def kernel(
        x_hbm, og_hbm, k1_in, k2_in, par_in, emb_in, tk_in, slot_v, slot_s, high_s,
        out_hbm, gi_hbm, wg1_o, wg2_o, tkg_o, vec_o,
        x_v, g2_v, a1_v, a2_v, g1_v, h_v, gm_v, kf1, kf2, kb2, kpad, agk, acc,
        rs1, rs2, rs3, qsh, nb1, nb2, ex3, ex4, pbuf, ta1, ta2, ta3, tout,
        osel, msg, cf, st, wr_s,
        ld_sem, halo_s, halo_r, ag_s, ag_r, rs_s, rs_r, ar_s, ar_r, ex_s, near_r, far_r, out_sem,
    ):
        my_x = lax.axis_index("gx")
        my_y = lax.axis_index("gy")
        me = my_x * gy_size + my_y
        core = lax.rem(my_x, 2)
        yy = lax.div(my_x, 2)
        zz = lax.div(my_y, nx)
        xx = lax.rem(my_y, nx)
        sib = 1 - core

        def dev(index):
            return (lax.div(index, gy_size), lax.rem(index, gy_size))

        def wait_bytes(ref, sem):
            pltpu.make_async_copy(ref, ref, sem).wait()

        def send(src, dst, send_sem, recv_sem, device):
            pltpu.make_async_remote_copy(
                src_ref=src, dst_ref=dst, send_sem=send_sem, recv_sem=recv_sem,
                device_id=device, device_id_type=MESH,
            ).start()

        load_x = pltpu.make_async_copy(x_hbm, x_v.at[:, pl.ds(cols, rows * cols)], ld_sem.at[0])
        load_g = pltpu.make_async_copy(og_hbm, g2_v.at[:, pl.ds(cols, rows * cols)], ld_sem.at[1])
        load_x.start()
        load_g.start()
        barrier = pltpu.get_barrier_semaphore()

        def greet(step, carry):
            pl.semaphore_signal(
                barrier, inc=1, device_id=dev(lax.rem(me + step, n)), device_id_type=MESH
            )
            return carry

        lax.fori_loop(1, n, greet, 0)

        for which, ref in enumerate((k1_in, k2_in)):
            own = ref[...].astype(F32)
            if padded > shard:
                own = jnp.concatenate([own, jnp.zeros((padded - shard, channels), F32)], axis=0)
            kpad[which] = own.astype(BF16)
            agk[which, me] = own.astype(BF16)

        same = []
        near_count = []
        own_count = []
        image_count = []
        own_image = []
        for g in range(batches):
            image = slot_s[g, me]
            before = jnp.int32(0)
            links = []
            for e in range(-reach, reach + 1):
                place = me + e
                inside = jnp.where((place >= 0) & (place < n), 1, 0)
                other = slot_s[g, jnp.clip(place, 0, n - 1)]
                link = inside * jnp.where(other == image, 1, 0)
                links.append(link)
                if e < 0:
                    before = before + link
            height = high_s[g, image]
            width = jnp.where(image < images // 2, cols, narrow)
            for r in range(-1, rows + 1):
                row_ok = jnp.where(before * rows + r < height, 1, 0)
                if r == -1:
                    row_ok = row_ok * links[reach - 1]
                if r == rows:
                    row_ok = row_ok * links[reach + 1]
                wr_s[g, r + 1] = row_ok * width
            counts = []
            for e in range(-reach, reach + 1):
                held = jnp.clip(height - (before + e) * rows, 0, rows) * links[e + reach]
                counts.append((held * width * group).astype(F32))
            same.append([link.astype(F32) for link in links])
            near_count.append(counts)
            own_count.append(counts[reach])
            image_count.append((height * width * group).astype(F32))
            own_image.append(image)

        row_id = lax.broadcasted_iota(jnp.int32, (8, channels), 0)
        col_id = lax.broadcasted_iota(jnp.int32, (cols, channels), 0)
        grp_r = lax.broadcasted_iota(jnp.int32, (channels, channels), 0)
        grp_c = lax.broadcasted_iota(jnp.int32, (channels, channels), 1)

        def per_row(values, rest=0.0):
            total = jnp.full((8, channels), rest, F32)
            for i, value in enumerate(values):
                total = jnp.where(row_id == i, value, total)
            return total

        def group_sum(tile):
            block = jnp.where(
                lax.shift_right_logical(grp_r, group_shift)
                == lax.shift_right_logical(grp_c, group_shift),
                1.0, 0.0,
            ).astype(F32)
            return jnp.dot(tile, block, precision=HIGHEST, preferred_element_type=F32)

        def keep(g, r, values):
            return jnp.where(col_id < wr_s[g, r + 1], values, 0.0)

        def span(r, count=1):
            start = (r + 1) * cols
            if not isinstance(start, int):
                start = pl.multiple_of(start, cols)
            return pl.ds(start, count * cols)

        def inner(r):
            start = r * cols
            if not isinstance(start, int):
                start = pl.multiple_of(start, cols)
            return pl.ds(start, cols)

        def coef(which, g):
            return cf[which, pl.ds(g, 1), :]

        def stat_tile(which):
            return per_row([jnp.sum(st[which, g], axis=0, keepdims=True) for g in range(batches)])

        def plane_peers():
            for dy in range(ny):
                for dx in range(nx):
                    if dy or dx:
                        py, px = lax.rem(yy + dy, ny), lax.rem(xx + dx, nx)
                        yield py, px, (py * 2 + core, zz * nx + px)

        def line_peers():
            for dz in range(1, nz):
                pz = lax.rem(zz + dz, nz)
                yield pz, (my_x, pz * nx + xx)

        sibling = (yy * 2 + sib, my_y)

        def gather_1(k):
            for _, _, peer in plane_peers():
                send(kpad.at[k], agk.at[k, me], ag_s.at[k, 0], ag_r.at[k, 0], peer)

        def gather_2(k):
            wait_bytes(agk.at[k, pl.ds(0, ny * nx - 1)], ag_r.at[k, 0])
            for _, peer in line_peers():
                for y in range(ny):
                    part = agk.at[k, pl.ds((y * 2 + core) * gy_size + zz * nx, nx)]
                    send(part, part, ag_s.at[k, 1], ag_r.at[k, 1], peer)

        def gather_3(k):
            wait_bytes(agk.at[k, pl.ds(0, (nz - 1) * ny * nx)], ag_r.at[k, 1])
            for y in range(ny):
                part = agk.at[k, pl.ds((y * 2 + core) * gy_size, gy_size)]
                send(part, part, ag_s.at[k, 2], ag_r.at[k, 2], sibling)

        def gather_end(k):
            wait_bytes(agk.at[k, pl.ds(0, n // 2)], ag_r.at[k, 2])

        def gather_sent(k):
            wait_bytes(agk.at[k, pl.ds(0, ny * nx - 1)], ag_s.at[k, 0])
            wait_bytes(agk.at[k, pl.ds(0, (nz - 1) * ny * nx)], ag_s.at[k, 1])
            wait_bytes(agk.at[k, pl.ds(0, n // 2)], ag_s.at[k, 2])

        def shards(body):
            if shard % 8 == 0:
                def step(i, carry):
                    body(i, pl.ds(pl.multiple_of(i * shard, 8), padded))
                    return carry

                lax.fori_loop(0, n, step, 0)
            else:
                for i in range(n):
                    body(i, pl.ds(i * shard, padded))

        def assemble(k):
            def one(i, place):
                acc[place, :] = agk[k, i].astype(F32)

            shards(one)

        def tap_block(a, b):
            return pl.ds((3 * a + b) * channels, channels)

        def fill_forward(ref):
            for a in range(3):
                for b in range(3):
                    ref[a * channels : (a + 1) * channels, b * channels : (b + 1) * channels] = acc[
                        tap_block(a, b), :
                    ].astype(BF16)

        def fill_backward(ref):
            for a in range(3):
                for b in range(3):
                    ref[a * channels : (a + 1) * channels, b * channels : (b + 1) * channels] = (
                        acc[tap_block(a, b), :].T.astype(BF16)
                    )

        def turn(ref):
            for a in range(3):
                for b in range(3):
                    place = (
                        slice(a * channels, (a + 1) * channels),
                        slice(b * channels, (b + 1) * channels),
                    )
                    ref[place] = ref[place].astype(F32).T.astype(BF16)

        def scatter_1(k):
            def one(i, place):
                agk[k, i] = acc[place, :].astype(BF16)

            gather_sent(k)
            shards(one)
            for y in range(ny):
                send(
                    agk.at[k, pl.ds((y * 2 + sib) * gy_size, gy_size)], rs1.at[k, y],
                    rs_s.at[k, 0], rs_r.at[k, 0], sibling,
                )

        def scatter_2(k):
            wait_bytes(rs1.at[k], rs_r.at[k, 0])
            for y in range(ny):
                def one(j, carry):
                    place = (y * 2 + core) * gy_size + j
                    total = agk[k, place].astype(F32) + rs1[k, y, j].astype(F32)
                    agk[k, place] = total.astype(BF16)
                    return carry

                lax.fori_loop(0, gy_size, one, 0)
            for pz, peer in line_peers():
                for y in range(ny):
                    send(
                        agk.at[k, pl.ds((y * 2 + core) * gy_size + pz * nx, nx)], rs2.at[k, zz, y],
                        rs_s.at[k, 1], rs_r.at[k, 1], peer,
                    )

        def scatter_3(k):
            wait_bytes(rs2.at[k, pl.ds(0, nz - 1)], rs_r.at[k, 1])
            for y in range(ny):
                for x in range(nx):
                    rs2[k, zz, y, x] = agk[k, (y * 2 + core) * gy_size + zz * nx + x]
            for y in range(ny):
                for x in range(nx):
                    total = rs2[k, 0, y, x].astype(F32)
                    for z in range(1, nz):
                        total = total + rs2[k, z, y, x].astype(F32)
                    qsh[k, y, x] = total.astype(BF16)
            for py, px, peer in plane_peers():
                send(
                    qsh.at[k, py, px], rs3.at[k, yy * nx + xx],
                    rs_s.at[k, 2], rs_r.at[k, 2], peer,
                )

        def scatter_end(k, out_ref):
            wait_bytes(rs3.at[k, pl.ds(0, ny * nx - 1)], rs_r.at[k, 2])
            rs3[k, yy * nx + xx] = qsh[k, yy, xx]
            total = rs3[k, 0].astype(F32)
            for i in range(1, ny * nx):
                total = total + rs3[k, i].astype(F32)
            out_ref[...] = total[:shard]

        def scatter_sent(k):
            wait_bytes(rs1.at[k], rs_s.at[k, 0])
            wait_bytes(rs2.at[k, pl.ds(0, nz - 1)], rs_s.at[k, 1])
            wait_bytes(rs3.at[k, pl.ds(0, ny * nx - 1)], rs_s.at[k, 2])

        def reduce_1(partial):
            own = yy * nx + xx
            ta1[own] = partial
            for _, _, peer in plane_peers():
                send(ta1.at[own], ta1.at[own], ar_s.at[0], ar_r.at[0], peer)

        def reduce_2():
            wait_bytes(ta1.at[pl.ds(0, ny * nx - 1)], ar_r.at[0])
            ta2[zz] = jnp.sum(ta1[...], axis=0)
            for _, peer in line_peers():
                send(ta2.at[zz], ta2.at[zz], ar_s.at[1], ar_r.at[1], peer)

        def reduce_3():
            wait_bytes(ta2.at[pl.ds(0, nz - 1)], ar_r.at[1])
            ta3[core] = jnp.sum(ta2[...], axis=0)
            send(ta3.at[core], ta3.at[core], ar_s.at[2], ar_r.at[2], sibling)

        def reduce_end():
            wait_bytes(ta3.at[0], ar_r.at[2])
            return ta3[0] + ta3[1]

        def reduce_sent():
            wait_bytes(ta1.at[pl.ds(0, ny * nx - 1)], ar_s.at[0])
            wait_bytes(ta2.at[pl.ds(0, nz - 1)], ar_s.at[1])
            wait_bytes(ta3.at[0], ar_s.at[2])

        def tell_all(src, buf, which):
            buf[me] = src[...]
            for d in range(1, reach + 1):
                for e in (d, -d):
                    peer = dev(lax.rem(me + e + n, n))
                    send(src, buf.at[me], ex_s.at[which], near_r.at[which], peer)

            def far(step, carry):
                peer = dev(lax.rem(me + step, n))
                send(src, buf.at[me], ex_s.at[which], far_r.at[which], peer)
                return carry

            lax.fori_loop(reach + 1, n - reach, far, 0)

        def near_all(buf, which):
            wait_bytes(buf.at[pl.ds(0, 2 * reach)], near_r.at[which])

        def far_all(buf, which):
            wait_bytes(buf.at[pl.ds(0, n - 1 - 2 * reach)], far_r.at[which])

        def sent_all(buf, which):
            wait_bytes(buf.at[pl.ds(0, n - 1)], ex_s.at[which])

        def tell_near(src, buf, which):
            buf[reach] = src[...]
            for d in range(1, reach + 1):
                for e in (d, -d):
                    peer = dev(lax.rem(me + e + n, n))
                    send(src, buf.at[reach - e], ex_s.at[which], near_r.at[which], peer)

        def near_wait(buf, which):
            wait_bytes(buf.at[pl.ds(0, 2 * reach)], near_r.at[which])

        def near_sent(buf, which):
            wait_bytes(buf.at[pl.ds(0, 2 * reach)], ex_s.at[which])

        def halo(field, which, source=None):
            if source is None:
                last, first = field.at[:, span(rows - 1)], field.at[:, span(0)]
            else:
                last, first = source.at[:, inner(rows - 1)], source.at[:, inner(0)]
            send(
                last, field.at[:, span(-1)], halo_s.at[which, 0], halo_r.at[which, 0],
                dev(lax.rem(me + 1, n)),
            )
            send(
                first, field.at[:, span(rows)], halo_s.at[which, 1], halo_r.at[which, 1],
                dev(lax.rem(me + n - 1, n)),
            )

        def halo_wait(field, which):
            wait_bytes(field.at[:, span(-1)], halo_r.at[which, 0])
            wait_bytes(field.at[:, span(rows)], halo_r.at[which, 1])

        def halo_sent(field, which):
            wait_bytes(field.at[:, span(-1)], halo_s.at[which, 0])
            wait_bytes(field.at[:, span(rows)], halo_s.at[which, 1])

        def keep_halo(field):
            def one(g, carry):
                for r in (-1, rows):
                    field[g, span(r), :] = keep(g, r, field[g, span(r), :].astype(F32)).astype(BF16)
                return carry

            lax.fori_loop(0, batches, one, 0)

        def gather_moments(buf):
            counts = per_row(image_count, 1.0)
            total = jnp.zeros((8, channels), F32)
            for e in range(2 * reach + 1):
                weight = per_row([same[g][e] for g in range(batches)] * 2)
                total = total + weight * buf[e]
            mean = total / counts
            squares = pltpu.roll(total, 8 - batches, 0)
            for e in range(2 * reach + 1):
                held = per_row([near_count[g][e] for g in range(batches)])
                shift = buf[e] / jnp.maximum(held, 1.0) - mean
                squares = squares + held * shift * shift
            return mean, lax.rsqrt(jnp.maximum(squares, 0.0) / counts + EPS)

        def gather_sums(buf):
            total = jnp.zeros((8, channels), F32)
            for e in range(-reach, reach + 1):
                weight = per_row([same[g][e + reach] for g in range(batches)] * 2)
                total = total + weight * buf[lax.rem(me + e + n, n)]
            return total, pltpu.roll(total, 8 - batches, 0)

        def pack_tile(plain, cross):
            return jnp.where(row_id < batches, plain, pltpu.roll(cross, batches, 0))

        def local_moments(read, which):
            total = group_sum(stat_tile(which))
            cf[15] = total / jnp.maximum(per_row(own_count, 1.0), 1.0)

            def one(g, carry):
                part = jnp.zeros((8, channels), F32)
                for r in range(rows):
                    gap = keep(g, r, read(g, r) - coef(15, g))
                    part = part + fold(gap * gap)
                st[which + 1, g] = part
                return carry

            lax.fori_loop(0, batches, one, 0)
            msg[which] = pack_tile(total, group_sum(stat_tile(which + 1)))

        def conv(field, weights, g, blocks, back):
            window = []
            for a in range(3):
                shift = (2 - a if back else a) - 1
                parts = [field[g, span(r + shift, count), :] for r, count in blocks]
                window.append(parts[0] if len(parts) == 1 else jnp.concatenate(parts, axis=0))
            result = jnp.dot(
                jnp.concatenate(window, axis=1), weights[...], preferred_element_type=F32
            )
            place = 0
            for r0, count in blocks:
                for q in range(count):
                    r = r0 + q
                    line = result[place * cols : (place + 1) * cols]
                    left, right = line[:, :channels], line[:, 2 * channels :]
                    if back:
                        left, right = right, left
                    left = jnp.where(col_id == 0, 0.0, pltpu.roll(left, 1, 0))
                    right = jnp.where(col_id == cols - 1, 0.0, pltpu.roll(right, cols - 1, 0))
                    yield r, left + line[:, channels : 2 * channels] + right
                    place += 1

        INSIDE = ((1, rows - 2),)
        EDGES = ((0, 1), (rows - 1, 1))

        def each_part(body):
            def one(i, carry):
                if plan.parts == 1:
                    body(i, INSIDE)
                else:
                    count = (rows - 2) // plan.parts
                    body(
                        lax.div(i, plan.parts), ((1 + lax.rem(i, plan.parts) * count, count),)
                    )
                return carry

            lax.fori_loop(0, batches * plan.parts, one, 0)

        def each_edge(body):
            def one(g, carry):
                body(g, EDGES)
                return carry

            lax.fori_loop(0, batches, one, 0)

        def each_batch(body):
            def one(g, carry):
                body(g)
                return carry

            lax.fori_loop(0, batches, one, 0)

        def shifted(values):
            right = jnp.where(col_id == 0, 0.0, pltpu.roll(values, 1, 0))
            left = jnp.where(col_id == cols - 1, 0.0, pltpu.roll(values, cols - 1, 0))
            return right, values, left

        def weight_grad_two(step_rows):
            acc[...] = jnp.zeros_like(acc)
            steps = rows // step_rows

            def one(i, carry):
                g = lax.div(i, steps)
                r0 = lax.rem(i, steps) * step_rows
                lines = []
                for q in range(step_rows):
                    right, mid, left = shifted(a2_v[g, span(r0 + q), :].astype(F32))
                    lines.append(jnp.concatenate([right, mid, left], axis=1).astype(BF16))
                lhs = jnp.concatenate(lines, axis=0)
                rhs = jnp.concatenate(
                    [g2_v[g, span(r0 + 1 - a, step_rows), :] for a in range(3)], axis=1
                )
                part = lax.dot_general(
                    lhs, rhs, (((0,), (0,)), ((), ())), preferred_element_type=F32
                )
                for a in range(3):
                    for b in range(3):
                        acc[tap_block(a, b), :] += part[
                            b * channels : (b + 1) * channels, a * channels : (a + 1) * channels
                        ]
                return carry

            lax.fori_loop(0, batches * steps, one, 0)

        def weight_grad_one(step_rows):
            acc[...] = jnp.zeros_like(acc)
            steps = rows // step_rows

            def one(i, carry):
                g = lax.div(i, steps)
                r0 = lax.rem(i, steps) * step_rows
                lines = []
                for q in range(step_rows):
                    right, mid, left = shifted(g1_v[g, span(r0 + q), :].astype(F32))
                    lines.append(jnp.concatenate([left, mid, right], axis=1).astype(BF16))
                rhs = jnp.concatenate(lines, axis=0)
                lhs = jnp.concatenate(
                    [a1_v[g, span(r0 + a - 1, step_rows), :] for a in range(3)], axis=1
                )
                part = lax.dot_general(
                    lhs, rhs, (((0,), (0,)), ((), ())), preferred_element_type=F32
                )
                for a in range(3):
                    for b in range(3):
                        acc[tap_block(a, b), :] += part[
                            a * channels : (a + 1) * channels, b * channels : (b + 1) * channels
                        ]
                return carry

            lax.fori_loop(0, batches * steps, one, 0)

        pl.semaphore_wait(barrier, n - 1)
        gather_1(0)
        tell_all(par_in, pbuf, 4)
        halo(x_v, 0, x_hbm)
        gather_1(1)

        embed = emb_in[...].astype(F32).reshape(batches * images, plan.embed)
        embed = silu(embed).astype(BF16)
        pick_r = lax.broadcasted_iota(jnp.int32, (plan.embed, 128), 0)
        pick_c = lax.broadcasted_iota(jnp.int32, (plan.embed, 128), 1)
        pick = jnp.where((pick_r == pick_c + me * embed_rows) & (pick_c < embed_rows), 1.0, 0.0)
        osel[...] = jnp.dot(embed, pick.astype(BF16), preferred_element_type=F32)
        own_tk = jnp.concatenate(
            [tk_in[...].astype(F32), jnp.zeros((128 - embed_rows, 2 * channels), F32)], axis=0
        ).astype(BF16)
        reduce_1(jnp.dot(osel[...].astype(BF16), own_tk, preferred_element_type=F32))

        load_x.wait()

        def sum_input(g):
            part = jnp.zeros((8, channels), F32)
            for r in range(rows):
                part = part + fold(keep(g, r, x_v[g, span(r), :].astype(F32)))
            st[0, g] = part

        each_batch(sum_input)
        local_moments(lambda g, r: x_v[g, span(r), :].astype(F32), 0)
        tell_near(msg.at[0], nb1, 0)
        gather_2(0)
        gather_2(1)

        near_all(pbuf, 4)
        far_all(pbuf, 4)
        tiles = pbuf[:, 0, :].astype(BF16)
        lane_r = lax.broadcasted_iota(jnp.int32, (128, channels), 0)
        lane_c = lax.broadcasted_iota(jnp.int32, (128, channels), 1)
        own_r = lax.broadcasted_iota(jnp.int32, (n, channels), 0)
        own_c = lax.broadcasted_iota(jnp.int32, (n, channels), 1)

        def vector(offset, width, start):
            spread = jnp.where(lane_r == offset + (lane_c & (width - 1)), 1.0, 0.0).astype(BF16)
            values = jnp.dot(tiles, spread, preferred_element_type=F32)
            owner = lax.shift_right_logical(own_c + start, width.bit_length() - 1)
            return jnp.sum(jnp.where(own_r == owner, values, 0.0), axis=0, keepdims=True)

        gain1, shift1, offset1, gain2, shift2, offset2 = (
            vector(i * param_width, param_width, 0) for i in range(6)
        )
        time_low = vector(6 * param_width, time_width, 0)
        time_high = vector(6 * param_width, time_width, channels)
        time_bias = jnp.concatenate([time_low, time_high], axis=1)

        near_wait(nb1, 0)
        mean1, inv1 = gather_moments(nb1)
        cf[0] = mean1
        cf[1] = inv1
        cf[2] = inv1 * gain1
        cf[3] = jnp.broadcast_to(shift1, (8, channels))
        cf[13] = jnp.broadcast_to(offset1, (8, channels))
        cf[14] = jnp.broadcast_to(offset2, (8, channels))

        def pre_one(g, values):
            return (values - coef(0, g)) * coef(2, g) + coef(3, g)

        def act_one(g, r):
            values = pre_one(g, x_v[g, span(r), :].astype(F32))
            a1_v[g, span(r), :] = keep(g, r, silu(values)).astype(BF16)

        def act_rows(g):
            for r in range(rows):
                act_one(g, r)

        each_batch(act_rows)
        gather_3(0)
        gather_3(1)
        reduce_2()
        gather_end(0)
        assemble(0)
        fill_forward(kf1)

        def hidden_rows(each):
            def body(g, blocks):
                part = jnp.zeros((8, channels), F32)
                for r, line in conv(a1_v, kf1, g, blocks, False):
                    line = line + coef(13, g)
                    h_v[g, inner(r), :] = line
                    part = part + fold(keep(g, r, line))
                st[2, g] = st[2, g] + part

            each(body)

        st[2] = jnp.zeros((batches, 8, channels), F32)
        hidden_rows(each_part)
        halo_wait(x_v, 0)
        halo(g2_v, 1, og_hbm)

        def act_halo(g):
            for r in (-1, rows):
                act_one(g, r)

        each_batch(act_halo)
        hidden_rows(each_edge)
        local_moments(lambda g, r: h_v[g, inner(r), :], 2)
        tell_near(msg.at[2], nb2, 1)
        reduce_3()

        gather_end(1)
        assemble(1)
        fill_forward(kf2)
        fill_backward(kb2)
        load_g.wait()

        def keep_grad(g):
            part = jnp.zeros((8, channels), F32)
            for r in range(rows):
                values = keep(g, r, g2_v[g, span(r), :].astype(F32))
                g2_v[g, span(r), :] = values.astype(BF16)
                part = part + fold(values)
            st[4, g] = part

        each_batch(keep_grad)

        def back_two(each):
            def body(g, blocks):
                for r, line in conv(g2_v, kb2, g, blocks, True):
                    gm_v[g, inner(r), :] = line.astype(plan.held)

            each(body)

        back_two(each_part)
        tout[...] = reduce_end() + time_bias
        picked = []
        image_id = lax.broadcasted_iota(jnp.int32, (images, 2 * channels), 0)
        for g in range(batches):
            block = tout[g * images : (g + 1) * images]
            picked.append(
                jnp.sum(jnp.where(image_id == own_image[g], block, 0.0), axis=0, keepdims=True)
            )
        scale = 1.0 + per_row([item[:, :channels] for item in picked])
        shift = per_row([item[:, channels:] for item in picked])
        near_wait(nb2, 1)
        mean2, inv2 = gather_moments(nb2)
        cf[4] = mean2
        cf[5] = inv2
        cf[6] = inv2 * gain2 * scale
        cf[7] = shift2 * scale + shift

        def modulated(g, values):
            return (values - coef(4, g)) * coef(6, g) + coef(7, g)

        def act_two(g, r):
            values = modulated(g, h_v[g, inner(r), :])
            a2_v[g, span(r), :] = keep(g, r, silu(values)).astype(BF16)

        def act_two_edges(g):
            act_two(g, 0)
            act_two(g, rows - 1)

        def act_two_inside(g):
            for r in range(1, rows - 1):
                act_two(g, r)

        each_batch(act_two_edges)
        halo(a2_v, 2)
        each_batch(act_two_inside)

        def output_rows(each, blocks, buf, sem):
            def body(g, blocks):
                for r, line in conv(a2_v, kf2, g, blocks, False):
                    line = line + coef(14, g) + x_v[g, span(r), :].astype(F32)
                    buf[g, span(r), :] = keep(g, r, line).astype(BF16)

            each(body)
            for i, (r, count) in enumerate(blocks):
                pltpu.make_async_copy(
                    buf.at[:, span(r, count)], out_hbm.at[:, pl.ds(r * cols, count * cols)],
                    out_sem.at[sem + i],
                ).start()

        def output_wait(blocks, buf, sem):
            for i, (r, count) in enumerate(blocks):
                wait_bytes(buf.at[:, span(r, count)], out_sem.at[sem + i])

        output_rows(each_part, INSIDE, g1_v, 2)
        halo_wait(g2_v, 1)
        keep_halo(g2_v)
        back_two(each_edge)

        def grad_mod(g):
            plain = jnp.zeros((8, channels), F32)
            cross = jnp.zeros((8, channels), F32)
            for r in range(rows):
                gap = h_v[g, inner(r), :] - coef(4, g)
                slope = silu_slope(gap * coef(6, g) + coef(7, g))
                grad = keep(g, r, gm_v[g, inner(r), :].astype(F32) * slope)
                gm_v[g, inner(r), :] = grad.astype(plan.held)
                plain = plain + fold(grad)
                cross = cross + fold(grad * gap)
            st[0, g] = plain
            st[1, g] = cross * coef(5, g)

        each_batch(grad_mod)
        offset_row = jnp.zeros((1, channels), F32)
        for g in range(batches):
            offset_row = offset_row + jnp.sum(st[4, g], axis=0, keepdims=True)
        tile = pack_tile(stat_tile(0), stat_tile(1))
        msg[1] = jnp.where(row_id == 2 * batches, offset_row, tile)
        tell_all(msg.at[1], ex3, 2)

        weight_grad_two(plan.grad_rows)
        scatter_1(1)

        near_all(ex3, 2)
        plain, cross = gather_sums(ex3)
        factor = gain2 * scale
        counts = per_row(image_count, 1.0)
        cf[8] = factor * inv2
        cf[9] = group_sum(factor * plain) / counts * inv2
        cf[10] = group_sum(factor * cross) / counts * inv2 * inv2

        def grad_one(g, r):
            gap = h_v[g, inner(r), :] - coef(4, g)
            values = gm_v[g, inner(r), :].astype(F32) * coef(8, g) - coef(9, g) - gap * coef(10, g)
            low = keep(g, r, values).astype(BF16)
            g1_v[g, span(r), :] = low
            return fold(low.astype(F32))

        def grad_one_edges(g):
            st[4, g] = grad_one(g, 0) + grad_one(g, rows - 1)

        def grad_one_inside(g):
            part = st[4, g]
            for r in range(1, rows - 1):
                part = part + grad_one(g, r)
            st[4, g] = part

        output_wait(INSIDE, g1_v, 2)
        each_batch(grad_one_edges)
        halo(g1_v, 3)
        each_batch(grad_one_inside)

        scatter_2(1)
        weight_grad_one(plan.grad_rows)
        scatter_3(1)
        scatter_1(0)
        turn(kf1)

        def back_one(each):
            def body(g, blocks):
                plain = jnp.zeros((8, channels), F32)
                cross = jnp.zeros((8, channels), F32)
                for r, line in conv(g1_v, kf1, g, blocks, True):
                    gap = x_v[g, span(r), :].astype(F32) - coef(0, g)
                    grad = keep(g, r, line * silu_slope(gap * coef(2, g) + coef(3, g)))
                    h_v[g, inner(r), :] = grad
                    plain = plain + fold(grad)
                    cross = cross + fold(grad * gap)
                cross = cross * coef(1, g)
                st[0, g] = st[0, g] + plain
                st[1, g] = st[1, g] + cross

            each(body)

        st[0] = jnp.zeros((batches, 8, channels), F32)
        st[1] = jnp.zeros((batches, 8, channels), F32)
        back_one(each_part)
        scatter_2(0)
        halo_wait(g1_v, 3)
        keep_halo(g1_v)
        back_one(each_edge)
        offset_row = jnp.zeros((1, channels), F32)
        for g in range(batches):
            offset_row = offset_row + jnp.sum(st[4, g], axis=0, keepdims=True)
        tile = pack_tile(stat_tile(0), stat_tile(1))
        msg[3] = jnp.where(row_id == 2 * batches, offset_row, tile)
        tell_all(msg.at[3], ex4, 3)

        halo_wait(a2_v, 2)
        keep_halo(a2_v)
        output_rows(each_edge, EDGES, a1_v, 0)

        near_all(ex4, 3)
        plain, cross = gather_sums(ex4)
        cf[11] = group_sum(gain1 * plain) / counts * inv1
        cf[12] = group_sum(gain1 * cross) / counts * inv1 * inv1

        def input_grad(g):
            for r in range(rows):
                gap = x_v[g, span(r), :].astype(F32) - coef(0, g)
                values = h_v[g, inner(r), :] * coef(2, g) - coef(11, g) - gap * coef(12, g)
                values = keep(g, r, values) + g2_v[g, span(r), :].astype(F32)
                x_v[g, span(r), :] = values.astype(BF16)
            pltpu.make_async_copy(
                x_v.at[g, pl.ds(cols, rows * cols)], gi_hbm.at[g], out_sem.at[3]
            ).start()

        each_batch(input_grad)
        scatter_3(0)
        scatter_end(1, wg2_o)

        far_all(ex3, 2)
        second_bias = jnp.zeros((1, channels), F32)
        gain_total = jnp.zeros((1, channels), F32)
        shift_total = jnp.zeros((1, channels), F32)
        time_rows = []
        slot_id = lax.broadcasted_iota(jnp.int32, (images, n), 0)
        for g in range(batches):
            hot = jnp.where(slot_v[g : g + 1, :] == slot_id, 1.0, 0.0).astype(F32)
            plain = jnp.dot(hot, ex3[:, g, :], precision=HIGHEST, preferred_element_type=F32)
            cross = jnp.dot(hot, ex3[:, batches + g, :], precision=HIGHEST, preferred_element_type=F32)
            factor = 1.0 + tout[g * images : (g + 1) * images, :channels]
            gain_total = gain_total + jnp.sum(factor * cross, axis=0, keepdims=True)
            shift_total = shift_total + jnp.sum(factor * plain, axis=0, keepdims=True)
            time_rows.append(jnp.concatenate([cross * gain2 + plain * shift2, plain], axis=1))
        second_bias = jnp.sum(ex3[:, 2 * batches, :], axis=0, keepdims=True)
        grad_time = jnp.concatenate(time_rows, axis=0)
        time_total = jnp.sum(grad_time, axis=0, keepdims=True)
        tkg_o[...] = lax.dot_general(
            osel[...], grad_time, (((0,), (0,)), ((), ())), precision=HIGHEST,
            preferred_element_type=F32,
        )[:embed_rows]

        far_all(ex4, 3)
        plain = jnp.zeros((1, channels), F32)
        cross = jnp.zeros((1, channels), F32)
        for g in range(batches):
            plain = plain + jnp.sum(ex4[:, g, :], axis=0, keepdims=True)
            cross = cross + jnp.sum(ex4[:, batches + g, :], axis=0, keepdims=True)
        first_bias = jnp.sum(ex4[:, 2 * batches, :], axis=0, keepdims=True)
        vec_c = lax.broadcasted_iota(jnp.int32, (channels, 128), 0)
        vec_j = lax.broadcasted_iota(jnp.int32, (channels, 128), 1)
        whole = jnp.concatenate(
            [cross, plain, first_bias, gain_total, shift_total, second_bias]
            + [jnp.zeros((2, channels), F32)], axis=0,
        )
        pick = jnp.where(vec_c == vec_j + me * param_width, 1.0, 0.0).astype(F32)
        vec_o[:8] = jnp.dot(whole, pick, precision=HIGHEST, preferred_element_type=F32)
        time_c = lax.broadcasted_iota(jnp.int32, (2 * channels, 128), 0)
        time_j = lax.broadcasted_iota(jnp.int32, (2 * channels, 128), 1)
        pick = jnp.where(time_c == time_j + me * time_width, 1.0, 0.0).astype(F32)
        vec_o[8:] = jnp.dot(
            jnp.broadcast_to(time_total, (8, 2 * channels)), pick, precision=HIGHEST,
            preferred_element_type=F32,
        )
        scatter_end(0, wg1_o)

        wait_bytes(gi_hbm, out_sem.at[3])
        output_wait(EDGES, a1_v, 0)
        for k in range(2):
            scatter_sent(k)
        reduce_sent()
        near_sent(nb1, 0)
        near_sent(nb2, 1)
        sent_all(ex3, 2)
        sent_all(ex4, 3)
        sent_all(pbuf, 4)
        for which, field in enumerate((x_v, g2_v, a2_v, g1_v)):
            halo_sent(field, which)

    margin = (batches, (rows + 2) * cols, channels)
    whole = (batches, rows * cols, channels)
    dma = pltpu.SemaphoreType.DMA
    scratch = [
        pltpu.VMEM(margin, BF16),
        pltpu.VMEM(margin, BF16),
        pltpu.VMEM(margin, BF16),
        pltpu.VMEM(margin, BF16),
        pltpu.VMEM(margin, BF16),
        pltpu.VMEM(whole, F32),
        pltpu.VMEM(whole, plan.held),
        pltpu.VMEM((3 * channels, 3 * channels), BF16),
        pltpu.VMEM((3 * channels, 3 * channels), BF16),
        pltpu.VMEM((3 * channels, 3 * channels), BF16),
        pltpu.VMEM((2, padded, channels), BF16),
        pltpu.VMEM((2, n, padded, channels), BF16),
        pltpu.VMEM((taps + 16, channels), F32),
        pltpu.VMEM((2, ny, gy_size, padded, channels), BF16),
        pltpu.VMEM((2, nz, ny, nx, padded, channels), BF16),
        pltpu.VMEM((2, ny * nx, padded, channels), BF16),
        pltpu.VMEM((2, ny, nx, padded, channels), BF16),
        pltpu.VMEM((2 * reach + 1, 8, channels), F32),
        pltpu.VMEM((2 * reach + 1, 8, channels), F32),
        pltpu.VMEM((n, 8, channels), F32),
        pltpu.VMEM((n, 8, channels), F32),
        pltpu.VMEM((n, 8, 128), F32),
        pltpu.VMEM((ny * nx, batches * images, 2 * channels), F32),
        pltpu.VMEM((nz, batches * images, 2 * channels), F32),
        pltpu.VMEM((2, batches * images, 2 * channels), F32),
        pltpu.VMEM((batches * images, 2 * channels), F32),
        pltpu.VMEM((batches * images, 128), F32),
        pltpu.VMEM((4, 8, channels), F32),
        pltpu.VMEM((16, 8, channels), F32),
        pltpu.VMEM((5, batches, 8, channels), F32),
        pltpu.SMEM((batches, 16), jnp.int32),
        dma((2,)),
        dma((4, 2)),
        dma((4, 2)),
        dma((2, 3)),
        dma((2, 3)),
        dma((2, 3)),
        dma((2, 3)),
        dma((3,)),
        dma((3,)),
        dma((5,)),
        dma((5,)),
        dma((5,)),
        dma((4,)),
    ]
    hbm = pl.BlockSpec(memory_space=pl.ANY)
    vmem = pl.BlockSpec(memory_space=pltpu.VMEM)
    smem = pl.BlockSpec(memory_space=pltpu.SMEM)
    return pl.pallas_call(
        kernel,
        name="block",
        out_shape=(
            jax.ShapeDtypeStruct(whole, BF16),
            jax.ShapeDtypeStruct(whole, BF16),
            jax.ShapeDtypeStruct((shard, channels), F32),
            jax.ShapeDtypeStruct((shard, channels), F32),
            jax.ShapeDtypeStruct((embed_rows, 2 * channels), F32),
            jax.ShapeDtypeStruct((16, 128), F32),
        ),
        in_specs=[hbm, hbm, vmem, vmem, vmem, vmem, vmem, vmem, smem, smem],
        out_specs=(hbm, hbm, vmem, vmem, vmem, vmem),
        scratch_shapes=scratch,
        compiler_params=pltpu.CompilerParams(
            collective_id=0, has_side_effects=True, vmem_limit_bytes=VMEM_LIMIT,
        ),
        cost_estimate=pl.CostEstimate(
            flops=12 * rows * cols * batches * taps * channels,
            bytes_accessed=8 * rows * cols * batches * channels,
            transcendentals=8 * rows * cols * batches * channels,
        ),
    )


VMEM_LIMIT = 63 * 2**20


def make_body(mesh_shape):
    def body(
        input_cells, time_embed, first_gain, first_shift, first_kernel, first_offset,
        time_kernel, time_offset, second_gain, second_shift, second_kernel, second_offset,
        output_grad, slot_image, image_height,
    ):
        cells = input_cells.shape
        plan = Plan(
            mesh_shape, cells, time_embed.shape, slot_image.shape,
            first_kernel.shape[0], time_kernel.shape[0],
        )
        flat = (cells[0], cells[1] * cells[2], cells[3])
        params = jnp.concatenate(
            [first_gain, first_shift, first_offset, second_gain, second_shift, second_offset,
             time_offset]
        ).astype(F32)
        params = jnp.pad(params[None, :], ((0, 7), (0, 128 - params.shape[0])))
        out, grad, wg1, wg2, tkg, vec = build_kernel(plan)(
            input_cells.reshape(flat), output_grad.reshape(flat), first_kernel, second_kernel,
            params, time_embed, time_kernel, slot_image, slot_image, image_height,
        )
        width = first_gain.shape[0]
        rows = [vec[i, :width] for i in range(6)]
        return (
            out.reshape(cells), grad.reshape(cells), rows[0], rows[1], wg1, rows[2],
            tkg, vec[8, : time_offset.shape[0]], rows[3], rows[4], wg2, rows[5],
        )

    return body


def solution(mesh):
    both = ("gx", "gy")
    cells, vector, matrix, whole = P(None, both, None, None), P(both), P(both, None), P()
    return jax.shard_map(
        make_body(dict(mesh.shape)),
        mesh=mesh,
        in_specs=(
            cells, whole, vector, vector, matrix, vector, matrix, vector, vector, vector, matrix,
            vector, cells, whole, whole,
        ),
        out_specs=(
            cells, cells, vector, vector, matrix, vector, matrix, vector, vector, vector, matrix,
            vector,
        ),
        check_vma=False,
    )
```

```python
import jax
import jax.numpy as jnp
from jax import lax
from jax.experimental import pallas as pl
from jax.experimental.pallas import tpu as pltpu
from jax.sharding import PartitionSpec as P

NORM_GROUPS = 32
EPS = 1e-05
HIGHEST = lax.Precision.HIGHEST
MESH = pl.DeviceIdType.MESH
F32 = jnp.float32
BF16 = jnp.bfloat16


def silu(values):
    return values * (0.5 + 0.5 * jnp.tanh(0.5 * values))


def silu_slope(values):
    gate = 0.5 + 0.5 * jnp.tanh(0.5 * values)
    return gate * (1.0 + values * (1.0 - gate))


def fold(values):
    rows, channels = values.shape
    return jnp.sum(values.reshape(rows // 8, 8, channels), axis=0)


class Plan:
    def __init__(self, mesh_shape, cells, time_embed, slot_image, kernel_rows, embed_rows):
        self.gx, self.gy = mesh_shape["gx"], mesh_shape["gy"]
        self.n = self.gx * self.gy
        self.ny = self.gx // 2
        self.nx = self.ny if self.gy % self.ny == 0 else 1
        self.nz = self.gy // self.nx
        self.batches, self.rows, self.cols, self.channels = cells
        self.images, self.embed = time_embed[1], time_embed[2]
        self.reach = slot_image[1] * 5 // 32 - 1
        self.shard = kernel_rows
        self.padded = (kernel_rows + 15) // 16 * 16
        self.embed_rows = embed_rows
        tight = self.n > 64
        self.parts, self.grad_rows, self.held = (2, 2, BF16) if tight else (1, 4, F32)


def build_kernel(plan):
    n, gx_size, gy_size = plan.n, plan.gx, plan.gy
    nx, ny, nz = plan.nx, plan.ny, plan.nz
    batches, rows, cols, channels = plan.batches, plan.rows, plan.cols, plan.channels
    images, reach = plan.images, plan.reach
    shard, padded, embed_rows = plan.shard, plan.padded, plan.embed_rows
    group = channels // NORM_GROUPS
    group_shift = group.bit_length() - 1
    narrow = cols * 3 // 5
    taps = 9 * channels
    param_width = channels // n
    time_width = 2 * channels // n

    def kernel(
        x_hbm, og_hbm, k1_in, k2_in, par_in, emb_in, tk_in, slot_v, slot_s, high_s,
        out_hbm, d1_hbm, wg1_o, wg2_o, tkg_o, vec_o, cf_o, wr_o,
        x_v, g2_v, a1_v, a2_v, g1_v, h_v, gm_v, kf1, kf2, kb2, agk, acc,
        rs1, rs2, rs3, rs4, nb1, nb2, ex3, ex4, pbuf, ta1, ta2, ta3, tout,
        osel, msg, cf, st, wr_s,
        ld_sem, halo_s, halo_r, ag_s, ag_r, rs_s, rs_r, ar_s, ar_r, ex_s, near_r, far_r, out_sem, back_sem,
    ):
        my_x = lax.axis_index("gx")
        my_y = lax.axis_index("gy")
        me = my_x * gy_size + my_y
        core = lax.rem(my_x, 2)
        yy = lax.div(my_x, 2)
        zz = lax.div(my_y, nx)
        xx = lax.rem(my_y, nx)
        sib = 1 - core

        def dev(index):
            return (lax.div(index, gy_size), lax.rem(index, gy_size))

        def wait_bytes(ref, sem):
            pltpu.make_async_copy(ref, ref, sem).wait()

        def send(src, dst, send_sem, recv_sem, device):
            pltpu.make_async_remote_copy(
                src_ref=src, dst_ref=dst, send_sem=send_sem, recv_sem=recv_sem,
                device_id=device, device_id_type=MESH,
            ).start()

        load_x = pltpu.make_async_copy(x_hbm, x_v.at[:, pl.ds(cols, rows * cols)], ld_sem.at[0])
        load_g = pltpu.make_async_copy(og_hbm, g2_v.at[:, pl.ds(cols, rows * cols)], ld_sem.at[1])
        load_x.start()
        load_g.start()
        barrier = pltpu.get_barrier_semaphore()

        def greet(step, carry):
            pl.semaphore_signal(
                barrier, inc=1, device_id=dev(lax.rem(me + step, n)), device_id_type=MESH
            )
            return carry

        lax.fori_loop(1, n, greet, 0)

        for which, ref in enumerate((k1_in, k2_in)):
            own = ref[...].astype(F32)
            if padded > shard:
                own = jnp.concatenate([own, jnp.zeros((padded - shard, channels), F32)], axis=0)
            agk[which, my_x, zz, xx] = own.astype(BF16)

        same = []
        near_count = []
        own_count = []
        image_count = []
        own_image = []
        for g in range(batches):
            image = slot_s[g, me]
            before = jnp.int32(0)
            links = []
            for e in range(-reach, reach + 1):
                place = me + e
                inside = jnp.where((place >= 0) & (place < n), 1, 0)
                other = slot_s[g, jnp.clip(place, 0, n - 1)]
                link = inside * jnp.where(other == image, 1, 0)
                links.append(link)
                if e < 0:
                    before = before + link
            height = high_s[g, image]
            width = jnp.where(image < images // 2, cols, narrow)
            for r in range(-1, rows + 1):
                row_ok = jnp.where(before * rows + r < height, 1, 0)
                if r == -1:
                    row_ok = row_ok * links[reach - 1]
                if r == rows:
                    row_ok = row_ok * links[reach + 1]
                wr_s[g, r + 1] = row_ok * width
            counts = []
            for e in range(-reach, reach + 1):
                held = jnp.clip(height - (before + e) * rows, 0, rows) * links[e + reach]
                counts.append((held * width * group).astype(F32))
            same.append([link.astype(F32) for link in links])
            near_count.append(counts)
            own_count.append(counts[reach])
            image_count.append((height * width * group).astype(F32))
            own_image.append(image)

        row_id = lax.broadcasted_iota(jnp.int32, (8, channels), 0)
        col_id = lax.broadcasted_iota(jnp.int32, (cols, channels), 0)
        grp_r = lax.broadcasted_iota(jnp.int32, (channels, channels), 0)
        grp_c = lax.broadcasted_iota(jnp.int32, (channels, channels), 1)

        def per_row(values, rest=0.0):
            total = jnp.full((8, channels), rest, F32)
            for i, value in enumerate(values):
                total = jnp.where(row_id == i, value, total)
            return total

        def group_sum(tile):
            block = jnp.where(
                lax.shift_right_logical(grp_r, group_shift)
                == lax.shift_right_logical(grp_c, group_shift),
                1.0, 0.0,
            ).astype(F32)
            return jnp.dot(tile, block, precision=HIGHEST, preferred_element_type=F32)

        def keep(g, r, values):
            return jnp.where(col_id < wr_s[g, r + 1], values, 0.0)

        def span(r, count=1):
            start = (r + 1) * cols
            if not isinstance(start, int):
                start = pl.multiple_of(start, cols)
            return pl.ds(start, count * cols)

        def inner(r):
            start = r * cols
            if not isinstance(start, int):
                start = pl.multiple_of(start, cols)
            return pl.ds(start, cols)

        def coef(which, g):
            return cf[which, pl.ds(g, 1), :]

        def stat_tile(which):
            return per_row([jnp.sum(st[which, g], axis=0, keepdims=True) for g in range(batches)])

        def x_peers():
            for dx in range(1, nx):
                px = lax.rem(xx + dx, nx)
                yield dx - 1, px, (my_x, zz * nx + px)

        def y_peers():
            for dy in range(1, ny):
                py = lax.rem(yy + dy, ny) * 2 + core
                yield dy - 1, py, (py, my_y)

        def z_peers():
            for dz in range(1, nz):
                pz = lax.rem(zz + dz, nz)
                yield dz - 1, pz, (my_x, pz * nx + xx)

        def plane_peers():
            for step in range(1, ny * nx):
                py = lax.rem(yy + step // nx, ny)
                px = lax.rem(xx + step % nx, nx)
                yield step - 1, (py * 2 + core, zz * nx + px)

        sibling = (yy * 2 + sib, my_y)

        def gather_send(k, hop, step, part, peer):
            send(part, part, ag_s.at[k, hop, step], ag_r.at[k, hop, step], peer)

        def gather_wait(k, hop, parts, ref):
            for step in range(parts):
                wait_bytes(ref, ag_r.at[k, hop, step])

        def gather_sent(k):
            for hop, parts, ref in gather_plan(k):
                for step in range(parts):
                    wait_bytes(ref, ag_s.at[k, hop, step])

        def gather_plan(k):
            one, row, plane = agk.at[k, 0, 0, 0], agk.at[k, 0, 0], agk.at[k, 0]
            if k == 0:
                return (
                    (0, nz - 1, one), (1, nz * (nx - 1), one), (2, nx * nz * (ny - 1), one),
                    (3, ny, plane),
                )
            return (0, nx - 1, one), (1, nz - 1, row), (2, nz * (ny - 1), row), (3, ny, plane)

        def came(dz, dx):
            return agk.at[0, my_x, lax.rem(zz - dz + nz, nz), lax.rem(xx - dx + nx, nx)]

        def pass_x(dz):
            for step, px, peer in x_peers():
                gather_send(0, 1, dz * (nx - 1) + step, came(dz, 0), peer)

        def pass_y(dz, dx):
            for step, py, peer in y_peers():
                gather_send(0, 2, (dz * nx + dx) * (ny - 1) + step, came(dz, dx), peer)

        def spread_start():
            for step, pz, peer in z_peers():
                gather_send(0, 0, step, came(0, 0), peer)
            pass_x(0)
            pass_y(0, 0)

        def spread_line():
            for dz in range(1, nz):
                wait_bytes(agk.at[0, 0, 0, 0], ag_r.at[0, 0, dz - 1])
                pass_x(dz)
                pass_y(dz, 0)

        def spread_plane():
            for dz in range(nz):
                for dx in range(1, nx):
                    wait_bytes(agk.at[0, 0, 0, 0], ag_r.at[0, 1, dz * (nx - 1) + dx - 1])
                    pass_y(dz, dx)

        def gather_x(k):
            for step, px, peer in x_peers():
                gather_send(k, 0, step, agk.at[k, my_x, zz, xx], peer)

        def forward_y(k, dz):
            row = agk.at[k, my_x, lax.rem(zz - dz + nz, nz)]
            for step, py, peer in y_peers():
                gather_send(k, 2, dz * (ny - 1) + step, row, peer)

        def gather_z(k):
            gather_wait(k, 0, nx - 1, agk.at[k, 0, 0, 0])
            for step, pz, peer in z_peers():
                gather_send(k, 1, step, agk.at[k, my_x, zz], peer)
            forward_y(k, 0)

        def gather_y(k, first=1, last=nz):
            for dz in range(first, last):
                wait_bytes(agk.at[k, 0, 0], ag_r.at[k, 1, dz - 1])
                forward_y(k, dz)

        def gather_core(k):
            hop, parts, ref = gather_plan(k)[2]
            gather_wait(k, hop, parts, ref)
            for y in range(ny):
                gather_send(k, 3, y, agk.at[k, y * 2 + core], sibling)

        def gather_end(k):
            gather_wait(k, 3, ny, agk.at[k, 0])

        def grid_place(i):
            left = lax.rem(i, gy_size)
            return lax.div(i, gy_size), lax.div(left, nx), lax.rem(left, nx)

        def shards(body):
            if shard % 8 == 0:
                def step(i, carry):
                    body(i, pl.ds(pl.multiple_of(i * shard, 8), padded))
                    return carry

                lax.fori_loop(0, n, step, 0)
            else:
                for i in range(n):
                    body(i, pl.ds(i * shard, padded))

        def assemble(k):
            def one(i, place):
                acc[place, :] = agk[(k, *grid_place(i))].astype(F32)

            shards(one)

        def tap_block(a, b):
            return pl.ds((3 * a + b) * channels, channels)

        def fill_forward(ref):
            for a in range(3):
                for b in range(3):
                    ref[a * channels : (a + 1) * channels, b * channels : (b + 1) * channels] = acc[
                        tap_block(a, b), :
                    ].astype(BF16)

        def fill_backward(ref):
            for a in range(3):
                for b in range(3):
                    ref[a * channels : (a + 1) * channels, b * channels : (b + 1) * channels] = (
                        acc[tap_block(a, b), :].T.astype(BF16)
                    )

        def turn(ref):
            for a in range(3):
                for b in range(3):
                    place = (
                        slice(a * channels, (a + 1) * channels),
                        slice(b * channels, (b + 1) * channels),
                    )
                    ref[place] = ref[place].astype(F32).T.astype(BF16)

        def scatter_core(k):
            gather_sent(k)

            def one(i, place):
                agk[(k, *grid_place(i))] = acc[place, :].astype(BF16)

            shards(one)
            for y in range(ny):
                send(
                    agk.at[k, y * 2 + sib], rs1.at[k, y],
                    rs_s.at[k, 0, y], rs_r.at[k, 0, y], sibling,
                )

        def add_up(k, place, parts):
            total = agk[(k, *place)].astype(F32)
            for part in parts:
                total = total + part.astype(F32)
            return total

        def scatter_y(k):
            for y in range(ny):
                wait_bytes(rs1.at[k, y], rs_r.at[k, 0, y])

            def one(i, carry):
                y, j = lax.div(i, gy_size), lax.rem(i, gy_size)
                z, x = lax.div(j, nx), lax.rem(j, nx)
                place = (y * 2 + core, z, x)
                agk[(k, *place)] = add_up(k, place, [rs1[k, y, z, x]]).astype(BF16)
                return carry

            lax.fori_loop(0, ny * gy_size, one, 0)
            for step, py, peer in y_peers():
                send(
                    agk.at[k, py], rs2.at[k, step], rs_s.at[k, 1, step], rs_r.at[k, 1, step], peer
                )

        def scatter_z(k):
            for step in range(ny - 1):
                wait_bytes(rs2.at[k, step], rs_r.at[k, 1, step])

            def one(j, carry):
                z, x = lax.div(j, nx), lax.rem(j, nx)
                place = (my_x, z, x)
                parts = [rs2[k, step, z, x] for step in range(ny - 1)]
                agk[(k, *place)] = add_up(k, place, parts).astype(BF16)
                return carry

            lax.fori_loop(0, gy_size, one, 0)
            for step, pz, peer in z_peers():
                send(
                    agk.at[k, my_x, pz], rs3.at[k, step],
                    rs_s.at[k, 2, step], rs_r.at[k, 2, step], peer,
                )

        def scatter_x(k):
            for step in range(nz - 1):
                wait_bytes(rs3.at[k, step], rs_r.at[k, 2, step])
            for x in range(nx):
                place = (my_x, zz, x)
                parts = [rs3[k, step, x] for step in range(nz - 1)]
                agk[(k, *place)] = add_up(k, place, parts).astype(BF16)
            for step, px, peer in x_peers():
                send(
                    agk.at[k, my_x, zz, px], rs4.at[k, step],
                    rs_s.at[k, 3, step], rs_r.at[k, 3, step], peer,
                )

        def scatter_end(k, out_ref):
            for step in range(nx - 1):
                wait_bytes(rs4.at[k, step], rs_r.at[k, 3, step])
            parts = [rs4[k, step] for step in range(nx - 1)]
            out_ref[...] = add_up(k, (my_x, zz, xx), parts)[:shard]

        def scatter_sent(k):
            for hop, (buf, parts) in enumerate(((rs1, ny), (rs2, ny - 1), (rs3, nz - 1), (rs4, nx - 1))):
                for step in range(parts):
                    wait_bytes(buf.at[k, 0], rs_s.at[k, hop, step])

        def reduce_1(partial):
            ta1[0] = partial
            for step, peer in plane_peers():
                send(ta1.at[0], ta1.at[step + 1], ar_s.at[0, step], ar_r.at[0, step], peer)

        def reduce_2():
            for step in range(ny * nx - 1):
                wait_bytes(ta1.at[0], ar_r.at[0, step])
            ta2[0] = jnp.sum(ta1[...], axis=0)
            for step, _, peer in z_peers():
                send(ta2.at[0], ta2.at[step + 1], ar_s.at[1, step], ar_r.at[1, step], peer)

        def reduce_3():
            for step in range(nz - 1):
                wait_bytes(ta1.at[0], ar_r.at[1, step])
            ta3[0] = jnp.sum(ta2[...], axis=0)
            send(ta3.at[0], ta3.at[1], ar_s.at[2, 0], ar_r.at[2, 0], sibling)

        def reduce_end():
            wait_bytes(ta3.at[0], ar_r.at[2, 0])
            return ta3[0] + ta3[1]

        def reduce_sent():
            for hop, parts in enumerate((ny * nx - 1, nz - 1, 1)):
                for step in range(parts):
                    wait_bytes(ta3.at[0], ar_s.at[hop, step])

        def tell_all(src, buf, which):
            buf[me] = src[...]
            for d in range(1, reach + 1):
                for e in (d, -d):
                    peer = dev(lax.rem(me + e + n, n))
                    send(src, buf.at[me], ex_s.at[which], near_r.at[which], peer)

            def far(step, carry):
                peer = dev(lax.rem(me + step, n))
                send(src, buf.at[me], ex_s.at[which], far_r.at[which], peer)
                return carry

            lax.fori_loop(reach + 1, n - reach, far, 0)

        def near_all(buf, which):
            wait_bytes(buf.at[pl.ds(0, 2 * reach)], near_r.at[which])

        def far_all(buf, which):
            wait_bytes(buf.at[pl.ds(0, n - 1 - 2 * reach)], far_r.at[which])

        def sent_all(buf, which):
            wait_bytes(buf.at[pl.ds(0, n - 1)], ex_s.at[which])

        def tell_near(src, buf, which):
            buf[reach] = src[...]
            for d in range(1, reach + 1):
                for e in (d, -d):
                    peer = dev(lax.rem(me + e + n, n))
                    send(src, buf.at[reach - e], ex_s.at[which], near_r.at[which], peer)

        def near_wait(buf, which):
            wait_bytes(buf.at[pl.ds(0, 2 * reach)], near_r.at[which])

        def near_sent(buf, which):
            wait_bytes(buf.at[pl.ds(0, 2 * reach)], ex_s.at[which])

        def halo(field, which, source=None, first=0, last=batches):
            for g in range(first, last):
                if source is None:
                    low, high = field.at[g, span(rows - 1)], field.at[g, span(0)]
                else:
                    low, high = source.at[g, inner(rows - 1)], source.at[g, inner(0)]
                send(
                    low, field.at[g, span(-1)], halo_s.at[which, 0, g], halo_r.at[which, 0, g],
                    dev(lax.rem(me + 1, n)),
                )
                send(
                    high, field.at[g, span(rows)], halo_s.at[which, 1, g], halo_r.at[which, 1, g],
                    dev(lax.rem(me + n - 1, n)),
                )

        def halo_wait(field, which, g):
            wait_bytes(field.at[g, span(-1)], halo_r.at[which, 0, g])
            wait_bytes(field.at[g, span(rows)], halo_r.at[which, 1, g])

        def halo_sent(field, which):
            for g in range(batches):
                wait_bytes(field.at[g, span(-1)], halo_s.at[which, 0, g])
                wait_bytes(field.at[g, span(rows)], halo_s.at[which, 1, g])

        def keep_halo(field, which, g):
            halo_wait(field, which, g)
            for r in (-1, rows):
                field[g, span(r), :] = keep(g, r, field[g, span(r), :].astype(F32)).astype(BF16)

        def gather_moments(buf):
            counts = per_row(image_count, 1.0)
            total = jnp.zeros((8, channels), F32)
            for e in range(2 * reach + 1):
                weight = per_row([same[g][e] for g in range(batches)] * 2)
                total = total + weight * buf[e]
            mean = total / counts
            squares = pltpu.roll(total, 8 - batches, 0)
            for e in range(2 * reach + 1):
                held = per_row([near_count[g][e] for g in range(batches)])
                shift = buf[e] / jnp.maximum(held, 1.0) - mean
                squares = squares + held * shift * shift
            return mean, lax.rsqrt(jnp.maximum(squares, 0.0) / counts + EPS)

        def gather_sums(buf):
            total = jnp.zeros((8, channels), F32)
            for e in range(-reach, reach + 1):
                weight = per_row([same[g][e + reach] for g in range(batches)] * 2)
                total = total + weight * buf[lax.rem(me + e + n, n)]
            return total, pltpu.roll(total, 8 - batches, 0)

        def pack_tile(plain, cross):
            return jnp.where(row_id < batches, plain, pltpu.roll(cross, batches, 0))

        def local_moments(read, which):
            total = group_sum(stat_tile(which))
            cf[15] = total / jnp.maximum(per_row(own_count, 1.0), 1.0)

            def one(g, carry):
                part = jnp.zeros((8, channels), F32)
                for r in range(rows):
                    gap = keep(g, r, read(g, r) - coef(15, g))
                    part = part + fold(gap * gap)
                st[which + 1, g] = part
                return carry

            lax.fori_loop(0, batches, one, 0)
            msg[which] = pack_tile(total, group_sum(stat_tile(which + 1)))

        def conv(field, weights, g, blocks, back):
            window = []
            for a in range(3):
                shift = (2 - a if back else a) - 1
                parts = [field[g, span(r + shift, count), :] for r, count in blocks]
                window.append(parts[0] if len(parts) == 1 else jnp.concatenate(parts, axis=0))
            result = jnp.dot(
                jnp.concatenate(window, axis=1), weights[...], preferred_element_type=F32
            )
            place = 0
            for r0, count in blocks:
                for q in range(count):
                    r = r0 + q
                    line = result[place * cols : (place + 1) * cols]
                    left, right = line[:, :channels], line[:, 2 * channels :]
                    if back:
                        left, right = right, left
                    left = jnp.where(col_id == 0, 0.0, pltpu.roll(left, 1, 0))
                    right = jnp.where(col_id == cols - 1, 0.0, pltpu.roll(right, cols - 1, 0))
                    yield r, left + line[:, channels : 2 * channels] + right
                    place += 1

        INSIDE = ((1, rows - 2),)
        EDGES = ((0, 1), (rows - 1, 1))

        def each_part(body, first=0, last=batches):
            def one(i, carry):
                if plan.parts == 1:
                    body(i, INSIDE)
                else:
                    count = (rows - 2) // plan.parts
                    body(
                        lax.div(i, plan.parts), ((1 + lax.rem(i, plan.parts) * count, count),)
                    )
                return carry

            lax.fori_loop(first * plan.parts, last * plan.parts, one, 0)

        def each_edge(body):
            def one(g, carry):
                body(g, EDGES)
                return carry

            lax.fori_loop(0, batches, one, 0)

        def each_batch(body):
            def one(g, carry):
                body(g)
                return carry

            lax.fori_loop(0, batches, one, 0)

        def shifted(values):
            right = jnp.where(col_id == 0, 0.0, pltpu.roll(values, 1, 0))
            left = jnp.where(col_id == cols - 1, 0.0, pltpu.roll(values, cols - 1, 0))
            return right, values, left

        def weight_grad_two(step_rows):
            acc[...] = jnp.zeros_like(acc)
            steps = rows // step_rows

            def one(i, carry):
                g = lax.div(i, steps)
                r0 = lax.rem(i, steps) * step_rows
                lines = []
                for q in range(step_rows):
                    right, mid, left = shifted(a2_v[g, span(r0 + q), :].astype(F32))
                    lines.append(jnp.concatenate([right, mid, left], axis=1).astype(BF16))
                lhs = jnp.concatenate(lines, axis=0)
                rhs = jnp.concatenate(
                    [g2_v[g, span(r0 + 1 - a, step_rows), :] for a in range(3)], axis=1
                )
                part = lax.dot_general(
                    lhs, rhs, (((0,), (0,)), ((), ())), preferred_element_type=F32
                )
                for a in range(3):
                    for b in range(3):
                        acc[tap_block(a, b), :] += part[
                            b * channels : (b + 1) * channels, a * channels : (a + 1) * channels
                        ]
                return carry

            lax.fori_loop(0, batches * steps, one, 0)

        def weight_grad_one(step_rows):
            acc[...] = jnp.zeros_like(acc)
            steps = rows // step_rows

            def one(i, carry):
                g = lax.div(i, steps)
                r0 = lax.rem(i, steps) * step_rows
                lines = []
                for q in range(step_rows):
                    right, mid, left = shifted(g1_v[g, span(r0 + q), :].astype(F32))
                    lines.append(jnp.concatenate([left, mid, right], axis=1).astype(BF16))
                rhs = jnp.concatenate(lines, axis=0)
                lhs = jnp.concatenate(
                    [a1_v[g, span(r0 + a - 1, step_rows), :] for a in range(3)], axis=1
                )
                part = lax.dot_general(
                    lhs, rhs, (((0,), (0,)), ((), ())), preferred_element_type=F32
                )
                for a in range(3):
                    for b in range(3):
                        acc[tap_block(a, b), :] += part[
                            a * channels : (a + 1) * channels, b * channels : (b + 1) * channels
                        ]
                return carry

            lax.fori_loop(0, batches * steps, one, 0)

        pl.semaphore_wait(barrier, n - 1)
        spread_start()
        gather_x(1)
        halo(x_v, 0, x_hbm, 0, 1)
        load_x.wait()

        def sum_input(g):
            part = jnp.zeros((8, channels), F32)
            for r in range(rows):
                part = part + fold(keep(g, r, x_v[g, span(r), :].astype(F32)))
            st[0, g] = part

        each_batch(sum_input)
        spread_line()
        tell_all(par_in, pbuf, 4)
        local_moments(lambda g, r: x_v[g, span(r), :].astype(F32), 0)
        tell_near(msg.at[0], nb1, 0)
        spread_plane()
        gather_z(1)
        halo(x_v, 0, x_hbm, 1)
        load_g.wait()

        def keep_grad(g):
            part = jnp.zeros((8, channels), F32)
            for r in range(rows):
                values = keep(g, r, g2_v[g, span(r), :].astype(F32))
                g2_v[g, span(r), :] = values.astype(BF16)
                part = part + fold(values)
            st[4, g] = part

        each_batch(keep_grad)
        embed = emb_in[...].astype(F32).reshape(batches * images, plan.embed)
        embed = silu(embed).astype(BF16)
        pick_r = lax.broadcasted_iota(jnp.int32, (plan.embed, 128), 0)
        pick_c = lax.broadcasted_iota(jnp.int32, (plan.embed, 128), 1)
        pick = jnp.where((pick_r == pick_c + me * embed_rows) & (pick_c < embed_rows), 1.0, 0.0)
        osel[...] = jnp.dot(embed, pick.astype(BF16), preferred_element_type=F32)
        own_tk = jnp.concatenate(
            [tk_in[...].astype(F32), jnp.zeros((128 - embed_rows, 2 * channels), F32)], axis=0
        ).astype(BF16)
        reduce_1(jnp.dot(osel[...].astype(BF16), own_tk, preferred_element_type=F32))
        gather_core(0)

        near_all(pbuf, 4)
        far_all(pbuf, 4)
        tiles = pbuf[:, 0, :].astype(BF16)
        lane_r = lax.broadcasted_iota(jnp.int32, (128, channels), 0)
        lane_c = lax.broadcasted_iota(jnp.int32, (128, channels), 1)
        own_r = lax.broadcasted_iota(jnp.int32, (n, channels), 0)
        own_c = lax.broadcasted_iota(jnp.int32, (n, channels), 1)

        def vector(offset, width, start):
            spread = jnp.where(lane_r == offset + (lane_c & (width - 1)), 1.0, 0.0).astype(BF16)
            values = jnp.dot(tiles, spread, preferred_element_type=F32)
            owner = lax.shift_right_logical(own_c + start, width.bit_length() - 1)
            return jnp.sum(jnp.where(own_r == owner, values, 0.0), axis=0, keepdims=True)

        gain1, shift1, offset1, gain2, shift2, offset2 = (
            vector(i * param_width, param_width, 0) for i in range(6)
        )
        time_low = vector(6 * param_width, time_width, 0)
        time_high = vector(6 * param_width, time_width, channels)
        time_bias = jnp.concatenate([time_low, time_high], axis=1)

        near_wait(nb1, 0)
        mean1, inv1 = gather_moments(nb1)
        cf[0] = mean1
        cf[1] = inv1
        cf[2] = inv1 * gain1
        cf[3] = jnp.broadcast_to(shift1, (8, channels))
        cf[13] = jnp.broadcast_to(offset1, (8, channels))
        cf[14] = jnp.broadcast_to(offset2, (8, channels))

        def pre_one(g, values):
            return (values - coef(0, g)) * coef(2, g) + coef(3, g)

        def act_one(g, r):
            values = pre_one(g, x_v[g, span(r), :].astype(F32))
            a1_v[g, span(r), :] = keep(g, r, silu(values)).astype(BF16)

        def act_rows(g):
            for r in range(rows):
                act_one(g, r)

        each_batch(act_rows)
        gather_end(0)
        assemble(0)
        fill_forward(kf1)

        def hidden_rows(each, pump=None):
            def body(g, blocks):
                if pump is not None:
                    pump(g)
                part = jnp.zeros((8, channels), F32)
                for r, line in conv(a1_v, kf1, g, blocks, False):
                    line = line + coef(13, g)
                    h_v[g, inner(r), :] = line
                    part = part + fold(keep(g, r, line))
                st[2, g] = st[2, g] + part

            each(body)

        st[2] = jnp.zeros((batches, 8, channels), F32)

        def pump_one(g):
            @pl.when(g == 1)
            def _():
                gather_y(1)
                reduce_2()
                halo(g2_v, 1, og_hbm, 0, 1)

            pl.when(g == batches - 1)(lambda: gather_core(1))


        hidden_rows(each_part, pump_one)
        reduce_3()

        gather_end(1)
        assemble(1)
        fill_forward(kf2)
        fill_backward(kb2)

        def back_two(each, *span_of):
            def body(g, blocks):
                for r, line in conv(g2_v, kb2, g, blocks, True):
                    gm_v[g, inner(r), :] = line.astype(plan.held)

            each(body, *span_of)

        back_two(each_part, 0, batches - 1)

        def act_halo(g):
            halo_wait(x_v, 0, g)
            for r in (-1, rows):
                act_one(g, r)

        hidden_rows(each_edge, act_halo)
        local_moments(lambda g, r: h_v[g, inner(r), :], 2)
        tell_near(msg.at[2], nb2, 1)
        halo(g2_v, 1, og_hbm, 1)
        back_two(each_part, batches - 1, batches)
        tout[...] = reduce_end() + time_bias
        picked = []
        image_id = lax.broadcasted_iota(jnp.int32, (images, 2 * channels), 0)
        for g in range(batches):
            block = tout[g * images : (g + 1) * images]
            picked.append(
                jnp.sum(jnp.where(image_id == own_image[g], block, 0.0), axis=0, keepdims=True)
            )
        scale = 1.0 + per_row([item[:, :channels] for item in picked])
        shift = per_row([item[:, channels:] for item in picked])
        near_wait(nb2, 1)
        mean2, inv2 = gather_moments(nb2)
        cf[4] = mean2
        cf[5] = inv2
        cf[6] = inv2 * gain2 * scale
        cf[7] = shift2 * scale + shift

        def modulated(g, values):
            return (values - coef(4, g)) * coef(6, g) + coef(7, g)

        def act_two(g, r):
            values = modulated(g, h_v[g, inner(r), :])
            a2_v[g, span(r), :] = keep(g, r, silu(values)).astype(BF16)

        def act_two_edges(g):
            act_two(g, 0)
            act_two(g, rows - 1)

        def act_two_inside(g):
            plain = jnp.zeros((8, channels), F32)
            cross = jnp.zeros((8, channels), F32)
            for r in range(1, rows - 1):
                gap = h_v[g, inner(r), :] - coef(4, g)
                values = gap * coef(6, g) + coef(7, g)
                gate = 0.5 + 0.5 * jnp.tanh(0.5 * values)
                a2_v[g, span(r), :] = keep(g, r, values * gate).astype(BF16)
                slope = gate * (1.0 + values * (1.0 - gate))
                grad = keep(g, r, gm_v[g, inner(r), :].astype(F32) * slope)
                gm_v[g, inner(r), :] = grad.astype(plan.held)
                plain = plain + fold(grad)
                cross = cross + fold(grad * gap)
            st[0, g] = plain
            st[1, g] = cross

        each_batch(act_two_edges)

        each_batch(act_two_inside)

        def grad_edges(g, blocks):
            keep_halo(g2_v, 1, g)
            plain = jnp.zeros((8, channels), F32)
            cross = jnp.zeros((8, channels), F32)
            for r, line in conv(g2_v, kb2, g, blocks, True):
                gap = h_v[g, inner(r), :] - coef(4, g)
                slope = silu_slope(gap * coef(6, g) + coef(7, g))
                grad = keep(g, r, line * slope)
                gm_v[g, inner(r), :] = grad.astype(plan.held)
                plain = plain + fold(grad)
                cross = cross + fold(grad * gap)
            st[0, g] = st[0, g] + plain
            st[1, g] = (st[1, g] + cross) * coef(5, g)

        each_edge(grad_edges)
        offset_row = jnp.zeros((1, channels), F32)
        for g in range(batches):
            offset_row = offset_row + jnp.sum(st[4, g], axis=0, keepdims=True)
        tile = pack_tile(stat_tile(0), stat_tile(1))
        msg[1] = jnp.where(row_id == 2 * batches, offset_row, tile)
        tell_all(msg.at[1], ex3, 2)
        halo(a2_v, 2, None, 0, batches - 1)

        weight_grad_two(plan.grad_rows)
        scatter_core(1)

        near_all(ex3, 2)
        plain, cross = gather_sums(ex3)
        factor = gain2 * scale
        counts = per_row(image_count, 1.0)
        cf[8] = factor * inv2
        cf[9] = group_sum(factor * plain) / counts * inv2
        cf[10] = group_sum(factor * cross) / counts * inv2 * inv2

        def grad_one(g, r):
            gap = h_v[g, inner(r), :] - coef(4, g)
            values = gm_v[g, inner(r), :].astype(F32) * coef(8, g) - coef(9, g) - gap * coef(10, g)
            low = keep(g, r, values).astype(BF16)
            g1_v[g, span(r), :] = low
            return fold(low.astype(F32))

        def grad_one_edges(g):
            st[4, g] = grad_one(g, 0) + grad_one(g, rows - 1)

        def grad_one_inside(g):
            part = st[4, g]
            for r in range(1, rows - 1):
                part = part + grad_one(g, r)
            st[4, g] = part

        each_batch(grad_one_edges)
        halo(g1_v, 3)
        each_batch(grad_one_inside)

        scatter_y(1)
        weight_grad_one(plan.grad_rows)
        scatter_z(1)
        scatter_core(0)
        turn(kf1)

        def back_one(each, pump=None):
            def body(g, blocks):
                if pump is not None:
                    pump(g)
                plain = jnp.zeros((8, channels), F32)
                cross = jnp.zeros((8, channels), F32)
                for r, line in conv(g1_v, kf1, g, blocks, True):
                    gap = x_v[g, span(r), :].astype(F32) - coef(0, g)
                    grad = keep(g, r, line * silu_slope(gap * coef(2, g) + coef(3, g)))
                    h_v[g, inner(r), :] = grad
                    plain = plain + fold(grad)
                    cross = cross + fold(grad * gap)
                cross = cross * coef(1, g)
                st[0, g] = st[0, g] + plain
                st[1, g] = st[1, g] + cross

            each(body)

        st[0] = jnp.zeros((batches, 8, channels), F32)
        st[1] = jnp.zeros((batches, 8, channels), F32)

        def pump_two(g):
            pl.when(g == 1)(lambda: scatter_y(0))

        def keep_back(blocks, sem):
            for i, (r, count) in enumerate(blocks):
                place = pl.ds(r * cols, count * cols)
                pltpu.make_async_copy(
                    h_v.at[:, place], d1_hbm.at[:, place], back_sem.at[sem + i]
                ).start()

        def keep_wait(blocks, sem):
            for i, (r, count) in enumerate(blocks):
                wait_bytes(h_v.at[:, pl.ds(r * cols, count * cols)], back_sem.at[sem + i])

        back_one(each_part, pump_two)
        keep_back(INSIDE, 2)
        back_one(each_edge, lambda g: keep_halo(g1_v, 3, g))
        keep_back(EDGES, 0)
        offset_row = jnp.zeros((1, channels), F32)
        for g in range(batches):
            offset_row = offset_row + jnp.sum(st[4, g], axis=0, keepdims=True)
        tile = pack_tile(stat_tile(0), stat_tile(1))
        msg[3] = jnp.where(row_id == 2 * batches, offset_row, tile)
        tell_all(msg.at[3], ex4, 3)
        scatter_z(0)
        scatter_x(1)
        halo(a2_v, 2, None, batches - 1)

        def output_rows(each, blocks, buf, sem, pump=None):
            def body(g, blocks):
                if pump is not None:
                    pump(g)
                for r, line in conv(a2_v, kf2, g, blocks, False):
                    line = line + coef(14, g) + x_v[g, span(r), :].astype(F32)
                    buf[g, span(r), :] = keep(g, r, line).astype(BF16)

            each(body)
            for i, (r, count) in enumerate(blocks):
                pltpu.make_async_copy(
                    buf.at[:, span(r, count)], out_hbm.at[:, pl.ds(r * cols, count * cols)],
                    out_sem.at[sem + i],
                ).start()

        def output_wait(blocks, buf, sem):
            for i, (r, count) in enumerate(blocks):
                wait_bytes(buf.at[:, span(r, count)], out_sem.at[sem + i])

        output_rows(each_part, INSIDE, g1_v, 2)
        scatter_x(0)
        halo_sent(g1_v, 3)
        output_rows(each_edge, EDGES, g1_v, 0, lambda g: keep_halo(a2_v, 2, g))

        near_all(ex4, 3)
        plain, cross = gather_sums(ex4)
        cf[11] = group_sum(gain1 * plain) / counts * inv1
        cf[12] = group_sum(gain1 * cross) / counts * inv1 * inv1

        cf_o[0] = cf[0]
        cf_o[1] = cf[2]
        cf_o[2] = cf[11]
        cf_o[3] = cf[12]
        for g in range(batches):
            for r in range(rows):
                wr_o[g, r] = wr_s[g, r + 1]
        scatter_end(1, wg2_o)

        far_all(ex3, 2)
        second_bias = jnp.zeros((1, channels), F32)
        gain_total = jnp.zeros((1, channels), F32)
        shift_total = jnp.zeros((1, channels), F32)
        time_rows = []
        slot_id = lax.broadcasted_iota(jnp.int32, (images, n), 0)
        for g in range(batches):
            hot = jnp.where(slot_v[g : g + 1, :] == slot_id, 1.0, 0.0).astype(F32)
            plain = jnp.dot(hot, ex3[:, g, :], precision=HIGHEST, preferred_element_type=F32)
            cross = jnp.dot(hot, ex3[:, batches + g, :], precision=HIGHEST, preferred_element_type=F32)
            factor = 1.0 + tout[g * images : (g + 1) * images, :channels]
            gain_total = gain_total + jnp.sum(factor * cross, axis=0, keepdims=True)
            shift_total = shift_total + jnp.sum(factor * plain, axis=0, keepdims=True)
            time_rows.append(jnp.concatenate([cross * gain2 + plain * shift2, plain], axis=1))
        second_bias = jnp.sum(ex3[:, 2 * batches, :], axis=0, keepdims=True)
        grad_time = jnp.concatenate(time_rows, axis=0)
        time_total = jnp.sum(grad_time, axis=0, keepdims=True)
        tkg_o[...] = lax.dot_general(
            osel[...], grad_time, (((0,), (0,)), ((), ())), precision=HIGHEST,
            preferred_element_type=F32,
        )[:embed_rows]

        far_all(ex4, 3)
        plain = jnp.zeros((1, channels), F32)
        cross = jnp.zeros((1, channels), F32)
        for g in range(batches):
            plain = plain + jnp.sum(ex4[:, g, :], axis=0, keepdims=True)
            cross = cross + jnp.sum(ex4[:, batches + g, :], axis=0, keepdims=True)
        first_bias = jnp.sum(ex4[:, 2 * batches, :], axis=0, keepdims=True)
        vec_c = lax.broadcasted_iota(jnp.int32, (channels, 128), 0)
        vec_j = lax.broadcasted_iota(jnp.int32, (channels, 128), 1)
        whole = jnp.concatenate(
            [cross, plain, first_bias, gain_total, shift_total, second_bias]
            + [jnp.zeros((2, channels), F32)], axis=0,
        )
        pick = jnp.where(vec_c == vec_j + me * param_width, 1.0, 0.0).astype(F32)
        vec_o[:8] = jnp.dot(whole, pick, precision=HIGHEST, preferred_element_type=F32)
        time_c = lax.broadcasted_iota(jnp.int32, (2 * channels, 128), 0)
        time_j = lax.broadcasted_iota(jnp.int32, (2 * channels, 128), 1)
        pick = jnp.where(time_c == time_j + me * time_width, 1.0, 0.0).astype(F32)
        vec_o[8:] = jnp.dot(
            jnp.broadcast_to(time_total, (8, 2 * channels)), pick, precision=HIGHEST,
            preferred_element_type=F32,
        )
        scatter_end(0, wg1_o)

        keep_wait(INSIDE, 2)
        keep_wait(EDGES, 0)
        output_wait(INSIDE, g1_v, 2)
        output_wait(EDGES, g1_v, 0)
        for k in range(2):
            scatter_sent(k)
        reduce_sent()
        near_sent(nb1, 0)
        near_sent(nb2, 1)
        sent_all(ex3, 2)
        sent_all(ex4, 3)
        sent_all(pbuf, 4)
        for which, field in enumerate((x_v, g2_v, a2_v)):
            halo_sent(field, which)

    margin = (batches, (rows + 2) * cols, channels)
    whole = (batches, rows * cols, channels)
    dma = pltpu.SemaphoreType.DMA
    hops = nx * nz * max(ny - 1, 1)
    few = max(nx * ny, nz)
    scratch = [
        pltpu.VMEM(margin, BF16),
        pltpu.VMEM(margin, BF16),
        pltpu.VMEM(margin, BF16),
        pltpu.VMEM(margin, BF16),
        pltpu.VMEM(margin, BF16),
        pltpu.VMEM(whole, F32),
        pltpu.VMEM(whole, plan.held),
        pltpu.VMEM((3 * channels, 3 * channels), BF16),
        pltpu.VMEM((3 * channels, 3 * channels), BF16),
        pltpu.VMEM((3 * channels, 3 * channels), BF16),
        pltpu.VMEM((2, gx_size, nz, nx, padded, channels), BF16),
        pltpu.VMEM((taps + 16, channels), F32),
        pltpu.VMEM((2, ny, nz, nx, padded, channels), BF16),
        pltpu.VMEM((2, max(ny - 1, 1), nz, nx, padded, channels), BF16),
        pltpu.VMEM((2, max(nz - 1, 1), nx, padded, channels), BF16),
        pltpu.VMEM((2, max(nx - 1, 1), padded, channels), BF16),
        pltpu.VMEM((2 * reach + 1, 8, channels), F32),
        pltpu.VMEM((2 * reach + 1, 8, channels), F32),
        pltpu.VMEM((n, 8, channels), F32),
        pltpu.VMEM((n, 8, channels), F32),
        pltpu.VMEM((n, 1, 128), F32),
        pltpu.VMEM((ny * nx, batches * images, 2 * channels), F32),
        pltpu.VMEM((nz, batches * images, 2 * channels), F32),
        pltpu.VMEM((2, batches * images, 2 * channels), F32),
        pltpu.VMEM((batches * images, 2 * channels), F32),
        pltpu.VMEM((batches * images, 128), F32),
        pltpu.VMEM((4, 8, channels), F32),
        pltpu.VMEM((16, 8, channels), F32),
        pltpu.VMEM((5, batches, 8, channels), F32),
        pltpu.SMEM((batches, 16), jnp.int32),
        dma((2,)),
        dma((4, 2, batches)),
        dma((4, 2, batches)),
        dma((2, 4, hops)),
        dma((2, 4, hops)),
        dma((2, 4, few)),
        dma((2, 4, few)),
        dma((3, few)),
        dma((3, few)),
        dma((5,)),
        dma((5,)),
        dma((5,)),
        dma((3,)),
        dma((3,)),
    ]
    hbm = pl.BlockSpec(memory_space=pl.ANY)
    vmem = pl.BlockSpec(memory_space=pltpu.VMEM)
    smem = pl.BlockSpec(memory_space=pltpu.SMEM)
    return pl.pallas_call(
        kernel,
        name="block",
        out_shape=(
            jax.ShapeDtypeStruct(whole, BF16),
            jax.ShapeDtypeStruct(whole, F32),
            jax.ShapeDtypeStruct((shard, channels), F32),
            jax.ShapeDtypeStruct((shard, channels), F32),
            jax.ShapeDtypeStruct((embed_rows, 2 * channels), F32),
            jax.ShapeDtypeStruct((16, 128), F32),
            jax.ShapeDtypeStruct((4, 8, channels), F32),
            jax.ShapeDtypeStruct((batches, rows), jnp.int32),
        ),
        in_specs=[hbm, hbm, vmem, vmem, vmem, vmem, vmem, vmem, smem, smem],
        out_specs=(hbm, hbm, vmem, vmem, vmem, vmem, vmem, smem),
        scratch_shapes=scratch,
        compiler_params=pltpu.CompilerParams(
            collective_id=0, has_side_effects=True, vmem_limit_bytes=VMEM_LIMIT,
        ),
        cost_estimate=pl.CostEstimate(
            flops=12 * rows * cols * batches * taps * channels,
            bytes_accessed=8 * rows * cols * batches * channels,
            transcendentals=8 * rows * cols * batches * channels,
        ),
    )


VMEM_LIMIT = 63 * 2**20


def build_tail(plan, vectors):
    batches, rows, cols, channels = plan.batches, plan.rows, plan.cols, plan.channels
    step_rows = rows if plan.parts == 1 else 2

    def kernel(
        wr_s, cf, x, og, d1, done, wg1, wg2, tkg, vec, out, gi, wg1_o, wg2_o, tkg_o, *small
    ):
        g, c = pl.program_id(0), pl.program_id(1)
        col_id = lax.broadcasted_iota(jnp.int32, (cols, channels), 0)

        def coef(which):
            return cf[which, pl.ds(g, 1), :]

        for q in range(step_rows):
            place = slice(q * cols, (q + 1) * cols)
            gap = x[0, place].astype(F32) - coef(0)
            values = d1[0, place] * coef(1) - coef(2) - gap * coef(3) + og[0, place].astype(F32)
            width = wr_s[g, c * step_rows + q]
            gi[0, place] = jnp.where(col_id < width, values, 0.0).astype(BF16)
        out[...] = done[...]

        @pl.when((g == 0) & (c == 0))
        def _():
            wg1_o[...] = wg1[...]
            wg2_o[...] = wg2[...]
            tkg_o[...] = tkg[...]
            for ref, (row, size) in zip(small, vectors):
                ref[...] = vec[row, :size]

    block = pl.BlockSpec((1, step_rows * cols, channels), lambda g, c: (g, c, 0))

    def fixed(*shape):
        return pl.BlockSpec(shape, lambda g, c: (0,) * len(shape))

    kernel_grad = fixed(plan.shard, channels)
    time_grad = fixed(plan.embed_rows, 2 * channels)
    whole = (batches, rows * cols, channels)
    return pl.pallas_call(
        kernel,
        name="tail",
        grid=(batches, rows // step_rows),
        in_specs=[
            pl.BlockSpec(memory_space=pltpu.SMEM), fixed(4, 8, channels),
            block, block, block, block,
            kernel_grad, kernel_grad, time_grad, fixed(16, 128),
        ],
        out_specs=[block, block, kernel_grad, kernel_grad, time_grad]
        + [fixed(size) for _, size in vectors],
        out_shape=[
            jax.ShapeDtypeStruct(whole, BF16),
            jax.ShapeDtypeStruct(whole, BF16),
            jax.ShapeDtypeStruct((plan.shard, channels), F32),
            jax.ShapeDtypeStruct((plan.shard, channels), F32),
            jax.ShapeDtypeStruct((plan.embed_rows, 2 * channels), F32),
        ]
        + [jax.ShapeDtypeStruct((size,), F32) for _, size in vectors],
        compiler_params=pltpu.CompilerParams(
            vmem_limit_bytes=VMEM_LIMIT, dimension_semantics=("arbitrary", "arbitrary")
        ),
    )


def make_body(mesh_shape):
    def body(
        input_cells, time_embed, first_gain, first_shift, first_kernel, first_offset,
        time_kernel, time_offset, second_gain, second_shift, second_kernel, second_offset,
        output_grad, slot_image, image_height,
    ):
        cells = input_cells.shape
        plan = Plan(
            mesh_shape, cells, time_embed.shape, slot_image.shape,
            first_kernel.shape[0], time_kernel.shape[0],
        )
        flat = (cells[0], cells[1] * cells[2], cells[3])
        params = jnp.concatenate(
            [first_gain, first_shift, first_offset, second_gain, second_shift, second_offset,
             time_offset]
        ).astype(F32)
        params = jnp.pad(params[None, :], ((0, 0), (0, 128 - params.shape[0])))
        cells_in, cells_grad = input_cells.reshape(flat), output_grad.reshape(flat)
        done, part, wg1, wg2, tkg, vec, cf, widths = build_kernel(plan)(
            cells_in, cells_grad, first_kernel, second_kernel,
            params, time_embed, time_kernel, slot_image, slot_image, image_height,
        )
        width = first_gain.shape[0]
        vectors = [(i, width) for i in range(6)] + [(8, time_offset.shape[0])]
        out, grad, wg1, wg2, tkg, *rows = build_tail(plan, vectors)(
            widths, cf, cells_in, cells_grad, part, done, wg1, wg2, tkg, vec
        )
        return (
            out.reshape(cells), grad.reshape(cells), rows[0], rows[1], wg1, rows[2],
            tkg, rows[6], rows[3], rows[4], wg2, rows[5],
        )

    return body


def solution(mesh):
    both = ("gx", "gy")
    cells, vector, matrix, whole = P(None, both, None, None), P(both), P(both, None), P()
    return jax.shard_map(
        make_body(dict(mesh.shape)),
        mesh=mesh,
        in_specs=(
            cells, whole, vector, vector, matrix, vector, matrix, vector, vector, vector, matrix,
            vector, cells, whole, whole,
        ),
        out_specs=(
            cells, cells, vector, vector, matrix, vector, matrix, vector, vector, vector, matrix,
            vector,
        ),
        check_vma=False,
    )
```

```python
import jax
import jax.numpy as jnp
from jax import lax
from jax.experimental import pallas as pl
from jax.experimental.pallas import tpu as pltpu
from jax.sharding import PartitionSpec as P

NORM_GROUPS = 32
EPS = 1e-05
HIGHEST = lax.Precision.HIGHEST
MESH = pl.DeviceIdType.MESH
F32 = jnp.float32
BF16 = jnp.bfloat16


def silu(values):
    return values * (0.5 + 0.5 * jnp.tanh(0.5 * values))


def silu_slope(values):
    gate = 0.5 + 0.5 * jnp.tanh(0.5 * values)
    return gate * (1.0 + values * (1.0 - gate))


def fold(values):
    rows, channels = values.shape
    return jnp.sum(values.reshape(rows // 8, 8, channels), axis=0)


class Plan:
    def __init__(self, mesh_shape, cells, time_embed, slot_image, kernel_rows, embed_rows):
        self.gx, self.gy = mesh_shape["gx"], mesh_shape["gy"]
        self.n = self.gx * self.gy
        self.ny = self.gx // 2
        self.nx = self.ny if self.gy % self.ny == 0 else 1
        self.nz = self.gy // self.nx
        self.batches, self.rows, self.cols, self.channels = cells
        self.images, self.embed = time_embed[1], time_embed[2]
        self.reach = slot_image[1] * 5 // 32 - 1
        self.shard = kernel_rows
        self.padded = (kernel_rows + 15) // 16 * 16
        self.embed_rows = embed_rows
        tight = self.n > 64
        self.parts, self.grad_rows, self.held = (2, 2, BF16) if tight else (1, 8, F32)


def build_kernel(plan):
    n, gx_size, gy_size = plan.n, plan.gx, plan.gy
    nx, ny, nz = plan.nx, plan.ny, plan.nz
    batches, rows, cols, channels = plan.batches, plan.rows, plan.cols, plan.channels
    images, reach = plan.images, plan.reach
    shard, padded, embed_rows = plan.shard, plan.padded, plan.embed_rows
    group = channels // NORM_GROUPS
    group_shift = group.bit_length() - 1
    narrow = cols * 3 // 5
    taps = 9 * channels
    param_width = channels // n
    time_width = 2 * channels // n

    def kernel(
        x_hbm, og_hbm, k1_in, k2_in, par_in, emb_in, tk_in, slot_v, slot_s, high_s,
        out_hbm, d1_hbm, wg1_o, wg2_o, tkg_o, vec_o, cf_o, wr_o,
        x_v, g2_v, a1_v, a2_v, g1_v, h_v, gm_v, kf1, kf2, kb2, agk, acc,
        rs1, rs2, rs3, rs4, nb1, nb2, ex3, ex4, pbuf, ta1, ta2, ta3, tout,
        osel, msg, cf, st, wr_s,
        ld_sem, halo_s, halo_r, ag_s, ag_r, rs_s, rs_r, ar_s, ar_r, ex_s, near_r, far_r, out_sem, back_sem,
    ):
        my_x = lax.axis_index("gx")
        my_y = lax.axis_index("gy")
        me = my_x * gy_size + my_y
        core = lax.rem(my_x, 2)
        yy = lax.div(my_x, 2)
        zz = lax.div(my_y, nx)
        xx = lax.rem(my_y, nx)
        sib = 1 - core

        def dev(index):
            return (lax.div(index, gy_size), lax.rem(index, gy_size))

        def wait_bytes(ref, sem):
            pltpu.make_async_copy(ref, ref, sem).wait()

        def send(src, dst, send_sem, recv_sem, device):
            pltpu.make_async_remote_copy(
                src_ref=src, dst_ref=dst, send_sem=send_sem, recv_sem=recv_sem,
                device_id=device, device_id_type=MESH,
            ).start()

        load_x = pltpu.make_async_copy(x_hbm, x_v.at[:, pl.ds(cols, rows * cols)], ld_sem.at[0])
        load_g = pltpu.make_async_copy(og_hbm, g2_v.at[:, pl.ds(cols, rows * cols)], ld_sem.at[1])
        load_x.start()
        load_g.start()
        barrier = pltpu.get_barrier_semaphore()

        def greet(step, carry):
            pl.semaphore_signal(
                barrier, inc=1, device_id=dev(lax.rem(me + step, n)), device_id_type=MESH
            )
            return carry

        lax.fori_loop(1, n, greet, 0)

        for which, ref in enumerate((k1_in, k2_in)):
            own = ref[...].astype(F32)
            if padded > shard:
                own = jnp.concatenate([own, jnp.zeros((padded - shard, channels), F32)], axis=0)
            agk[which, my_x, zz, xx] = own.astype(BF16)

        same = []
        near_count = []
        own_count = []
        image_count = []
        own_image = []
        for g in range(batches):
            image = slot_s[g, me]
            before = jnp.int32(0)
            links = []
            for e in range(-reach, reach + 1):
                place = me + e
                inside = jnp.where((place >= 0) & (place < n), 1, 0)
                other = slot_s[g, jnp.clip(place, 0, n - 1)]
                link = inside * jnp.where(other == image, 1, 0)
                links.append(link)
                if e < 0:
                    before = before + link
            height = high_s[g, image]
            width = jnp.where(image < images // 2, cols, narrow)
            for r in range(-1, rows + 1):
                row_ok = jnp.where(before * rows + r < height, 1, 0)
                if r == -1:
                    row_ok = row_ok * links[reach - 1]
                if r == rows:
                    row_ok = row_ok * links[reach + 1]
                wr_s[g, r + 1] = row_ok * width
            counts = []
            for e in range(-reach, reach + 1):
                held = jnp.clip(height - (before + e) * rows, 0, rows) * links[e + reach]
                counts.append((held * width * group).astype(F32))
            same.append([link.astype(F32) for link in links])
            near_count.append(counts)
            own_count.append(counts[reach])
            image_count.append((height * width * group).astype(F32))
            own_image.append(image)

        row_id = lax.broadcasted_iota(jnp.int32, (8, channels), 0)
        col_id = lax.broadcasted_iota(jnp.int32, (cols, channels), 0)
        grp_r = lax.broadcasted_iota(jnp.int32, (channels, channels), 0)
        grp_c = lax.broadcasted_iota(jnp.int32, (channels, channels), 1)

        def per_row(values, rest=0.0):
            total = jnp.full((8, channels), rest, F32)
            for i, value in enumerate(values):
                total = jnp.where(row_id == i, value, total)
            return total

        def group_sum(tile):
            block = jnp.where(
                lax.shift_right_logical(grp_r, group_shift)
                == lax.shift_right_logical(grp_c, group_shift),
                1.0, 0.0,
            ).astype(F32)
            return jnp.dot(tile, block, precision=HIGHEST, preferred_element_type=F32)

        def keep(g, r, values):
            return jnp.where(col_id < wr_s[g, r + 1], values, 0.0)

        def span(r, count=1):
            start = (r + 1) * cols
            if not isinstance(start, int):
                start = pl.multiple_of(start, cols)
            return pl.ds(start, count * cols)

        def inner(r):
            start = r * cols
            if not isinstance(start, int):
                start = pl.multiple_of(start, cols)
            return pl.ds(start, cols)

        def coef(which, g):
            return cf[which, pl.ds(g, 1), :]

        def stat_tile(which):
            return per_row([jnp.sum(st[which, g], axis=0, keepdims=True) for g in range(batches)])

        def x_peers():
            for dx in range(1, nx):
                px = lax.rem(xx + dx, nx)
                yield dx - 1, px, (my_x, zz * nx + px)

        def y_peers():
            for dy in range(1, ny):
                py = lax.rem(yy + dy, ny) * 2 + core
                yield dy - 1, py, (py, my_y)

        def z_peers():
            for dz in range(1, nz):
                pz = lax.rem(zz + dz, nz)
                yield dz - 1, pz, (my_x, pz * nx + xx)

        def plane_peers():
            for step in range(1, ny * nx):
                py = lax.rem(yy + step // nx, ny)
                px = lax.rem(xx + step % nx, nx)
                yield step - 1, (py * 2 + core, zz * nx + px)

        sibling = (yy * 2 + sib, my_y)

        def gather_send(k, hop, step, part, peer):
            send(part, part, ag_s.at[k, hop, step], ag_r.at[k, hop, step], peer)

        def gather_wait(k, hop, parts, ref):
            for step in range(parts):
                wait_bytes(ref, ag_r.at[k, hop, step])

        def gather_sent(k):
            for hop, parts, ref in gather_plan(k):
                for step in range(parts):
                    wait_bytes(ref, ag_s.at[k, hop, step])

        def gather_plan(k):
            one, row, plane = agk.at[k, 0, 0, 0], agk.at[k, 0, 0], agk.at[k, 0]
            if k == 0:
                return (
                    (0, nz - 1, one), (1, nz * (nx - 1), one), (2, nx * nz * (ny - 1), one),
                    (3, ny, plane),
                )
            return (0, nx - 1, one), (1, nz - 1, row), (2, nz * (ny - 1), row), (3, ny, plane)

        def came(dz, dx):
            return agk.at[0, my_x, lax.rem(zz - dz + nz, nz), lax.rem(xx - dx + nx, nx)]

        def pass_x(dz):
            for step, px, peer in x_peers():
                gather_send(0, 1, dz * (nx - 1) + step, came(dz, 0), peer)

        def pass_y(dz, dx):
            for step, py, peer in y_peers():
                gather_send(0, 2, (dz * nx + dx) * (ny - 1) + step, came(dz, dx), peer)

        def spread_start():
            for step, pz, peer in z_peers():
                gather_send(0, 0, step, came(0, 0), peer)
            pass_x(0)
            pass_y(0, 0)

        def spread_line():
            for dz in range(1, nz):
                wait_bytes(agk.at[0, 0, 0, 0], ag_r.at[0, 0, dz - 1])
                pass_x(dz)
                pass_y(dz, 0)

        def spread_plane():
            for dz in range(nz):
                for dx in range(1, nx):
                    wait_bytes(agk.at[0, 0, 0, 0], ag_r.at[0, 1, dz * (nx - 1) + dx - 1])
                    pass_y(dz, dx)

        def gather_x(k):
            for step, px, peer in x_peers():
                gather_send(k, 0, step, agk.at[k, my_x, zz, xx], peer)

        def forward_y(k, dz):
            row = agk.at[k, my_x, lax.rem(zz - dz + nz, nz)]
            for step, py, peer in y_peers():
                gather_send(k, 2, dz * (ny - 1) + step, row, peer)

        def gather_z(k):
            gather_wait(k, 0, nx - 1, agk.at[k, 0, 0, 0])
            for step, pz, peer in z_peers():
                gather_send(k, 1, step, agk.at[k, my_x, zz], peer)
            forward_y(k, 0)

        def gather_y(k, first=1, last=nz):
            for dz in range(first, last):
                wait_bytes(agk.at[k, 0, 0], ag_r.at[k, 1, dz - 1])
                forward_y(k, dz)

        def gather_core(k):
            hop, parts, ref = gather_plan(k)[2]
            gather_wait(k, hop, parts, ref)
            for y in range(ny):
                gather_send(k, 3, y, agk.at[k, y * 2 + core], sibling)

        def gather_end(k):
            gather_wait(k, 3, ny, agk.at[k, 0])

        def grid_place(i):
            left = lax.rem(i, gy_size)
            return lax.div(i, gy_size), lax.div(left, nx), lax.rem(left, nx)

        def shards(body):
            if shard % 8 == 0:
                def step(i, carry):
                    body(i, pl.ds(pl.multiple_of(i * shard, 8), padded))
                    return carry

                lax.fori_loop(0, n, step, 0)
            else:
                for i in range(n):
                    body(i, pl.ds(i * shard, padded))

        def assemble(k):
            def one(i, place):
                acc[place, :] = agk[(k, *grid_place(i))].astype(F32)

            shards(one)

        def tap_block(a, b):
            return pl.ds((3 * a + b) * channels, channels)

        def fill_forward(ref):
            for a in range(3):
                for b in range(3):
                    ref[a * channels : (a + 1) * channels, b * channels : (b + 1) * channels] = acc[
                        tap_block(a, b), :
                    ].astype(BF16)

        def fill_backward(ref):
            for a in range(3):
                for b in range(3):
                    ref[a * channels : (a + 1) * channels, b * channels : (b + 1) * channels] = (
                        acc[tap_block(a, b), :].T.astype(BF16)
                    )

        def turn(ref):
            for a in range(3):
                for b in range(3):
                    place = (
                        slice(a * channels, (a + 1) * channels),
                        slice(b * channels, (b + 1) * channels),
                    )
                    ref[place] = ref[place].astype(F32).T.astype(BF16)

        def scatter_core(k):
            gather_sent(k)

            def one(i, place):
                agk[(k, *grid_place(i))] = acc[place, :].astype(BF16)

            shards(one)
            for y in range(ny):
                send(
                    agk.at[k, y * 2 + sib], rs1.at[k, y],
                    rs_s.at[k, 0, y], rs_r.at[k, 0, y], sibling,
                )

        def add_up(k, place, parts):
            total = agk[(k, *place)].astype(F32)
            for part in parts:
                total = total + part.astype(F32)
            return total

        def scatter_y(k):
            for y in range(ny):
                wait_bytes(rs1.at[k, y], rs_r.at[k, 0, y])

            def one(i, carry):
                y, j = lax.div(i, gy_size), lax.rem(i, gy_size)
                z, x = lax.div(j, nx), lax.rem(j, nx)
                place = (y * 2 + core, z, x)
                agk[(k, *place)] = add_up(k, place, [rs1[k, y, z, x]]).astype(BF16)
                return carry

            lax.fori_loop(0, ny * gy_size, one, 0)
            for step, py, peer in y_peers():
                send(
                    agk.at[k, py], rs2.at[k, step], rs_s.at[k, 1, step], rs_r.at[k, 1, step], peer
                )

        def scatter_z(k):
            for step in range(ny - 1):
                wait_bytes(rs2.at[k, step], rs_r.at[k, 1, step])

            def one(j, carry):
                z, x = lax.div(j, nx), lax.rem(j, nx)
                place = (my_x, z, x)
                parts = [rs2[k, step, z, x] for step in range(ny - 1)]
                agk[(k, *place)] = add_up(k, place, parts).astype(BF16)
                return carry

            lax.fori_loop(0, gy_size, one, 0)
            for step, pz, peer in z_peers():
                send(
                    agk.at[k, my_x, pz], rs3.at[k, step],
                    rs_s.at[k, 2, step], rs_r.at[k, 2, step], peer,
                )

        def scatter_x(k):
            for step in range(nz - 1):
                wait_bytes(rs3.at[k, step], rs_r.at[k, 2, step])
            for x in range(nx):
                place = (my_x, zz, x)
                parts = [rs3[k, step, x] for step in range(nz - 1)]
                agk[(k, *place)] = add_up(k, place, parts).astype(BF16)
            for step, px, peer in x_peers():
                send(
                    agk.at[k, my_x, zz, px], rs4.at[k, step],
                    rs_s.at[k, 3, step], rs_r.at[k, 3, step], peer,
                )

        def scatter_end(k, out_ref):
            for step in range(nx - 1):
                wait_bytes(rs4.at[k, step], rs_r.at[k, 3, step])
            parts = [rs4[k, step] for step in range(nx - 1)]
            out_ref[...] = add_up(k, (my_x, zz, xx), parts)[:shard]

        def scatter_sent(k):
            for hop, (buf, parts) in enumerate(((rs1, ny), (rs2, ny - 1), (rs3, nz - 1), (rs4, nx - 1))):
                for step in range(parts):
                    wait_bytes(buf.at[k, 0], rs_s.at[k, hop, step])

        def reduce_1(partial):
            ta1[0] = partial
            for step, peer in plane_peers():
                send(ta1.at[0], ta1.at[step + 1], ar_s.at[0, step], ar_r.at[0, step], peer)

        def reduce_2():
            for step in range(ny * nx - 1):
                wait_bytes(ta1.at[0], ar_r.at[0, step])
            ta2[0] = jnp.sum(ta1[...], axis=0)
            for step, _, peer in z_peers():
                send(ta2.at[0], ta2.at[step + 1], ar_s.at[1, step], ar_r.at[1, step], peer)

        def reduce_3():
            for step in range(nz - 1):
                wait_bytes(ta1.at[0], ar_r.at[1, step])
            ta3[0] = jnp.sum(ta2[...], axis=0)
            send(ta3.at[0], ta3.at[1], ar_s.at[2, 0], ar_r.at[2, 0], sibling)

        def reduce_end():
            wait_bytes(ta3.at[0], ar_r.at[2, 0])
            return ta3[0] + ta3[1]

        def reduce_sent():
            for hop, parts in enumerate((ny * nx - 1, nz - 1, 1)):
                for step in range(parts):
                    wait_bytes(ta3.at[0], ar_s.at[hop, step])

        def tell_all(src, buf, which):
            buf[me] = src[...]
            for d in range(1, reach + 1):
                for e in (d, -d):
                    peer = dev(lax.rem(me + e + n, n))
                    send(src, buf.at[me], ex_s.at[which], near_r.at[which], peer)

            def far(step, carry):
                peer = dev(lax.rem(me + step, n))
                send(src, buf.at[me], ex_s.at[which], far_r.at[which], peer)
                return carry

            lax.fori_loop(reach + 1, n - reach, far, 0)

        def near_all(buf, which):
            wait_bytes(buf.at[pl.ds(0, 2 * reach)], near_r.at[which])

        def far_all(buf, which):
            wait_bytes(buf.at[pl.ds(0, n - 1 - 2 * reach)], far_r.at[which])

        def sent_all(buf, which):
            wait_bytes(buf.at[pl.ds(0, n - 1)], ex_s.at[which])

        def tell_near(src, buf, which):
            buf[reach] = src[...]
            for d in range(1, reach + 1):
                for e in (d, -d):
                    peer = dev(lax.rem(me + e + n, n))
                    send(src, buf.at[reach - e], ex_s.at[which], near_r.at[which], peer)

        def near_wait(buf, which):
            wait_bytes(buf.at[pl.ds(0, 2 * reach)], near_r.at[which])

        def near_sent(buf, which):
            wait_bytes(buf.at[pl.ds(0, 2 * reach)], ex_s.at[which])

        def halo(field, which, source=None, first=0, last=batches):
            for g in range(first, last):
                if source is None:
                    low, high = field.at[g, span(rows - 1)], field.at[g, span(0)]
                else:
                    low, high = source.at[g, inner(rows - 1)], source.at[g, inner(0)]
                send(
                    low, field.at[g, span(-1)], halo_s.at[which, 0, g], halo_r.at[which, 0, g],
                    dev(lax.rem(me + 1, n)),
                )
                send(
                    high, field.at[g, span(rows)], halo_s.at[which, 1, g], halo_r.at[which, 1, g],
                    dev(lax.rem(me + n - 1, n)),
                )

        def halo_wait(field, which, g):
            wait_bytes(field.at[g, span(-1)], halo_r.at[which, 0, g])
            wait_bytes(field.at[g, span(rows)], halo_r.at[which, 1, g])

        def halo_sent(field, which):
            for g in range(batches):
                wait_bytes(field.at[g, span(-1)], halo_s.at[which, 0, g])
                wait_bytes(field.at[g, span(rows)], halo_s.at[which, 1, g])

        def keep_halo(field, which, g):
            halo_wait(field, which, g)
            for r in (-1, rows):
                field[g, span(r), :] = keep(g, r, field[g, span(r), :].astype(F32)).astype(BF16)

        def gather_moments(buf):
            counts = per_row(image_count, 1.0)
            total = jnp.zeros((8, channels), F32)
            for e in range(2 * reach + 1):
                weight = per_row([same[g][e] for g in range(batches)] * 2)
                total = total + weight * buf[e]
            mean = total / counts
            squares = pltpu.roll(total, 8 - batches, 0)
            for e in range(2 * reach + 1):
                held = per_row([near_count[g][e] for g in range(batches)])
                shift = buf[e] / jnp.maximum(held, 1.0) - mean
                squares = squares + held * shift * shift
            return mean, lax.rsqrt(jnp.maximum(squares, 0.0) / counts + EPS)

        def gather_sums(buf):
            total = jnp.zeros((8, channels), F32)
            for e in range(-reach, reach + 1):
                weight = per_row([same[g][e + reach] for g in range(batches)] * 2)
                total = total + weight * buf[lax.rem(me + e + n, n)]
            return total, pltpu.roll(total, 8 - batches, 0)

        def pack_tile(plain, cross):
            return jnp.where(row_id < batches, plain, pltpu.roll(cross, batches, 0))

        def local_moments(read, which):
            total = group_sum(stat_tile(which))
            cf[15] = total / jnp.maximum(per_row(own_count, 1.0), 1.0)

            def one(g, carry):
                part = jnp.zeros((8, channels), F32)
                for r in range(rows):
                    gap = keep(g, r, read(g, r) - coef(15, g))
                    part = part + fold(gap * gap)
                st[which + 1, g] = part
                return carry

            lax.fori_loop(0, batches, one, 0)
            msg[which] = pack_tile(total, group_sum(stat_tile(which + 1)))

        def conv(field, weights, g, blocks, back):
            window = []
            for a in range(3):
                shift = (2 - a if back else a) - 1
                parts = [field[g, span(r + shift, count), :] for r, count in blocks]
                window.append(parts[0] if len(parts) == 1 else jnp.concatenate(parts, axis=0))
            result = jnp.dot(
                jnp.concatenate(window, axis=1), weights[...], preferred_element_type=F32
            )
            place = 0
            for r0, count in blocks:
                for q in range(count):
                    r = r0 + q
                    line = result[place * cols : (place + 1) * cols]
                    left, right = line[:, :channels], line[:, 2 * channels :]
                    if back:
                        left, right = right, left
                    left = jnp.where(col_id == 0, 0.0, pltpu.roll(left, 1, 0))
                    right = jnp.where(col_id == cols - 1, 0.0, pltpu.roll(right, cols - 1, 0))
                    yield r, left + line[:, channels : 2 * channels] + right
                    place += 1

        INSIDE = ((1, rows - 2),)
        EDGES = ((0, 1), (rows - 1, 1))

        def each_part(body, first=0, last=batches, pump=None):
            def one(i, carry):
                g, part = lax.div(i, plan.parts), lax.rem(i, plan.parts)
                if pump is not None:
                    pl.when(part == 0)(lambda: pump(g))
                count = (rows - 2) // plan.parts
                body(g, INSIDE if plan.parts == 1 else ((1 + part * count, count),))
                return carry

            lax.fori_loop(first * plan.parts, last * plan.parts, one, 0)

        def each_edge(body, pump=None):
            def one(g, carry):
                if pump is not None:
                    pump(g)
                body(g, EDGES)
                return carry

            lax.fori_loop(0, batches, one, 0)

        def each_batch(body):
            def one(g, carry):
                body(g)
                return carry

            lax.fori_loop(0, batches, one, 0)

        def shifted(values):
            right = jnp.where(col_id == 0, 0.0, pltpu.roll(values, 1, 0))
            left = jnp.where(col_id == cols - 1, 0.0, pltpu.roll(values, cols - 1, 0))
            return right, values, left

        def weight_grad_two(step_rows):
            acc[...] = jnp.zeros_like(acc)
            steps = rows // step_rows

            def one(i, carry):
                g = lax.div(i, steps)
                r0 = lax.rem(i, steps) * step_rows
                lines = []
                for q in range(step_rows):
                    right, mid, left = shifted(a2_v[g, span(r0 + q), :].astype(F32))
                    lines.append(jnp.concatenate([right, mid, left], axis=1).astype(BF16))
                lhs = jnp.concatenate(lines, axis=0)
                rhs = jnp.concatenate(
                    [g2_v[g, span(r0 + 1 - a, step_rows), :] for a in range(3)], axis=1
                )
                part = lax.dot_general(
                    lhs, rhs, (((0,), (0,)), ((), ())), preferred_element_type=F32
                )
                for a in range(3):
                    for b in range(3):
                        acc[tap_block(a, b), :] += part[
                            b * channels : (b + 1) * channels, a * channels : (a + 1) * channels
                        ]
                return carry

            lax.fori_loop(0, batches * steps, one, 0)

        def weight_grad_one(step_rows):
            acc[...] = jnp.zeros_like(acc)
            steps = rows // step_rows

            def one(i, carry):
                g = lax.div(i, steps)
                r0 = lax.rem(i, steps) * step_rows
                lines = []
                for q in range(step_rows):
                    right, mid, left = shifted(g1_v[g, span(r0 + q), :].astype(F32))
                    lines.append(jnp.concatenate([left, mid, right], axis=1).astype(BF16))
                rhs = jnp.concatenate(lines, axis=0)
                lhs = jnp.concatenate(
                    [a1_v[g, span(r0 + a - 1, step_rows), :] for a in range(3)], axis=1
                )
                part = lax.dot_general(
                    lhs, rhs, (((0,), (0,)), ((), ())), preferred_element_type=F32
                )
                for a in range(3):
                    for b in range(3):
                        acc[tap_block(a, b), :] += part[
                            a * channels : (a + 1) * channels, b * channels : (b + 1) * channels
                        ]
                return carry

            lax.fori_loop(0, batches * steps, one, 0)

        embed = emb_in[...].astype(F32).reshape(batches * images, plan.embed)
        embed = silu(embed).astype(BF16)
        pick_r = lax.broadcasted_iota(jnp.int32, (plan.embed, 128), 0)
        pick_c = lax.broadcasted_iota(jnp.int32, (plan.embed, 128), 1)
        pick = jnp.where((pick_r == pick_c + me * embed_rows) & (pick_c < embed_rows), 1.0, 0.0)
        osel[...] = jnp.dot(embed, pick.astype(BF16), preferred_element_type=F32)
        own_tk = jnp.concatenate(
            [tk_in[...].astype(F32), jnp.zeros((128 - embed_rows, 2 * channels), F32)], axis=0
        ).astype(BF16)
        partial = (jnp.dot(osel[...].astype(BF16), own_tk, preferred_element_type=F32))
        pl.semaphore_wait(barrier, n - 1)
        spread_start()
        gather_x(1)
        load_x.wait()

        def sum_input(g):
            part = jnp.zeros((8, channels), F32)
            for r in range(rows):
                part = part + fold(keep(g, r, x_v[g, span(r), :].astype(F32)))
            st[0, g] = part

        each_batch(sum_input)
        spread_line()
        tell_all(par_in, pbuf, 4)
        halo(x_v, 0, x_hbm, 0, 1)
        local_moments(lambda g, r: x_v[g, span(r), :].astype(F32), 0)
        tell_near(msg.at[0], nb1, 0)
        reduce_1(partial)
        spread_plane()
        gather_z(1)
        halo(x_v, 0, x_hbm, 1)
        load_g.wait()

        def keep_grad(g):
            part = jnp.zeros((8, channels), F32)
            for r in range(rows):
                values = keep(g, r, g2_v[g, span(r), :].astype(F32))
                g2_v[g, span(r), :] = values.astype(BF16)
                part = part + fold(values)
            st[4, g] = part

        each_batch(keep_grad)
        gather_core(0)

        near_all(pbuf, 4)
        far_all(pbuf, 4)
        tiles = pbuf[:, 0, :].astype(BF16)
        lane_r = lax.broadcasted_iota(jnp.int32, (128, channels), 0)
        lane_c = lax.broadcasted_iota(jnp.int32, (128, channels), 1)
        own_r = lax.broadcasted_iota(jnp.int32, (n, channels), 0)
        own_c = lax.broadcasted_iota(jnp.int32, (n, channels), 1)

        def vector(offset, width, start):
            spread = jnp.where(lane_r == offset + (lane_c & (width - 1)), 1.0, 0.0).astype(BF16)
            values = jnp.dot(tiles, spread, preferred_element_type=F32)
            owner = lax.shift_right_logical(own_c + start, width.bit_length() - 1)
            return jnp.sum(jnp.where(own_r == owner, values, 0.0), axis=0, keepdims=True)

        gain1, shift1, offset1, gain2, shift2, offset2 = (
            vector(i * param_width, param_width, 0) for i in range(6)
        )
        time_low = vector(6 * param_width, time_width, 0)
        time_high = vector(6 * param_width, time_width, channels)
        time_bias = jnp.concatenate([time_low, time_high], axis=1)

        near_wait(nb1, 0)
        mean1, inv1 = gather_moments(nb1)
        cf[0] = mean1
        cf[1] = inv1
        cf[2] = inv1 * gain1
        cf[3] = jnp.broadcast_to(shift1, (8, channels))
        cf[13] = jnp.broadcast_to(offset1, (8, channels))
        cf[14] = jnp.broadcast_to(offset2, (8, channels))

        def pre_one(g, values):
            return (values - coef(0, g)) * coef(2, g) + coef(3, g)

        def act_one(g, r):
            values = pre_one(g, x_v[g, span(r), :].astype(F32))
            a1_v[g, span(r), :] = keep(g, r, silu(values)).astype(BF16)

        def act_rows(g):
            for r in range(rows):
                act_one(g, r)

        each_batch(act_rows)
        gather_end(0)
        assemble(0)
        fill_forward(kf1)

        def hidden_rows(each, pump=None):
            def body(g, blocks):
                part = jnp.zeros((8, channels), F32)
                for r, line in conv(a1_v, kf1, g, blocks, False):
                    line = line + coef(13, g)
                    h_v[g, inner(r), :] = line
                    part = part + fold(keep(g, r, line))
                st[2, g] = st[2, g] + part

            each(body, pump=pump)

        st[2] = jnp.zeros((batches, 8, channels), F32)

        def pump_one(g):
            @pl.when(g == 1)
            def _():
                gather_y(1)
                reduce_2()
                halo(g2_v, 1, og_hbm, 0, 1)

            pl.when(g == batches - 1)(lambda: gather_core(1))

        hidden_rows(each_part, pump_one)

        gather_end(1)
        assemble(1)
        fill_forward(kf2)
        fill_backward(kb2)

        def back_two(each, *span_of):
            def body(g, blocks):
                for r, line in conv(g2_v, kb2, g, blocks, True):
                    gm_v[g, inner(r), :] = line.astype(plan.held)

            each(body, *span_of)

        back_two(each_part, 0, batches - 1)

        def act_halo(g):
            halo_wait(x_v, 0, g)
            for r in (-1, rows):
                act_one(g, r)

        reduce_3()
        hidden_rows(each_edge, act_halo)
        local_moments(lambda g, r: h_v[g, inner(r), :], 2)
        tell_near(msg.at[2], nb2, 1)
        halo(g2_v, 1, og_hbm, 1)
        back_two(each_part, batches - 1, batches)
        tout[...] = reduce_end() + time_bias
        picked = []
        image_id = lax.broadcasted_iota(jnp.int32, (images, 2 * channels), 0)
        for g in range(batches):
            block = tout[g * images : (g + 1) * images]
            picked.append(
                jnp.sum(jnp.where(image_id == own_image[g], block, 0.0), axis=0, keepdims=True)
            )
        scale = 1.0 + per_row([item[:, :channels] for item in picked])
        shift = per_row([item[:, channels:] for item in picked])
        near_wait(nb2, 1)
        mean2, inv2 = gather_moments(nb2)
        cf[4] = mean2
        cf[5] = inv2
        cf[6] = inv2 * gain2 * scale
        cf[7] = shift2 * scale + shift

        def modulated(g, values):
            return (values - coef(4, g)) * coef(6, g) + coef(7, g)

        def act_two(g, r):
            values = modulated(g, h_v[g, inner(r), :])
            a2_v[g, span(r), :] = keep(g, r, silu(values)).astype(BF16)

        def act_two_edges(g):
            act_two(g, 0)
            act_two(g, rows - 1)

        def act_two_inside(g):
            plain = jnp.zeros((8, channels), F32)
            cross = jnp.zeros((8, channels), F32)
            for r in range(1, rows - 1):
                gap = h_v[g, inner(r), :] - coef(4, g)
                values = gap * coef(6, g) + coef(7, g)
                gate = 0.5 + 0.5 * jnp.tanh(0.5 * values)
                a2_v[g, span(r), :] = keep(g, r, values * gate).astype(BF16)
                slope = gate * (1.0 + values * (1.0 - gate))
                grad = keep(g, r, gm_v[g, inner(r), :].astype(F32) * slope)
                gm_v[g, inner(r), :] = grad.astype(plan.held)
                plain = plain + fold(grad)
                cross = cross + fold(grad * gap)
            st[0, g] = plain
            st[1, g] = cross

        each_batch(act_two_edges)

        each_batch(act_two_inside)

        def grad_edges(g, blocks):
            keep_halo(g2_v, 1, g)
            plain = jnp.zeros((8, channels), F32)
            cross = jnp.zeros((8, channels), F32)
            for r, line in conv(g2_v, kb2, g, blocks, True):
                gap = h_v[g, inner(r), :] - coef(4, g)
                slope = silu_slope(gap * coef(6, g) + coef(7, g))
                grad = keep(g, r, line * slope)
                gm_v[g, inner(r), :] = grad.astype(plan.held)
                plain = plain + fold(grad)
                cross = cross + fold(grad * gap)
            st[0, g] = st[0, g] + plain
            st[1, g] = (st[1, g] + cross) * coef(5, g)

        each_edge(grad_edges)
        offset_row = jnp.zeros((1, channels), F32)
        for g in range(batches):
            offset_row = offset_row + jnp.sum(st[4, g], axis=0, keepdims=True)
        tile = pack_tile(stat_tile(0), stat_tile(1))
        msg[1] = jnp.where(row_id == 2 * batches, offset_row, tile)
        tell_all(msg.at[1], ex3, 2)
        halo(a2_v, 2, None, 0, 1)

        weight_grad_two(plan.grad_rows)
        scatter_core(1)

        near_all(ex3, 2)
        plain, cross = gather_sums(ex3)
        factor = gain2 * scale
        counts = per_row(image_count, 1.0)
        cf[8] = factor * inv2
        cf[9] = group_sum(factor * plain) / counts * inv2
        cf[10] = group_sum(factor * cross) / counts * inv2 * inv2

        def grad_one(g, r):
            gap = h_v[g, inner(r), :] - coef(4, g)
            values = gm_v[g, inner(r), :].astype(F32) * coef(8, g) - coef(9, g) - gap * coef(10, g)
            low = keep(g, r, values).astype(BF16)
            g1_v[g, span(r), :] = low
            return fold(low.astype(F32))

        def grad_one_edges(g):
            st[4, g] = grad_one(g, 0) + grad_one(g, rows - 1)

        def grad_one_inside(g):
            part = st[4, g]
            for r in range(1, rows - 1):
                part = part + grad_one(g, r)
            st[4, g] = part

        each_batch(grad_one_edges)
        halo(g1_v, 3)
        halo(a2_v, 2, None, 1, batches - 1)
        each_batch(grad_one_inside)

        scatter_y(1)
        weight_grad_one(plan.grad_rows)
        scatter_z(1)
        scatter_core(0)
        turn(kf1)

        def back_one(each, pump=None):
            def body(g, blocks):
                plain = jnp.zeros((8, channels), F32)
                cross = jnp.zeros((8, channels), F32)
                for r, line in conv(g1_v, kf1, g, blocks, True):
                    gap = x_v[g, span(r), :].astype(F32) - coef(0, g)
                    grad = keep(g, r, line * silu_slope(gap * coef(2, g) + coef(3, g)))
                    a1_v[g, span(r), :] = grad.astype(BF16)
                    plain = plain + fold(grad)
                    cross = cross + fold(grad * gap)
                cross = cross * coef(1, g)
                st[0, g] = st[0, g] + plain
                st[1, g] = st[1, g] + cross

            each(body, pump=pump)

        st[0] = jnp.zeros((batches, 8, channels), F32)
        st[1] = jnp.zeros((batches, 8, channels), F32)

        def pump_two(g):
            pl.when(g == 1)(lambda: scatter_y(0))

        def keep_back(blocks, sem):
            for i, (r, count) in enumerate(blocks):
                pltpu.make_async_copy(
                    a1_v.at[:, span(r, count)], d1_hbm.at[:, pl.ds(r * cols, count * cols)],
                    back_sem.at[sem + i],
                ).start()

        def keep_wait(blocks, sem):
            for i, (r, count) in enumerate(blocks):
                wait_bytes(a1_v.at[:, span(r, count)], back_sem.at[sem + i])

        back_one(each_part, pump_two)
        keep_back(INSIDE, 2)
        def pump_three(g):
            keep_halo(g1_v, 3, g)
            pl.when(g == 1)(lambda: scatter_z(0))

        back_one(each_edge, pump_three)
        keep_back(EDGES, 0)
        offset_row = jnp.zeros((1, channels), F32)
        for g in range(batches):
            offset_row = offset_row + jnp.sum(st[4, g], axis=0, keepdims=True)
        tile = pack_tile(stat_tile(0), stat_tile(1))
        msg[3] = jnp.where(row_id == 2 * batches, offset_row, tile)
        tell_all(msg.at[3], ex4, 3)
        halo(a2_v, 2, None, batches - 1)

        def output_rows(each, blocks, buf, sem, pump=None):
            def body(g, blocks):
                for r, line in conv(a2_v, kf2, g, blocks, False):
                    line = line + coef(14, g) + x_v[g, span(r), :].astype(F32)
                    buf[g, span(r), :] = keep(g, r, line).astype(BF16)

            each(body, pump=pump)
            for i, (r, count) in enumerate(blocks):
                pltpu.make_async_copy(
                    buf.at[:, span(r, count)], out_hbm.at[:, pl.ds(r * cols, count * cols)],
                    out_sem.at[sem + i],
                ).start()

        def output_wait(blocks, buf, sem):
            for i, (r, count) in enumerate(blocks):
                wait_bytes(buf.at[:, span(r, count)], out_sem.at[sem + i])

        def pump_four(g):
            pl.when(g == 1)(lambda: scatter_x(1))

        output_rows(each_part, INSIDE, g1_v, 2, pump_four)
        halo_sent(g1_v, 3)

        def pump_five(g):
            keep_halo(a2_v, 2, g)
            pl.when(g == 1)(lambda: scatter_x(0))

        output_rows(each_edge, EDGES, g1_v, 0, pump_five)

        near_all(ex4, 3)
        plain, cross = gather_sums(ex4)
        cf[11] = group_sum(gain1 * plain) / counts * inv1
        cf[12] = group_sum(gain1 * cross) / counts * inv1 * inv1

        cf_o[0] = cf[0]
        cf_o[1] = cf[2]
        cf_o[2] = cf[11]
        cf_o[3] = cf[12]
        for g in range(batches):
            for r in range(rows):
                wr_o[g, r] = wr_s[g, r + 1]
        scatter_end(1, wg2_o)

        far_all(ex3, 2)
        second_bias = jnp.zeros((1, channels), F32)
        gain_total = jnp.zeros((1, channels), F32)
        shift_total = jnp.zeros((1, channels), F32)
        time_rows = []
        slot_id = lax.broadcasted_iota(jnp.int32, (images, n), 0)
        for g in range(batches):
            hot = jnp.where(slot_v[g : g + 1, :] == slot_id, 1.0, 0.0).astype(F32)
            plain = jnp.dot(hot, ex3[:, g, :], precision=HIGHEST, preferred_element_type=F32)
            cross = jnp.dot(hot, ex3[:, batches + g, :], precision=HIGHEST, preferred_element_type=F32)
            factor = 1.0 + tout[g * images : (g + 1) * images, :channels]
            gain_total = gain_total + jnp.sum(factor * cross, axis=0, keepdims=True)
            shift_total = shift_total + jnp.sum(factor * plain, axis=0, keepdims=True)
            time_rows.append(jnp.concatenate([cross * gain2 + plain * shift2, plain], axis=1))
        second_bias = jnp.sum(ex3[:, 2 * batches, :], axis=0, keepdims=True)
        grad_time = jnp.concatenate(time_rows, axis=0)
        time_total = jnp.sum(grad_time, axis=0, keepdims=True)
        tkg_o[...] = lax.dot_general(
            osel[...], grad_time, (((0,), (0,)), ((), ())), precision=HIGHEST,
            preferred_element_type=F32,
        )[:embed_rows]

        far_all(ex4, 3)
        plain = jnp.zeros((1, channels), F32)
        cross = jnp.zeros((1, channels), F32)
        for g in range(batches):
            plain = plain + jnp.sum(ex4[:, g, :], axis=0, keepdims=True)
            cross = cross + jnp.sum(ex4[:, batches + g, :], axis=0, keepdims=True)
        first_bias = jnp.sum(ex4[:, 2 * batches, :], axis=0, keepdims=True)
        vec_c = lax.broadcasted_iota(jnp.int32, (channels, 128), 0)
        vec_j = lax.broadcasted_iota(jnp.int32, (channels, 128), 1)
        whole = jnp.concatenate(
            [cross, plain, first_bias, gain_total, shift_total, second_bias]
            + [jnp.zeros((2, channels), F32)], axis=0,
        )
        pick = jnp.where(vec_c == vec_j + me * param_width, 1.0, 0.0).astype(F32)
        vec_o[:8] = jnp.dot(whole, pick, precision=HIGHEST, preferred_element_type=F32)
        time_c = lax.broadcasted_iota(jnp.int32, (2 * channels, 128), 0)
        time_j = lax.broadcasted_iota(jnp.int32, (2 * channels, 128), 1)
        pick = jnp.where(time_c == time_j + me * time_width, 1.0, 0.0).astype(F32)
        vec_o[8:] = jnp.dot(
            jnp.broadcast_to(time_total, (8, 2 * channels)), pick, precision=HIGHEST,
            preferred_element_type=F32,
        )
        scatter_end(0, wg1_o)

        keep_wait(INSIDE, 2)
        keep_wait(EDGES, 0)
        output_wait(INSIDE, g1_v, 2)
        output_wait(EDGES, g1_v, 0)
        for k in range(2):
            scatter_sent(k)
        reduce_sent()
        near_sent(nb1, 0)
        near_sent(nb2, 1)
        sent_all(ex3, 2)
        sent_all(ex4, 3)
        sent_all(pbuf, 4)
        for which, field in enumerate((x_v, g2_v, a2_v)):
            halo_sent(field, which)

    margin = (batches, (rows + 2) * cols, channels)
    whole = (batches, rows * cols, channels)
    dma = pltpu.SemaphoreType.DMA
    hops = nx * nz * max(ny - 1, 1)
    few = max(nx * ny, nz)
    scratch = [
        pltpu.VMEM(margin, BF16),
        pltpu.VMEM(margin, BF16),
        pltpu.VMEM(margin, BF16),
        pltpu.VMEM(margin, BF16),
        pltpu.VMEM(margin, BF16),
        pltpu.VMEM(whole, F32),
        pltpu.VMEM(whole, plan.held),
        pltpu.VMEM((3 * channels, 3 * channels), BF16),
        pltpu.VMEM((3 * channels, 3 * channels), BF16),
        pltpu.VMEM((3 * channels, 3 * channels), BF16),
        pltpu.VMEM((2, gx_size, nz, nx, padded, channels), BF16),
        pltpu.VMEM((taps + 16, channels), F32),
        pltpu.VMEM((2, ny, nz, nx, padded, channels), BF16),
        pltpu.VMEM((2, max(ny - 1, 1), nz, nx, padded, channels), BF16),
        pltpu.VMEM((2, max(nz - 1, 1), nx, padded, channels), BF16),
        pltpu.VMEM((2, max(nx - 1, 1), padded, channels), BF16),
        pltpu.VMEM((2 * reach + 1, 8, channels), F32),
        pltpu.VMEM((2 * reach + 1, 8, channels), F32),
        pltpu.VMEM((n, 8, channels), F32),
        pltpu.VMEM((n, 8, channels), F32),
        pltpu.VMEM((n, 1, 128), F32),
        pltpu.VMEM((ny * nx, batches * images, 2 * channels), F32),
        pltpu.VMEM((nz, batches * images, 2 * channels), F32),
        pltpu.VMEM((2, batches * images, 2 * channels), F32),
        pltpu.VMEM((batches * images, 2 * channels), F32),
        pltpu.VMEM((batches * images, 128), F32),
        pltpu.VMEM((4, 8, channels), F32),
        pltpu.VMEM((16, 8, channels), F32),
        pltpu.VMEM((5, batches, 8, channels), F32),
        pltpu.SMEM((batches, 16), jnp.int32),
        dma((2,)),
        dma((4, 2, batches)),
        dma((4, 2, batches)),
        dma((2, 4, hops)),
        dma((2, 4, hops)),
        dma((2, 4, few)),
        dma((2, 4, few)),
        dma((3, few)),
        dma((3, few)),
        dma((5,)),
        dma((5,)),
        dma((5,)),
        dma((3,)),
        dma((3,)),
    ]
    hbm = pl.BlockSpec(memory_space=pl.ANY)
    vmem = pl.BlockSpec(memory_space=pltpu.VMEM)
    smem = pl.BlockSpec(memory_space=pltpu.SMEM)
    return pl.pallas_call(
        kernel,
        name="block",
        out_shape=(
            jax.ShapeDtypeStruct(whole, BF16),
            jax.ShapeDtypeStruct(whole, BF16),
            jax.ShapeDtypeStruct((shard, channels), F32),
            jax.ShapeDtypeStruct((shard, channels), F32),
            jax.ShapeDtypeStruct((embed_rows, 2 * channels), F32),
            jax.ShapeDtypeStruct((16, 128), F32),
            jax.ShapeDtypeStruct((4, 8, channels), F32),
            jax.ShapeDtypeStruct((batches, rows), jnp.int32),
        ),
        in_specs=[hbm, hbm, vmem, vmem, vmem, vmem, vmem, vmem, smem, smem],
        out_specs=(hbm, hbm, vmem, vmem, vmem, vmem, vmem, smem),
        scratch_shapes=scratch,
        compiler_params=pltpu.CompilerParams(
            collective_id=0, has_side_effects=True, vmem_limit_bytes=VMEM_LIMIT,
        ),
        cost_estimate=pl.CostEstimate(
            flops=12 * rows * cols * batches * taps * channels,
            bytes_accessed=8 * rows * cols * batches * channels,
            transcendentals=8 * rows * cols * batches * channels,
        ),
    )


VMEM_LIMIT = 63 * 2**20


def build_tail(plan, vectors):
    batches, rows, cols, channels = plan.batches, plan.rows, plan.cols, plan.channels
    step_rows = rows if plan.parts == 1 else 2

    def kernel(
        wr_s, cf, x, og, d1, done, wg1, wg2, tkg, vec, out, gi, wg1_o, wg2_o, tkg_o, *small
    ):
        g, c = pl.program_id(0), pl.program_id(1)
        col_id = lax.broadcasted_iota(jnp.int32, (cols, channels), 0)

        def coef(which):
            return cf[which, pl.ds(g, 1), :]

        for q in range(step_rows):
            place = slice(q * cols, (q + 1) * cols)
            gap = x[0, place].astype(F32) - coef(0)
            values = d1[0, place].astype(F32) * coef(1) - coef(2) - gap * coef(3) + og[0, place].astype(F32)
            width = wr_s[g, c * step_rows + q]
            gi[0, place] = jnp.where(col_id < width, values, 0.0).astype(BF16)
        out[...] = done[...]

        @pl.when((g == 0) & (c == 0))
        def _():
            wg1_o[...] = wg1[...]
            wg2_o[...] = wg2[...]
            tkg_o[...] = tkg[...]
            for ref, (row, size) in zip(small, vectors):
                ref[...] = vec[row, :size]

    block = pl.BlockSpec((1, step_rows * cols, channels), lambda g, c: (g, c, 0))

    def fixed(*shape):
        return pl.BlockSpec(shape, lambda g, c: (0,) * len(shape))

    kernel_grad = fixed(plan.shard, channels)
    time_grad = fixed(plan.embed_rows, 2 * channels)
    whole = (batches, rows * cols, channels)
    return pl.pallas_call(
        kernel,
        name="tail",
        grid=(batches, rows // step_rows),
        in_specs=[
            pl.BlockSpec(memory_space=pltpu.SMEM), fixed(4, 8, channels),
            block, block, block, block,
            kernel_grad, kernel_grad, time_grad, fixed(16, 128),
        ],
        out_specs=[block, block, kernel_grad, kernel_grad, time_grad]
        + [fixed(size) for _, size in vectors],
        out_shape=[
            jax.ShapeDtypeStruct(whole, BF16),
            jax.ShapeDtypeStruct(whole, BF16),
            jax.ShapeDtypeStruct((plan.shard, channels), F32),
            jax.ShapeDtypeStruct((plan.shard, channels), F32),
            jax.ShapeDtypeStruct((plan.embed_rows, 2 * channels), F32),
        ]
        + [jax.ShapeDtypeStruct((size,), F32) for _, size in vectors],
        compiler_params=pltpu.CompilerParams(
            vmem_limit_bytes=VMEM_LIMIT, dimension_semantics=("arbitrary", "arbitrary")
        ),
    )


def make_body(mesh_shape):
    def body(
        input_cells, time_embed, first_gain, first_shift, first_kernel, first_offset,
        time_kernel, time_offset, second_gain, second_shift, second_kernel, second_offset,
        output_grad, slot_image, image_height,
    ):
        cells = input_cells.shape
        plan = Plan(
            mesh_shape, cells, time_embed.shape, slot_image.shape,
            first_kernel.shape[0], time_kernel.shape[0],
        )
        flat = (cells[0], cells[1] * cells[2], cells[3])
        params = jnp.concatenate(
            [first_gain, first_shift, first_offset, second_gain, second_shift, second_offset,
             time_offset]
        ).astype(F32)
        params = jnp.pad(params[None, :], ((0, 0), (0, 128 - params.shape[0])))
        cells_in, cells_grad = input_cells.reshape(flat), output_grad.reshape(flat)
        done, part, wg1, wg2, tkg, vec, cf, widths = build_kernel(plan)(
            cells_in, cells_grad, first_kernel, second_kernel,
            params, time_embed, time_kernel, slot_image, slot_image, image_height,
        )
        width = first_gain.shape[0]
        vectors = [(i, width) for i in range(6)] + [(8, time_offset.shape[0])]
        out, grad, wg1, wg2, tkg, *rows = build_tail(plan, vectors)(
            widths, cf, cells_in, cells_grad, part, done, wg1, wg2, tkg, vec
        )
        return (
            out.reshape(cells), grad.reshape(cells), rows[0], rows[1], wg1, rows[2],
            tkg, rows[6], rows[3], rows[4], wg2, rows[5],
        )

    return body


def solution(mesh):
    both = ("gx", "gy")
    cells, vector, matrix, whole = P(None, both, None, None), P(both), P(both, None), P()
    return jax.shard_map(
        make_body(dict(mesh.shape)),
        mesh=mesh,
        in_specs=(
            cells, whole, vector, vector, matrix, vector, matrix, vector, vector, vector, matrix,
            vector, cells, whole, whole,
        ),
        out_specs=(
            cells, cells, vector, vector, matrix, vector, matrix, vector, vector, vector, matrix,
            vector,
        ),
        check_vma=False,
    )
```

```python
import jax
import jax.numpy as jnp
from jax import lax
from jax.experimental import pallas as pl
from jax.experimental.pallas import tpu as pltpu
from jax.sharding import PartitionSpec as P

NORM_GROUPS = 32
EPS = 1e-05
HIGHEST = lax.Precision.HIGHEST
MESH = pl.DeviceIdType.MESH
F32 = jnp.float32
BF16 = jnp.bfloat16


def silu(values):
    return values * (0.5 + 0.5 * jnp.tanh(0.5 * values))


def silu_slope(values):
    gate = 0.5 + 0.5 * jnp.tanh(0.5 * values)
    return gate * (1.0 + values * (1.0 - gate))


def fold(values):
    rows, channels = values.shape
    return jnp.sum(values.reshape(rows // 8, 8, channels), axis=0)


class Plan:
    def __init__(self, mesh_shape, cells, time_embed, slot_image, kernel_rows, embed_rows):
        self.gx, self.gy = mesh_shape["gx"], mesh_shape["gy"]
        self.n = self.gx * self.gy
        self.ny = self.gx // 2
        self.nx = self.ny if self.gy % self.ny == 0 else 1
        self.nz = self.gy // self.nx
        self.batches, self.rows, self.cols, self.channels = cells
        self.images, self.embed = time_embed[1], time_embed[2]
        self.reach = slot_image[1] * 5 // 32 - 1
        self.shard = kernel_rows
        self.padded = (kernel_rows + 15) // 16 * 16
        self.embed_rows = embed_rows
        tight = self.n > 64
        self.parts, self.grad_rows, self.held = (2, 2, BF16) if tight else (1, 8, F32)


def build_kernel(plan):
    n, gx_size, gy_size = plan.n, plan.gx, plan.gy
    nx, ny, nz = plan.nx, plan.ny, plan.nz
    batches, rows, cols, channels = plan.batches, plan.rows, plan.cols, plan.channels
    images, reach = plan.images, plan.reach
    shard, padded, embed_rows = plan.shard, plan.padded, plan.embed_rows
    group = channels // NORM_GROUPS
    group_shift = group.bit_length() - 1
    narrow = cols * 3 // 5
    taps = 9 * channels
    param_width = channels // n
    time_width = 2 * channels // n

    def kernel(
        x_hbm, og_hbm, k1_in, k2_in, par_in, emb_in, tk_in, slot_v, slot_s, high_s,
        out_hbm, d1_hbm, wg1_o, wg2_o, tkg_o, vec_o, cf_o, wr_o,
        x_v, g2_v, a1_v, a2_v, g1_v, h_v, gm_v, kf1, kf2, kb2, agk, acc,
        rs1, rs2, rs3, rs4, nb1, nb2, ex3, ex4, pbuf, ta1, ta2, ta3, tout,
        osel, msg, cf, st, wr_s,
        ld_sem, halo_s, halo_r, ag_s, ag_r, rs_s, rs_r, ar_s, ar_r, ex_s, near_r, far_r, out_sem, back_sem,
    ):
        my_x = lax.axis_index("gx")
        my_y = lax.axis_index("gy")
        me = my_x * gy_size + my_y
        core = lax.rem(my_x, 2)
        yy = lax.div(my_x, 2)
        zz = lax.div(my_y, nx)
        xx = lax.rem(my_y, nx)
        sib = 1 - core

        def dev(index):
            return (lax.div(index, gy_size), lax.rem(index, gy_size))

        def wait_bytes(ref, sem):
            pltpu.make_async_copy(ref, ref, sem).wait()

        def send(src, dst, send_sem, recv_sem, device):
            pltpu.make_async_remote_copy(
                src_ref=src, dst_ref=dst, send_sem=send_sem, recv_sem=recv_sem,
                device_id=device, device_id_type=MESH,
            ).start()

        load_x = pltpu.make_async_copy(x_hbm, x_v.at[:, pl.ds(cols, rows * cols)], ld_sem.at[0])
        load_g = pltpu.make_async_copy(og_hbm, g2_v.at[:, pl.ds(cols, rows * cols)], ld_sem.at[1])
        load_x.start()
        load_g.start()
        barrier = pltpu.get_barrier_semaphore()

        def greet(step, carry):
            pl.semaphore_signal(
                barrier, inc=1, device_id=dev(lax.rem(me + step, n)), device_id_type=MESH
            )
            return carry

        lax.fori_loop(1, n, greet, 0)

        for which, ref in enumerate((k1_in, k2_in)):
            own = ref[...].astype(F32)
            if padded > shard:
                own = jnp.concatenate([own, jnp.zeros((padded - shard, channels), F32)], axis=0)
            agk[which, my_x, zz, xx] = own.astype(BF16)

        same = []
        near_count = []
        own_count = []
        image_count = []
        own_image = []
        for g in range(batches):
            image = slot_s[g, me]
            before = jnp.int32(0)
            links = []
            for e in range(-reach, reach + 1):
                place = me + e
                inside = jnp.where((place >= 0) & (place < n), 1, 0)
                other = slot_s[g, jnp.clip(place, 0, n - 1)]
                link = inside * jnp.where(other == image, 1, 0)
                links.append(link)
                if e < 0:
                    before = before + link
            height = high_s[g, image]
            width = jnp.where(image < images // 2, cols, narrow)
            for r in range(-1, rows + 1):
                row_ok = jnp.where(before * rows + r < height, 1, 0)
                if r == -1:
                    row_ok = row_ok * links[reach - 1]
                if r == rows:
                    row_ok = row_ok * links[reach + 1]
                wr_s[g, r + 1] = row_ok * width
            counts = []
            for e in range(-reach, reach + 1):
                held = jnp.clip(height - (before + e) * rows, 0, rows) * links[e + reach]
                counts.append((held * width * group).astype(F32))
            same.append([link.astype(F32) for link in links])
            near_count.append(counts)
            own_count.append(counts[reach])
            image_count.append((height * width * group).astype(F32))
            own_image.append(image)

        row_id = lax.broadcasted_iota(jnp.int32, (8, channels), 0)
        col_id = lax.broadcasted_iota(jnp.int32, (cols, channels), 0)
        grp_r = lax.broadcasted_iota(jnp.int32, (channels, channels), 0)
        grp_c = lax.broadcasted_iota(jnp.int32, (channels, channels), 1)

        def per_row(values, rest=0.0):
            total = jnp.full((8, channels), rest, F32)
            for i, value in enumerate(values):
                total = jnp.where(row_id == i, value, total)
            return total

        def group_sum(tile):
            block = jnp.where(
                lax.shift_right_logical(grp_r, group_shift)
                == lax.shift_right_logical(grp_c, group_shift),
                1.0, 0.0,
            ).astype(F32)
            return jnp.dot(tile, block, precision=HIGHEST, preferred_element_type=F32)

        def keep(g, r, values):
            return jnp.where(col_id < wr_s[g, r + 1], values, 0.0)

        def span(r, count=1):
            start = (r + 1) * cols
            if not isinstance(start, int):
                start = pl.multiple_of(start, cols)
            return pl.ds(start, count * cols)

        def inner(r):
            start = r * cols
            if not isinstance(start, int):
                start = pl.multiple_of(start, cols)
            return pl.ds(start, cols)

        def coef(which, g):
            return cf[which, pl.ds(g, 1), :]

        def stat_tile(which):
            return per_row([jnp.sum(st[which, g], axis=0, keepdims=True) for g in range(batches)])

        def x_peers():
            for dx in range(1, nx):
                px = lax.rem(xx + dx, nx)
                yield dx - 1, px, (my_x, zz * nx + px)

        def y_peers():
            for dy in range(1, ny):
                py = lax.rem(yy + dy, ny) * 2 + core
                yield dy - 1, py, (py, my_y)

        def z_peers():
            for dz in range(1, nz):
                pz = lax.rem(zz + dz, nz)
                yield dz - 1, pz, (my_x, pz * nx + xx)

        def plane_peers():
            for step in range(1, ny * nx):
                py = lax.rem(yy + step // nx, ny)
                px = lax.rem(xx + step % nx, nx)
                yield step - 1, (py * 2 + core, zz * nx + px)

        sibling = (yy * 2 + sib, my_y)

        def gather_send(k, hop, step, part, peer):
            send(part, part, ag_s.at[k, hop, step], ag_r.at[k, hop, step], peer)

        def gather_wait(k, hop, parts, ref):
            for step in range(parts):
                wait_bytes(ref, ag_r.at[k, hop, step])

        def gather_sent(k):
            for hop, parts, ref in gather_plan(k):
                for step in range(parts):
                    wait_bytes(ref, ag_s.at[k, hop, step])

        def gather_plan(k):
            one, row, plane = agk.at[k, 0, 0, 0], agk.at[k, 0, 0], agk.at[k, 0]
            if k == 0:
                return (
                    (0, nz - 1, one), (1, nz * (nx - 1), one), (2, nx * nz * (ny - 1), one),
                    (3, ny, plane),
                )
            return (0, nx - 1, one), (1, nz - 1, row), (2, nz * (ny - 1), row), (3, ny, plane)

        def came(dz, dx):
            return agk.at[0, my_x, lax.rem(zz - dz + nz, nz), lax.rem(xx - dx + nx, nx)]

        def pass_x(dz):
            for step, px, peer in x_peers():
                gather_send(0, 1, dz * (nx - 1) + step, came(dz, 0), peer)

        def pass_y(dz, dx):
            for step, py, peer in y_peers():
                gather_send(0, 2, (dz * nx + dx) * (ny - 1) + step, came(dz, dx), peer)

        def spread_start():
            for step, pz, peer in z_peers():
                gather_send(0, 0, step, came(0, 0), peer)
            pass_x(0)
            pass_y(0, 0)

        def spread_line():
            for dz in range(1, nz):
                wait_bytes(agk.at[0, 0, 0, 0], ag_r.at[0, 0, dz - 1])
                pass_x(dz)
                pass_y(dz, 0)

        def spread_plane():
            for dz in range(nz):
                for dx in range(1, nx):
                    wait_bytes(agk.at[0, 0, 0, 0], ag_r.at[0, 1, dz * (nx - 1) + dx - 1])
                    pass_y(dz, dx)

        def gather_x(k):
            for step, px, peer in x_peers():
                gather_send(k, 0, step, agk.at[k, my_x, zz, xx], peer)

        def forward_y(k, dz):
            row = agk.at[k, my_x, lax.rem(zz - dz + nz, nz)]
            for step, py, peer in y_peers():
                gather_send(k, 2, dz * (ny - 1) + step, row, peer)

        def gather_z(k):
            gather_wait(k, 0, nx - 1, agk.at[k, 0, 0, 0])
            for step, pz, peer in z_peers():
                gather_send(k, 1, step, agk.at[k, my_x, zz], peer)
            forward_y(k, 0)

        def gather_y(k, first=1, last=nz):
            for dz in range(first, last):
                wait_bytes(agk.at[k, 0, 0], ag_r.at[k, 1, dz - 1])
                forward_y(k, dz)

        def gather_core(k):
            hop, parts, ref = gather_plan(k)[2]
            gather_wait(k, hop, parts, ref)
            for y in range(ny):
                gather_send(k, 3, y, agk.at[k, y * 2 + core], sibling)

        def gather_end(k):
            gather_wait(k, 3, ny, agk.at[k, 0])

        def grid_place(i):
            left = lax.rem(i, gy_size)
            return lax.div(i, gy_size), lax.div(left, nx), lax.rem(left, nx)

        def shards(body):
            if shard % 8 == 0:
                def step(i, carry):
                    body(i, pl.ds(pl.multiple_of(i * shard, 8), padded))
                    return carry

                lax.fori_loop(0, n, step, 0)
            else:
                for i in range(n):
                    body(i, pl.ds(i * shard, padded))

        def assemble(k):
            def one(i, place):
                acc[place, :] = agk[(k, *grid_place(i))].astype(F32)

            shards(one)

        def tap_block(a, b):
            return pl.ds((3 * a + b) * channels, channels)

        def fill_forward(ref):
            for a in range(3):
                for b in range(3):
                    ref[a * channels : (a + 1) * channels, b * channels : (b + 1) * channels] = acc[
                        tap_block(a, b), :
                    ].astype(BF16)

        def fill_backward(ref):
            for a in range(3):
                for b in range(3):
                    ref[a * channels : (a + 1) * channels, b * channels : (b + 1) * channels] = (
                        acc[tap_block(a, b), :].T.astype(BF16)
                    )

        def turn(ref):
            for a in range(3):
                for b in range(3):
                    place = (
                        slice(a * channels, (a + 1) * channels),
                        slice(b * channels, (b + 1) * channels),
                    )
                    ref[place] = ref[place].astype(F32).T.astype(BF16)

        def scatter_core(k):
            gather_sent(k)

            def one(i, place):
                agk[(k, *grid_place(i))] = acc[place, :].astype(BF16)

            shards(one)
            for y in range(ny):
                send(
                    agk.at[k, y * 2 + sib], rs1.at[k, y],
                    rs_s.at[k, 0, y], rs_r.at[k, 0, y], sibling,
                )

        def add_up(k, place, parts):
            total = agk[(k, *place)].astype(F32)
            for part in parts:
                total = total + part.astype(F32)
            return total

        def scatter_y(k):
            for y in range(ny):
                wait_bytes(rs1.at[k, y], rs_r.at[k, 0, y])

            def one(i, carry):
                y, j = lax.div(i, gy_size), lax.rem(i, gy_size)
                z, x = lax.div(j, nx), lax.rem(j, nx)
                place = (y * 2 + core, z, x)
                agk[(k, *place)] = add_up(k, place, [rs1[k, y, z, x]]).astype(BF16)
                return carry

            lax.fori_loop(0, ny * gy_size, one, 0)
            for step, py, peer in y_peers():
                send(
                    agk.at[k, py], rs2.at[k, step], rs_s.at[k, 1, step], rs_r.at[k, 1, step], peer
                )

        def scatter_z(k):
            for step in range(ny - 1):
                wait_bytes(rs2.at[k, step], rs_r.at[k, 1, step])

            def one(j, carry):
                z, x = lax.div(j, nx), lax.rem(j, nx)
                place = (my_x, z, x)
                parts = [rs2[k, step, z, x] for step in range(ny - 1)]
                agk[(k, *place)] = add_up(k, place, parts).astype(BF16)
                return carry

            lax.fori_loop(0, gy_size, one, 0)
            for step, pz, peer in z_peers():
                send(
                    agk.at[k, my_x, pz], rs3.at[k, step],
                    rs_s.at[k, 2, step], rs_r.at[k, 2, step], peer,
                )

        def scatter_x(k):
            for step in range(nz - 1):
                wait_bytes(rs3.at[k, step], rs_r.at[k, 2, step])
            for x in range(nx):
                place = (my_x, zz, x)
                parts = [rs3[k, step, x] for step in range(nz - 1)]
                agk[(k, *place)] = add_up(k, place, parts).astype(BF16)
            for step, px, peer in x_peers():
                send(
                    agk.at[k, my_x, zz, px], rs4.at[k, step],
                    rs_s.at[k, 3, step], rs_r.at[k, 3, step], peer,
                )

        def scatter_end(k, out_ref):
            for step in range(nx - 1):
                wait_bytes(rs4.at[k, step], rs_r.at[k, 3, step])
            parts = [rs4[k, step] for step in range(nx - 1)]
            out_ref[...] = add_up(k, (my_x, zz, xx), parts)[:shard]

        def scatter_sent(k):
            for hop, (buf, parts) in enumerate(((rs1, ny), (rs2, ny - 1), (rs3, nz - 1), (rs4, nx - 1))):
                for step in range(parts):
                    wait_bytes(buf.at[k, 0], rs_s.at[k, hop, step])

        def reduce_1(partial):
            ta1[0] = partial
            for step, peer in plane_peers():
                send(ta1.at[0], ta1.at[step + 1], ar_s.at[0, step], ar_r.at[0, step], peer)

        def reduce_2():
            for step in range(ny * nx - 1):
                wait_bytes(ta1.at[0], ar_r.at[0, step])
            ta2[0] = jnp.sum(ta1[...], axis=0)
            for step, _, peer in z_peers():
                send(ta2.at[0], ta2.at[step + 1], ar_s.at[1, step], ar_r.at[1, step], peer)

        def reduce_3():
            for step in range(nz - 1):
                wait_bytes(ta1.at[0], ar_r.at[1, step])
            ta3[0] = jnp.sum(ta2[...], axis=0)
            send(ta3.at[0], ta3.at[1], ar_s.at[2, 0], ar_r.at[2, 0], sibling)

        def reduce_end():
            wait_bytes(ta3.at[0], ar_r.at[2, 0])
            return ta3[0] + ta3[1]

        def reduce_sent():
            for hop, parts in enumerate((ny * nx - 1, nz - 1, 1)):
                for step in range(parts):
                    wait_bytes(ta3.at[0], ar_s.at[hop, step])

        def tell_all(src, buf, which):
            buf[me] = src[...]
            for d in range(1, reach + 1):
                for e in (d, -d):
                    peer = dev(lax.rem(me + e + n, n))
                    send(src, buf.at[me], ex_s.at[which], near_r.at[which], peer)

            def far(step, carry):
                peer = dev(lax.rem(me + step, n))
                send(src, buf.at[me], ex_s.at[which], far_r.at[which], peer)
                return carry

            lax.fori_loop(reach + 1, n - reach, far, 0)

        def near_all(buf, which):
            wait_bytes(buf.at[pl.ds(0, 2 * reach)], near_r.at[which])

        def far_all(buf, which):
            wait_bytes(buf.at[pl.ds(0, n - 1 - 2 * reach)], far_r.at[which])

        def sent_all(buf, which):
            wait_bytes(buf.at[pl.ds(0, n - 1)], ex_s.at[which])

        def tell_near(src, buf, which):
            buf[reach] = src[...]
            for d in range(1, reach + 1):
                for e in (d, -d):
                    peer = dev(lax.rem(me + e + n, n))
                    send(src, buf.at[reach - e], ex_s.at[which], near_r.at[which], peer)

        def near_wait(buf, which):
            wait_bytes(buf.at[pl.ds(0, 2 * reach)], near_r.at[which])

        def near_sent(buf, which):
            wait_bytes(buf.at[pl.ds(0, 2 * reach)], ex_s.at[which])

        def halo(field, which, source=None, first=0, last=batches):
            for g in range(first, last):
                if source is None:
                    low, high = field.at[g, span(rows - 1)], field.at[g, span(0)]
                else:
                    low, high = source.at[g, inner(rows - 1)], source.at[g, inner(0)]
                send(
                    low, field.at[g, span(-1)], halo_s.at[which, 0, g], halo_r.at[which, 0, g],
                    dev(lax.rem(me + 1, n)),
                )
                send(
                    high, field.at[g, span(rows)], halo_s.at[which, 1, g], halo_r.at[which, 1, g],
                    dev(lax.rem(me + n - 1, n)),
                )

        def halo_wait(field, which, g):
            wait_bytes(field.at[g, span(-1)], halo_r.at[which, 0, g])
            wait_bytes(field.at[g, span(rows)], halo_r.at[which, 1, g])

        def halo_sent(field, which):
            for g in range(batches):
                wait_bytes(field.at[g, span(-1)], halo_s.at[which, 0, g])
                wait_bytes(field.at[g, span(rows)], halo_s.at[which, 1, g])

        def keep_halo(field, which, g):
            halo_wait(field, which, g)
            for r in (-1, rows):
                field[g, span(r), :] = keep(g, r, field[g, span(r), :].astype(F32)).astype(BF16)

        def gather_moments(buf):
            counts = per_row(image_count, 1.0)
            total = jnp.zeros((8, channels), F32)
            for e in range(2 * reach + 1):
                weight = per_row([same[g][e] for g in range(batches)] * 2)
                total = total + weight * buf[e]
            mean = total / counts
            squares = pltpu.roll(total, 8 - batches, 0)
            for e in range(2 * reach + 1):
                held = per_row([near_count[g][e] for g in range(batches)])
                shift = buf[e] / jnp.maximum(held, 1.0) - mean
                squares = squares + held * shift * shift
            return mean, lax.rsqrt(jnp.maximum(squares, 0.0) / counts + EPS)

        def gather_sums(buf):
            total = jnp.zeros((8, channels), F32)
            for e in range(-reach, reach + 1):
                weight = per_row([same[g][e + reach] for g in range(batches)] * 2)
                total = total + weight * buf[lax.rem(me + e + n, n)]
            return total, pltpu.roll(total, 8 - batches, 0)

        def pack_tile(plain, cross):
            return jnp.where(row_id < batches, plain, pltpu.roll(cross, batches, 0))

        def local_moments(read, which):
            total = group_sum(stat_tile(which))
            cf[15] = total / jnp.maximum(per_row(own_count, 1.0), 1.0)

            def one(g, carry):
                part = jnp.zeros((8, channels), F32)
                for r in range(rows):
                    gap = keep(g, r, read(g, r) - coef(15, g))
                    part = part + fold(gap * gap)
                st[which + 1, g] = part
                return carry

            lax.fori_loop(0, batches, one, 0)
            msg[which] = pack_tile(total, group_sum(stat_tile(which + 1)))

        def conv(field, weights, g, blocks, back):
            window = []
            for a in range(3):
                shift = (2 - a if back else a) - 1
                parts = [field[g, span(r + shift, count), :] for r, count in blocks]
                window.append(parts[0] if len(parts) == 1 else jnp.concatenate(parts, axis=0))
            result = jnp.dot(
                jnp.concatenate(window, axis=1), weights[...], preferred_element_type=F32
            )
            place = 0
            for r0, count in blocks:
                for q in range(count):
                    r = r0 + q
                    line = result[place * cols : (place + 1) * cols]
                    left, right = line[:, :channels], line[:, 2 * channels :]
                    if back:
                        left, right = right, left
                    left = jnp.where(col_id == 0, 0.0, pltpu.roll(left, 1, 0))
                    right = jnp.where(col_id == cols - 1, 0.0, pltpu.roll(right, cols - 1, 0))
                    yield r, left + line[:, channels : 2 * channels] + right
                    place += 1

        INSIDE = ((1, rows - 2),)
        EDGES = ((0, 1), (rows - 1, 1))

        def each_part(body, first=0, last=batches, pump=None):
            def one(i, carry):
                g, part = lax.div(i, plan.parts), lax.rem(i, plan.parts)
                if pump is not None:
                    pl.when(part == 0)(lambda: pump(g))
                count = (rows - 2) // plan.parts
                body(g, INSIDE if plan.parts == 1 else ((1 + part * count, count),))
                return carry

            lax.fori_loop(first * plan.parts, last * plan.parts, one, 0)

        def each_edge(body, pump=None):
            def one(g, carry):
                if pump is not None:
                    pump(g)
                body(g, EDGES)
                return carry

            lax.fori_loop(0, batches, one, 0)

        def each_batch(body):
            def one(g, carry):
                body(g)
                return carry

            lax.fori_loop(0, batches, one, 0)

        def shifted(values):
            right = jnp.where(col_id == 0, 0.0, pltpu.roll(values, 1, 0))
            left = jnp.where(col_id == cols - 1, 0.0, pltpu.roll(values, cols - 1, 0))
            return right, values, left

        def weight_grad_two(step_rows):
            acc[...] = jnp.zeros_like(acc)
            steps = rows // step_rows

            def one(i, carry):
                g = lax.div(i, steps)
                r0 = lax.rem(i, steps) * step_rows
                lines = []
                for q in range(step_rows):
                    right, mid, left = shifted(a2_v[g, span(r0 + q), :].astype(F32))
                    lines.append(jnp.concatenate([right, mid, left], axis=1).astype(BF16))
                lhs = jnp.concatenate(lines, axis=0)
                rhs = jnp.concatenate(
                    [g2_v[g, span(r0 + 1 - a, step_rows), :] for a in range(3)], axis=1
                )
                part = lax.dot_general(
                    lhs, rhs, (((0,), (0,)), ((), ())), preferred_element_type=F32
                )
                for a in range(3):
                    for b in range(3):
                        acc[tap_block(a, b), :] += part[
                            b * channels : (b + 1) * channels, a * channels : (a + 1) * channels
                        ]
                return carry

            lax.fori_loop(0, batches * steps, one, 0)

        def weight_grad_one(step_rows):
            acc[...] = jnp.zeros_like(acc)
            steps = rows // step_rows

            def one(i, carry):
                g = lax.div(i, steps)
                r0 = lax.rem(i, steps) * step_rows
                lines = []
                for q in range(step_rows):
                    right, mid, left = shifted(g1_v[g, span(r0 + q), :].astype(F32))
                    lines.append(jnp.concatenate([left, mid, right], axis=1).astype(BF16))
                rhs = jnp.concatenate(lines, axis=0)
                lhs = jnp.concatenate(
                    [a1_v[g, span(r0 + a - 1, step_rows), :] for a in range(3)], axis=1
                )
                part = lax.dot_general(
                    lhs, rhs, (((0,), (0,)), ((), ())), preferred_element_type=F32
                )
                for a in range(3):
                    for b in range(3):
                        acc[tap_block(a, b), :] += part[
                            a * channels : (a + 1) * channels, b * channels : (b + 1) * channels
                        ]
                return carry

            lax.fori_loop(0, batches * steps, one, 0)

        embed = emb_in[...].astype(F32).reshape(batches * images, plan.embed)
        embed = silu(embed).astype(BF16)
        pick_r = lax.broadcasted_iota(jnp.int32, (plan.embed, 128), 0)
        pick_c = lax.broadcasted_iota(jnp.int32, (plan.embed, 128), 1)
        pick = jnp.where((pick_r == pick_c + me * embed_rows) & (pick_c < embed_rows), 1.0, 0.0)
        osel[...] = jnp.dot(embed, pick.astype(BF16), preferred_element_type=F32)
        own_tk = jnp.concatenate(
            [tk_in[...].astype(F32), jnp.zeros((128 - embed_rows, 2 * channels), F32)], axis=0
        ).astype(BF16)
        partial = (jnp.dot(osel[...].astype(BF16), own_tk, preferred_element_type=F32))
        pl.semaphore_wait(barrier, n - 1)
        spread_start()
        gather_x(1)
        load_x.wait()

        def sum_input(g):
            part = jnp.zeros((8, channels), F32)
            for r in range(rows):
                part = part + fold(keep(g, r, x_v[g, span(r), :].astype(F32)))
            st[0, g] = part

        each_batch(sum_input)
        spread_line()
        tell_all(par_in, pbuf, 4)
        halo(x_v, 0, x_hbm, 0, 1)
        local_moments(lambda g, r: x_v[g, span(r), :].astype(F32), 0)
        tell_near(msg.at[0], nb1, 0)
        reduce_1(partial)
        spread_plane()
        gather_z(1)
        halo(x_v, 0, x_hbm, 1)
        load_g.wait()

        def keep_grad(g):
            part = jnp.zeros((8, channels), F32)
            for r in range(rows):
                values = keep(g, r, g2_v[g, span(r), :].astype(F32))
                g2_v[g, span(r), :] = values.astype(BF16)
                part = part + fold(values)
            st[4, g] = part

        each_batch(keep_grad)
        gather_core(0)

        near_all(pbuf, 4)
        far_all(pbuf, 4)
        tiles = pbuf[:, 0, :].astype(BF16)
        lane_r = lax.broadcasted_iota(jnp.int32, (128, channels), 0)
        lane_c = lax.broadcasted_iota(jnp.int32, (128, channels), 1)
        own_r = lax.broadcasted_iota(jnp.int32, (n, channels), 0)
        own_c = lax.broadcasted_iota(jnp.int32, (n, channels), 1)

        def vector(offset, width, start):
            spread = jnp.where(lane_r == offset + (lane_c & (width - 1)), 1.0, 0.0).astype(BF16)
            values = jnp.dot(tiles, spread, preferred_element_type=F32)
            owner = lax.shift_right_logical(own_c + start, width.bit_length() - 1)
            return jnp.sum(jnp.where(own_r == owner, values, 0.0), axis=0, keepdims=True)

        gain1, shift1, offset1, gain2, shift2, offset2 = (
            vector(i * param_width, param_width, 0) for i in range(6)
        )
        time_low = vector(6 * param_width, time_width, 0)
        time_high = vector(6 * param_width, time_width, channels)
        time_bias = jnp.concatenate([time_low, time_high], axis=1)

        near_wait(nb1, 0)
        mean1, inv1 = gather_moments(nb1)
        cf[0] = mean1
        cf[1] = inv1
        cf[2] = inv1 * gain1
        cf[3] = jnp.broadcast_to(shift1, (8, channels))
        cf[13] = jnp.broadcast_to(offset1, (8, channels))
        cf[14] = jnp.broadcast_to(offset2, (8, channels))

        def pre_one(g, values):
            return (values - coef(0, g)) * coef(2, g) + coef(3, g)

        def act_one(g, r):
            values = pre_one(g, x_v[g, span(r), :].astype(F32))
            a1_v[g, span(r), :] = keep(g, r, silu(values)).astype(BF16)

        def act_rows(g):
            for r in range(rows):
                act_one(g, r)

        each_batch(act_rows)
        gather_end(0)
        assemble(0)
        fill_forward(kf1)

        def hidden_rows(each, pump=None):
            def body(g, blocks):
                part = jnp.zeros((8, channels), F32)
                for r, line in conv(a1_v, kf1, g, blocks, False):
                    line = line + coef(13, g)
                    h_v[g, inner(r), :] = line
                    part = part + fold(keep(g, r, line))
                st[2, g] = st[2, g] + part

            each(body, pump=pump)

        st[2] = jnp.zeros((batches, 8, channels), F32)

        def pump_one(g):
            @pl.when(g == 1)
            def _():
                gather_y(1)
                reduce_2()
                halo(g2_v, 1, og_hbm, 0, 1)

            pl.when(g == batches - 1)(lambda: gather_core(1))

        hidden_rows(each_part, pump_one)

        gather_end(1)
        assemble(1)
        fill_forward(kf2)
        fill_backward(kb2)

        def back_two(each, *span_of):
            def body(g, blocks):
                for r, line in conv(g2_v, kb2, g, blocks, True):
                    gm_v[g, inner(r), :] = line.astype(plan.held)

            each(body, *span_of)

        halo(g2_v, 1, og_hbm, 1, batches - 1)
        back_two(each_part, 0, batches - 1)

        def act_halo(g):
            halo_wait(x_v, 0, g)
            for r in (-1, rows):
                act_one(g, r)

        reduce_3()
        hidden_rows(each_edge, act_halo)
        local_moments(lambda g, r: h_v[g, inner(r), :], 2)
        tell_near(msg.at[2], nb2, 1)
        halo(g2_v, 1, og_hbm, batches - 1)
        back_two(each_part, batches - 1, batches)
        tout[...] = reduce_end() + time_bias
        picked = []
        image_id = lax.broadcasted_iota(jnp.int32, (images, 2 * channels), 0)
        for g in range(batches):
            block = tout[g * images : (g + 1) * images]
            picked.append(
                jnp.sum(jnp.where(image_id == own_image[g], block, 0.0), axis=0, keepdims=True)
            )
        scale = 1.0 + per_row([item[:, :channels] for item in picked])
        shift = per_row([item[:, channels:] for item in picked])
        near_wait(nb2, 1)
        mean2, inv2 = gather_moments(nb2)
        cf[4] = mean2
        cf[5] = inv2
        cf[6] = inv2 * gain2 * scale
        cf[7] = shift2 * scale + shift

        def modulated(g, values):
            return (values - coef(4, g)) * coef(6, g) + coef(7, g)

        def act_two(g, r):
            values = modulated(g, h_v[g, inner(r), :])
            a2_v[g, span(r), :] = keep(g, r, silu(values)).astype(BF16)

        def act_two_edges(g):
            act_two(g, 0)
            act_two(g, rows - 1)

        def act_two_inside(g):
            plain = jnp.zeros((8, channels), F32)
            cross = jnp.zeros((8, channels), F32)
            for r in range(1, rows - 1):
                gap = h_v[g, inner(r), :] - coef(4, g)
                values = gap * coef(6, g) + coef(7, g)
                gate = 0.5 + 0.5 * jnp.tanh(0.5 * values)
                a2_v[g, span(r), :] = keep(g, r, values * gate).astype(BF16)
                slope = gate * (1.0 + values * (1.0 - gate))
                grad = keep(g, r, gm_v[g, inner(r), :].astype(F32) * slope)
                gm_v[g, inner(r), :] = grad.astype(plan.held)
                plain = plain + fold(grad)
                cross = cross + fold(grad * gap)
            st[0, g] = plain
            st[1, g] = cross

        each_batch(act_two_edges)

        each_batch(act_two_inside)

        def grad_edges(g, blocks):
            keep_halo(g2_v, 1, g)
            plain = jnp.zeros((8, channels), F32)
            cross = jnp.zeros((8, channels), F32)
            for r, line in conv(g2_v, kb2, g, blocks, True):
                gap = h_v[g, inner(r), :] - coef(4, g)
                slope = silu_slope(gap * coef(6, g) + coef(7, g))
                grad = keep(g, r, line * slope)
                gm_v[g, inner(r), :] = grad.astype(plan.held)
                plain = plain + fold(grad)
                cross = cross + fold(grad * gap)
            st[0, g] = st[0, g] + plain
            st[1, g] = (st[1, g] + cross) * coef(5, g)

        each_edge(grad_edges)
        offset_row = jnp.zeros((1, channels), F32)
        for g in range(batches):
            offset_row = offset_row + jnp.sum(st[4, g], axis=0, keepdims=True)
        tile = pack_tile(stat_tile(0), stat_tile(1))
        msg[1] = jnp.where(row_id == 2 * batches, offset_row, tile)
        tell_all(msg.at[1], ex3, 2)
        halo(a2_v, 2, None, 0, 1)

        weight_grad_two(plan.grad_rows)
        scatter_core(1)

        near_all(ex3, 2)
        plain, cross = gather_sums(ex3)
        factor = gain2 * scale
        counts = per_row(image_count, 1.0)
        cf[8] = factor * inv2
        cf[9] = group_sum(factor * plain) / counts * inv2
        cf[10] = group_sum(factor * cross) / counts * inv2 * inv2

        def grad_one(g, r):
            gap = h_v[g, inner(r), :] - coef(4, g)
            values = gm_v[g, inner(r), :].astype(F32) * coef(8, g) - coef(9, g) - gap * coef(10, g)
            low = keep(g, r, values).astype(BF16)
            g1_v[g, span(r), :] = low
            return fold(low.astype(F32))

        def grad_one_edges(g):
            st[4, g] = grad_one(g, 0) + grad_one(g, rows - 1)

        def grad_one_inside(g):
            part = st[4, g]
            for r in range(1, rows - 1):
                part = part + grad_one(g, r)
            st[4, g] = part

        each_batch(grad_one_edges)
        halo(g1_v, 3)
        halo(a2_v, 2, None, 1)
        each_batch(grad_one_inside)

        scatter_y(1)
        weight_grad_one(plan.grad_rows)
        scatter_z(1)
        scatter_core(0)
        turn(kf1)

        def back_one(each, pump=None):
            def body(g, blocks):
                plain = jnp.zeros((8, channels), F32)
                cross = jnp.zeros((8, channels), F32)
                for r, line in conv(g1_v, kf1, g, blocks, True):
                    gap = x_v[g, span(r), :].astype(F32) - coef(0, g)
                    grad = keep(g, r, line * silu_slope(gap * coef(2, g) + coef(3, g)))
                    a1_v[g, span(r), :] = grad.astype(BF16)
                    plain = plain + fold(grad)
                    cross = cross + fold(grad * gap)
                cross = cross * coef(1, g)
                st[0, g] = st[0, g] + plain
                st[1, g] = st[1, g] + cross

            each(body, pump=pump)

        st[0] = jnp.zeros((batches, 8, channels), F32)
        st[1] = jnp.zeros((batches, 8, channels), F32)

        def pump_two(g):
            pl.when(g == 1)(lambda: scatter_y(0))

        def keep_back(blocks, sem):
            for i, (r, count) in enumerate(blocks):
                pltpu.make_async_copy(
                    a1_v.at[:, span(r, count)], d1_hbm.at[:, pl.ds(r * cols, count * cols)],
                    back_sem.at[sem + i],
                ).start()

        def keep_wait(blocks, sem):
            for i, (r, count) in enumerate(blocks):
                wait_bytes(a1_v.at[:, span(r, count)], back_sem.at[sem + i])

        back_one(each_part, pump_two)
        keep_back(INSIDE, 2)
        def pump_three(g):
            keep_halo(g1_v, 3, g)
            pl.when(g == 1)(lambda: scatter_z(0))

        back_one(each_edge, pump_three)
        keep_back(EDGES, 0)
        offset_row = jnp.zeros((1, channels), F32)
        for g in range(batches):
            offset_row = offset_row + jnp.sum(st[4, g], axis=0, keepdims=True)
        tile = pack_tile(stat_tile(0), stat_tile(1))
        msg[3] = jnp.where(row_id == 2 * batches, offset_row, tile)
        tell_all(msg.at[3], ex4, 3)

        def output_rows(each, blocks, buf, sem, pump=None):
            def body(g, blocks):
                for r, line in conv(a2_v, kf2, g, blocks, False):
                    line = line + coef(14, g) + x_v[g, span(r), :].astype(F32)
                    buf[g, span(r), :] = keep(g, r, line).astype(BF16)

            each(body, pump=pump)
            for i, (r, count) in enumerate(blocks):
                pltpu.make_async_copy(
                    buf.at[:, span(r, count)], out_hbm.at[:, pl.ds(r * cols, count * cols)],
                    out_sem.at[sem + i],
                ).start()

        def output_wait(blocks, buf, sem):
            for i, (r, count) in enumerate(blocks):
                wait_bytes(buf.at[:, span(r, count)], out_sem.at[sem + i])

        def pump_four(g):
            pl.when(g == 1)(lambda: scatter_x(1))

        output_rows(each_part, INSIDE, g1_v, 2, pump_four)
        halo_sent(g1_v, 3)

        def pump_five(g):
            keep_halo(a2_v, 2, g)
            pl.when(g == 1)(lambda: scatter_x(0))

        output_rows(each_edge, EDGES, g1_v, 0, pump_five)

        near_all(ex4, 3)
        plain, cross = gather_sums(ex4)
        cf[11] = group_sum(gain1 * plain) / counts * inv1
        cf[12] = group_sum(gain1 * cross) / counts * inv1 * inv1

        cf_o[0] = cf[0]
        cf_o[1] = cf[2]
        cf_o[2] = cf[11]
        cf_o[3] = cf[12]
        for g in range(batches):
            for r in range(rows):
                wr_o[g, r] = wr_s[g, r + 1]
        scatter_end(1, wg2_o)

        far_all(ex3, 2)
        second_bias = jnp.zeros((1, channels), F32)
        gain_total = jnp.zeros((1, channels), F32)
        shift_total = jnp.zeros((1, channels), F32)
        time_rows = []
        slot_id = lax.broadcasted_iota(jnp.int32, (images, n), 0)
        for g in range(batches):
            hot = jnp.where(slot_v[g : g + 1, :] == slot_id, 1.0, 0.0).astype(F32)
            plain = jnp.dot(hot, ex3[:, g, :], precision=HIGHEST, preferred_element_type=F32)
            cross = jnp.dot(hot, ex3[:, batches + g, :], precision=HIGHEST, preferred_element_type=F32)
            factor = 1.0 + tout[g * images : (g + 1) * images, :channels]
            gain_total = gain_total + jnp.sum(factor * cross, axis=0, keepdims=True)
            shift_total = shift_total + jnp.sum(factor * plain, axis=0, keepdims=True)
            time_rows.append(jnp.concatenate([cross * gain2 + plain * shift2, plain], axis=1))
        second_bias = jnp.sum(ex3[:, 2 * batches, :], axis=0, keepdims=True)
        grad_time = jnp.concatenate(time_rows, axis=0)
        time_total = jnp.sum(grad_time, axis=0, keepdims=True)
        tkg_o[...] = lax.dot_general(
            osel[...], grad_time, (((0,), (0,)), ((), ())), precision=HIGHEST,
            preferred_element_type=F32,
        )[:embed_rows]

        far_all(ex4, 3)
        plain = jnp.zeros((1, channels), F32)
        cross = jnp.zeros((1, channels), F32)
        for g in range(batches):
            plain = plain + jnp.sum(ex4[:, g, :], axis=0, keepdims=True)
            cross = cross + jnp.sum(ex4[:, batches + g, :], axis=0, keepdims=True)
        first_bias = jnp.sum(ex4[:, 2 * batches, :], axis=0, keepdims=True)
        vec_c = lax.broadcasted_iota(jnp.int32, (channels, 128), 0)
        vec_j = lax.broadcasted_iota(jnp.int32, (channels, 128), 1)
        whole = jnp.concatenate(
            [cross, plain, first_bias, gain_total, shift_total, second_bias]
            + [jnp.zeros((2, channels), F32)], axis=0,
        )
        pick = jnp.where(vec_c == vec_j + me * param_width, 1.0, 0.0).astype(F32)
        vec_o[:8] = jnp.dot(whole, pick, precision=HIGHEST, preferred_element_type=F32)
        time_c = lax.broadcasted_iota(jnp.int32, (2 * channels, 128), 0)
        time_j = lax.broadcasted_iota(jnp.int32, (2 * channels, 128), 1)
        pick = jnp.where(time_c == time_j + me * time_width, 1.0, 0.0).astype(F32)
        vec_o[8:] = jnp.dot(
            jnp.broadcast_to(time_total, (8, 2 * channels)), pick, precision=HIGHEST,
            preferred_element_type=F32,
        )
        scatter_end(0, wg1_o)

        keep_wait(INSIDE, 2)
        keep_wait(EDGES, 0)
        output_wait(INSIDE, g1_v, 2)
        output_wait(EDGES, g1_v, 0)
        for k in range(2):
            scatter_sent(k)
        reduce_sent()
        near_sent(nb1, 0)
        near_sent(nb2, 1)
        sent_all(ex3, 2)
        sent_all(ex4, 3)
        sent_all(pbuf, 4)
        for which, field in enumerate((x_v, g2_v, a2_v)):
            halo_sent(field, which)

    margin = (batches, (rows + 2) * cols, channels)
    whole = (batches, rows * cols, channels)
    dma = pltpu.SemaphoreType.DMA
    hops = nx * nz * max(ny - 1, 1)
    few = max(nx * ny, nz)
    scratch = [
        pltpu.VMEM(margin, BF16),
        pltpu.VMEM(margin, BF16),
        pltpu.VMEM(margin, BF16),
        pltpu.VMEM(margin, BF16),
        pltpu.VMEM(margin, BF16),
        pltpu.VMEM(whole, F32),
        pltpu.VMEM(whole, plan.held),
        pltpu.VMEM((3 * channels, 3 * channels), BF16),
        pltpu.VMEM((3 * channels, 3 * channels), BF16),
        pltpu.VMEM((3 * channels, 3 * channels), BF16),
        pltpu.VMEM((2, gx_size, nz, nx, padded, channels), BF16),
        pltpu.VMEM((taps + 16, channels), F32),
        pltpu.VMEM((2, ny, nz, nx, padded, channels), BF16),
        pltpu.VMEM((2, max(ny - 1, 1), nz, nx, padded, channels), BF16),
        pltpu.VMEM((2, max(nz - 1, 1), nx, padded, channels), BF16),
        pltpu.VMEM((2, max(nx - 1, 1), padded, channels), BF16),
        pltpu.VMEM((2 * reach + 1, 8, channels), F32),
        pltpu.VMEM((2 * reach + 1, 8, channels), F32),
        pltpu.VMEM((n, 8, channels), F32),
        pltpu.VMEM((n, 8, channels), F32),
        pltpu.VMEM((n, 1, 128), F32),
        pltpu.VMEM((ny * nx, batches * images, 2 * channels), F32),
        pltpu.VMEM((nz, batches * images, 2 * channels), F32),
        pltpu.VMEM((2, batches * images, 2 * channels), F32),
        pltpu.VMEM((batches * images, 2 * channels), F32),
        pltpu.VMEM((batches * images, 128), F32),
        pltpu.VMEM((4, 8, channels), F32),
        pltpu.VMEM((16, 8, channels), F32),
        pltpu.VMEM((5, batches, 8, channels), F32),
        pltpu.SMEM((batches, 16), jnp.int32),
        dma((2,)),
        dma((4, 2, batches)),
        dma((4, 2, batches)),
        dma((2, 4, hops)),
        dma((2, 4, hops)),
        dma((2, 4, few)),
        dma((2, 4, few)),
        dma((3, few)),
        dma((3, few)),
        dma((5,)),
        dma((5,)),
        dma((5,)),
        dma((3,)),
        dma((3,)),
    ]
    hbm = pl.BlockSpec(memory_space=pl.ANY)
    vmem = pl.BlockSpec(memory_space=pltpu.VMEM)
    smem = pl.BlockSpec(memory_space=pltpu.SMEM)
    return pl.pallas_call(
        kernel,
        name="block",
        out_shape=(
            jax.ShapeDtypeStruct(whole, BF16),
            jax.ShapeDtypeStruct(whole, BF16),
            jax.ShapeDtypeStruct((shard, channels), F32),
            jax.ShapeDtypeStruct((shard, channels), F32),
            jax.ShapeDtypeStruct((embed_rows, 2 * channels), F32),
            jax.ShapeDtypeStruct((16, 128), F32),
            jax.ShapeDtypeStruct((4, 8, channels), F32),
            jax.ShapeDtypeStruct((batches, rows), jnp.int32),
        ),
        in_specs=[hbm, hbm, vmem, vmem, vmem, vmem, vmem, vmem, smem, smem],
        out_specs=(hbm, hbm, vmem, vmem, vmem, vmem, vmem, smem),
        scratch_shapes=scratch,
        compiler_params=pltpu.CompilerParams(
            collective_id=0, has_side_effects=True, vmem_limit_bytes=VMEM_LIMIT,
        ),
        cost_estimate=pl.CostEstimate(
            flops=12 * rows * cols * batches * taps * channels,
            bytes_accessed=8 * rows * cols * batches * channels,
            transcendentals=8 * rows * cols * batches * channels,
        ),
    )


VMEM_LIMIT = 63 * 2**20


def build_tail(plan, vectors):
    batches, rows, cols, channels = plan.batches, plan.rows, plan.cols, plan.channels
    step_rows = rows if plan.parts == 1 else 2

    def kernel(
        wr_s, cf, x, og, d1, done, wg1, wg2, tkg, vec, out, gi, wg1_o, wg2_o, tkg_o, *small
    ):
        g, c = pl.program_id(0), pl.program_id(1)
        col_id = lax.broadcasted_iota(jnp.int32, (cols, channels), 0)

        def coef(which):
            return cf[which, pl.ds(g, 1), :]

        for q in range(step_rows):
            place = slice(q * cols, (q + 1) * cols)
            gap = x[0, place].astype(F32) - coef(0)
            values = d1[0, place].astype(F32) * coef(1) - coef(2) - gap * coef(3) + og[0, place].astype(F32)
            width = wr_s[g, c * step_rows + q]
            gi[0, place] = jnp.where(col_id < width, values, 0.0).astype(BF16)
        out[...] = done[...]

        @pl.when((g == 0) & (c == 0))
        def _():
            wg1_o[...] = wg1[...]
            wg2_o[...] = wg2[...]
            tkg_o[...] = tkg[...]
            for ref, (row, size) in zip(small, vectors):
                ref[...] = vec[row, :size]

    block = pl.BlockSpec((1, step_rows * cols, channels), lambda g, c: (g, c, 0))

    def fixed(*shape):
        return pl.BlockSpec(shape, lambda g, c: (0,) * len(shape))

    kernel_grad = fixed(plan.shard, channels)
    time_grad = fixed(plan.embed_rows, 2 * channels)
    whole = (batches, rows * cols, channels)
    return pl.pallas_call(
        kernel,
        name="tail",
        grid=(batches, rows // step_rows),
        in_specs=[
            pl.BlockSpec(memory_space=pltpu.SMEM), fixed(4, 8, channels),
            block, block, block, block,
            kernel_grad, kernel_grad, time_grad, fixed(16, 128),
        ],
        out_specs=[block, block, kernel_grad, kernel_grad, time_grad]
        + [fixed(size) for _, size in vectors],
        out_shape=[
            jax.ShapeDtypeStruct(whole, BF16),
            jax.ShapeDtypeStruct(whole, BF16),
            jax.ShapeDtypeStruct((plan.shard, channels), F32),
            jax.ShapeDtypeStruct((plan.shard, channels), F32),
            jax.ShapeDtypeStruct((plan.embed_rows, 2 * channels), F32),
        ]
        + [jax.ShapeDtypeStruct((size,), F32) for _, size in vectors],
        compiler_params=pltpu.CompilerParams(
            vmem_limit_bytes=VMEM_LIMIT, dimension_semantics=("arbitrary", "arbitrary")
        ),
    )


def make_body(mesh_shape):
    def body(
        input_cells, time_embed, first_gain, first_shift, first_kernel, first_offset,
        time_kernel, time_offset, second_gain, second_shift, second_kernel, second_offset,
        output_grad, slot_image, image_height,
    ):
        cells = input_cells.shape
        plan = Plan(
            mesh_shape, cells, time_embed.shape, slot_image.shape,
            first_kernel.shape[0], time_kernel.shape[0],
        )
        flat = (cells[0], cells[1] * cells[2], cells[3])
        params = jnp.concatenate(
            [first_gain, first_shift, first_offset, second_gain, second_shift, second_offset,
             time_offset]
        ).astype(F32)
        params = jnp.pad(params[None, :], ((0, 0), (0, 128 - params.shape[0])))
        cells_in, cells_grad = input_cells.reshape(flat), output_grad.reshape(flat)
        done, part, wg1, wg2, tkg, vec, cf, widths = build_kernel(plan)(
            cells_in, cells_grad, first_kernel, second_kernel,
            params, time_embed, time_kernel, slot_image, slot_image, image_height,
        )
        width = first_gain.shape[0]
        vectors = [(i, width) for i in range(6)] + [(8, time_offset.shape[0])]
        out, grad, wg1, wg2, tkg, *rows = build_tail(plan, vectors)(
            widths, cf, cells_in, cells_grad, part, done, wg1, wg2, tkg, vec
        )
        return (
            out.reshape(cells), grad.reshape(cells), rows[0], rows[1], wg1, rows[2],
            tkg, rows[6], rows[3], rows[4], wg2, rows[5],
        )

    return body


def solution(mesh):
    both = ("gx", "gy")
    cells, vector, matrix, whole = P(None, both, None, None), P(both), P(both, None), P()
    return jax.shard_map(
        make_body(dict(mesh.shape)),
        mesh=mesh,
        in_specs=(
            cells, whole, vector, vector, matrix, vector, matrix, vector, vector, vector, matrix,
            vector, cells, whole, whole,
        ),
        out_specs=(
            cells, cells, vector, vector, matrix, vector, matrix, vector, vector, vector, matrix,
            vector,
        ),
        check_vma=False,
    )
```
